32 devices in a mesh: dp: 8 (over z, x), mp: 4 (over y, core).
Axes of the slice: x: 2, y: 2, z: 4, core: 2. Of those that a mesh axis runs over, the one named last changes fastest.
Arguments:
- latents: float32 [8, 1792, 16], P('dp', 'mp'), may hold values from -6 to 6
- noise: float32 [8, 1792, 16], P('dp', 'mp'), may hold values from -6 to 6
- caption: bfloat16 [8, 120, 4096], P('dp'), may hold values from -3 to 3
- caption_lens: int32 [8], replicated, may hold values from 15 to 120
- timesteps: int32 [8], replicated, may hold values from 50 to 999
- grid_hw: int32 [8, 2], replicated, may hold values from 8 to 56, as said below
- frame_counts: int32 [8], replicated, may hold values from 1 to 4, as said below
- attn_mats: float32 [3, 1152, 4608], P(None, 'dp', 'mp'), may hold values from -0.1875 to 0.1875
- ffn_mats: float32 [2, 2, 1152, 4608], P(None, None, 'dp', 'mp'), may hold values from -0.1875 to 0.1875
- embed_mats: float32 [13568, 1152], P('dp', 'mp'), may hold values from -0.1875 to 0.1875
- vectors: float32 [106016], replicated
- attn_first: float32 [3, 1152, 4608], P(None, 'dp', 'mp'), may hold values from -1.5258789e-05 to 1.5258789e-05
- ffn_first: float32 [2, 2, 1152, 4608], P(None, None, 'dp', 'mp'), may hold values from -1.5258789e-05 to 1.5258789e-05
- embed_first: float32 [13568, 1152], P('dp', 'mp'), may hold values from -1.5258789e-05 to 1.5258789e-05
- vector_first: float32 [106016], replicated, may hold values from -1.0999719e-05 to 1.0999719e-05
- attn_second: float32 [3, 1152, 4608], P(None, 'dp', 'mp'), may hold values from 7.562113e-12 to 3.0248453e-11
- ffn_second: float32 [2, 2, 1152, 4608], P(None, None, 'dp', 'mp'), may hold values from 7.562113e-12 to 3.0248453e-11
- embed_second: float32 [13568, 1152], P('dp', 'mp'), may hold values from 7.562113e-12 to 3.0248453e-11
- vector_second: float32 [106016], replicated, may hold values from 4.726321e-13 to 1.20993819e-10
- attn_ema: float32 [3, 1152, 4608], P(None, 'dp', 'mp'), may hold values from -0.1875 to 0.1875
- ffn_ema: float32 [2, 2, 1152, 4608], P(None, None, 'dp', 'mp'), may hold values from -0.1875 to 0.1875
- embed_ema: float32 [13568, 1152], P('dp', 'mp'), may hold values from -0.1875 to 0.1875
- vector_ema: float32 [106016], replicated
Outputs:
- loss_sum: float32 [], replicated
- token_count: float32 [], replicated
- grad_norm: float32 [], replicated
- attn_first_new: float32 [3, 1152, 4608], P(None, 'dp', 'mp')
- ffn_first_new: float32 [2, 2, 1152, 4608], P(None, None, 'dp', 'mp')
- embed_first_new: float32 [13568, 1152], P('dp', 'mp')
- vector_first_new: float32 [106016], replicated
- attn_second_new: float32 [3, 1152, 4608], P(None, 'dp', 'mp')
- ffn_second_new: float32 [2, 2, 1152, 4608], P(None, None, 'dp', 'mp')
- embed_second_new: float32 [13568, 1152], P('dp', 'mp')
- vector_second_new: float32 [106016], replicated
- attn_new: float32 [3, 1152, 4608], P(None, 'dp', 'mp')
- ffn_new: float32 [2, 2, 1152, 4608], P(None, None, 'dp', 'mp')
- embed_new: float32 [13568, 1152], P('dp', 'mp')
- vector_new: float32 [106016], replicated
- attn_ema_new: float32 [3, 1152, 4608], P(None, 'dp', 'mp')
- ffn_ema_new: float32 [2, 2, 1152, 4608], P(None, None, 'dp', 'mp')
- embed_ema_new: float32 [13568, 1152], P('dp', 'mp')
- vector_ema_new: float32 [106016], replicated
The draws below stay inside these ranges and needn't reach their ends.
Inputs may be any that keep to these rules, and one draw needn't show every extreme that they name: `grid_hw`: each row is a clip's grid: rows between 8 and 31, columns = 448 // rows, so a frame has at most 448 patches; in every draw some clip has exactly 16 rows and 448 patches, some clip has 8 rows and some clip has 31 rows. `frame_counts`: the last clip has 4 frames in every draw.
All inputs are finite; a program needn't handle non-finite values.
Results may differ from the reference program's by a relative error of at most 0.015.
Values may be sent and summed in bfloat16 or wider, within the bound.
A program may use at most 320 MiB of HBM per device.

```python
import math
import jax
import jax.numpy as jnp
from jax import lax

D = 1152
HEADS = 16
HD = 72
FF = 4608
TFREQ = 256
TXT = 4096
CIN = 16
COUT = 32
CAP = 120
FR = 4
PM = 448
PH = 16
STEP = 5
GROUPS = 8
TOKG = 1792
EMB_ROWS = 13568
NV = 106016
PARAMS = 52895264


def draw_grid_hw(key, part):
    key_rows, key_full = jax.random.split(jax.random.fold_in(key, 3))
    heights = jax.random.randint(key_rows, (GROUPS,), PH // 2, 2 * PH)
    chosen = jax.random.randint(key_full, (), 0, GROUPS)
    slots = jnp.arange(GROUPS)
    heights = jnp.where(slots == chosen, PH, heights)
    heights = jnp.where(slots == (chosen + 1) % GROUPS, PH // 2, heights)
    heights = jnp.where(slots == (chosen + 2) % GROUPS, 2 * PH - 1, heights)
    return jnp.stack([heights, PM // heights], 1).astype(jnp.int32)


def draw_frame_counts(key, part):
    ramp = 1 + jnp.arange(GROUPS) * FR // GROUPS
    jitter = jax.random.randint(jax.random.fold_in(key, 5), (GROUPS,), -1, 2)
    counts = jnp.clip(ramp + jitter, 1, FR)
    return jnp.where(jnp.arange(GROUPS) == GROUPS - 1, FR, counts).astype(jnp.int32)


def vector_noise(key, extent):
    return jax.random.normal(key, extent, jnp.float32)


def vector_draw(key):
    keys = jax.random.split(key, 18)
    rise_model = jnp.linspace(0.0, 1.0, D)
    rise_units = jnp.linspace(0.0, 1.0, FF)
    height = 1.0
    lows = 0.1 * vector_noise(keys[9], (3, 3, D))
    ramped = (0.2 + 1.3 * rise_model) * vector_noise(keys[10], (3, D))
    attn_bias = jnp.stack([lows[:, 0], ramped, lows[:, 2]], 1)
    shifts = 0.2 * vector_noise(keys[13], (2, 2, D))
    scales = -0.5 + height * rise_model + 0.1 * vector_noise(keys[14], (2, 2, D))
    gates = 0.6 + 0.2 * vector_noise(keys[15], (2, 2, D))
    tables = jnp.stack([shifts[:, 0], scales[:, 0], gates[:, 0], shifts[:, 1], scales[:, 1], gates[:, 1]], 1)
    final_table = jnp.stack([0.2 * vector_noise(keys[16], (D,)), -0.5 + height * rise_model + 0.1 * vector_noise(keys[17], (D,))])
    pieces = [0.3 * vector_noise(keys[0], (CIN, D)), 0.1 * vector_noise(keys[1], (D,)), vector_noise(keys[2], (COUT, D)) / math.sqrt(D), 0.1 * vector_noise(keys[3], (COUT,)), 0.1 * vector_noise(keys[4], (D,)), 0.1 * vector_noise(keys[5], (D,)), 0.1 * vector_noise(keys[6], (6 * D,)), 0.1 * vector_noise(keys[7], (D,)), 0.1 * vector_noise(keys[8], (D,)), attn_bias, (0.1 + rise_units) * vector_noise(keys[11], (2, FF)), 0.1 * vector_noise(keys[12], (2, D)), tables, final_table]
    return jnp.concatenate([piece.reshape(-1) for piece in pieces]).astype(jnp.float32)


def draw_vectors(key, part):
    return vector_draw(jax.random.fold_in(key, 11))


def draw_vector_ema(key, part):
    return vector_draw(jax.random.fold_in(key, 12))


def second_levels(key):
    spread = jax.random.uniform(jax.random.fold_in(key, 21), (NV,), jnp.float32, 0.0, math.log(256.0))
    return 2.5e-05 / PARAMS * jnp.exp(spread)


def draw_vector_second(key, part):
    return second_levels(key).astype(jnp.float32)


def draw_vector_first(key, part):
    levels = second_levels(key)
    key = jax.random.fold_in(key, 22)
    sided = jax.random.uniform(key, (NV,), jnp.float32, -1.0, 1.0)
    sizes = 0.5 + 0.5 * jnp.abs(sided)
    return (jnp.where(sided >= 0.0, 1.0, -1.0) * sizes * jnp.sqrt(levels)).astype(jnp.float32)


def with_ends(values, stream_key, low, top_value):
    shape = values.shape
    place = [jax.random.randint(jax.random.fold_in(stream_key, axis), (), 0, shape[axis]) for axis in range(len(shape))]
    values = values.at[tuple(place)].set(low)
    longest = shape.index(max(shape))
    place[longest] = (place[longest] + 1) % shape[longest]
    return values.at[tuple(place)].set(top_value)


def block_levels(rng, dims, cuts, low, top_value):
    loudness = 1.0
    for axis_at, blocks in cuts:
        draws = jax.random.uniform(jax.random.fold_in(jax.random.fold_in(rng, 6), axis_at), (blocks,), jnp.float32, low / len(cuts), top_value / len(cuts))
        loudness = loudness * jnp.repeat(jnp.exp(draws), dims[axis_at] // blocks).reshape((-1,) + (1,) * (len(dims) - 1 - axis_at))
    return loudness


def gaussian(stream_key, shape, scale, limit, cuts=(), kind=jnp.bfloat16):
    drawn = scale * jax.random.normal(stream_key, shape, jnp.float32)
    if cuts:
        drawn = drawn * block_levels(stream_key, shape, cuts, -0.22, 0.18)
    return jnp.clip(drawn, -limit, limit).astype(kind)


def setup_inputs(seed: int = 0) -> dict:
    seeds = jax.random.split(jax.random.key(seed), 24)
    return {
        "latents": gaussian(seeds[0], (GROUPS, TOKG, CIN), 1.0, 6.0, ((0, 8), (1, 4)), jnp.float32),
        "noise": gaussian(seeds[1], (GROUPS, TOKG, CIN), 1.0, 6.0, ((0, 8), (1, 4)), jnp.float32),
        "caption": gaussian(seeds[2], (GROUPS, CAP, TXT), 0.5, 3.0, ((0, 8),)),
        "caption_lens": with_ends(jax.random.randint(seeds[3], (GROUPS,), CAP // 8, CAP + 1), jax.random.fold_in(seeds[3], 1), CAP // 8, CAP).astype(jnp.int32),
        "timesteps": with_ends(jax.random.randint(seeds[4], (GROUPS,), 50, 1000), jax.random.fold_in(seeds[4], 1), 50, 999).astype(jnp.int32),
        "grid_hw": draw_grid_hw(jax.random.fold_in(seeds[23], 71), 0),
        "frame_counts": draw_frame_counts(jax.random.fold_in(seeds[23], 71), 0),
        "attn_mats": gaussian(seeds[7], (3, D, 4 * D), D ** -0.5, 0.1875, ((1, 8), (2, 4)), jnp.float32),
        "ffn_mats": gaussian(seeds[8], (2, 2, D, FF), D ** -0.5, 0.1875, ((2, 8), (3, 4)), jnp.float32),
        "embed_mats": gaussian(seeds[9], (EMB_ROWS, D), D ** -0.5, 0.1875, ((0, 8), (1, 4)), jnp.float32),
        "vectors": draw_vectors(jax.random.fold_in(seeds[23], 71), 0),
        "attn_first": gaussian(seeds[11], (3, D, 4 * D), (0.02 / PARAMS ** 0.5), 1.52587890625e-05, ((1, 8), (2, 4)), jnp.float32),
        "ffn_first": gaussian(seeds[12], (2, 2, D, FF), (0.02 / PARAMS ** 0.5), 1.52587890625e-05, ((2, 8), (3, 4)), jnp.float32),
        "embed_first": gaussian(seeds[13], (EMB_ROWS, D), (0.02 / PARAMS ** 0.5), 1.52587890625e-05, ((0, 8), (1, 4)), jnp.float32),
        "vector_first": draw_vector_first(jax.random.fold_in(seeds[23], 71), 0),
        "attn_second": jnp.clip(jnp.exp(math.log(3.024845304788748e-11) - 1.3862944 * jax.random.uniform(seeds[15], (3, D, 4 * D), jnp.float32) ** block_levels(seeds[15], (3, D, 4 * D), ((1, 8), (2, 4)), -0.2, 0.2)), 7.56211326197187e-12, 3.024845304788748e-11),
        "ffn_second": jnp.clip(jnp.exp(math.log(3.024845304788748e-11) - 1.3862944 * jax.random.uniform(seeds[16], (2, 2, D, FF), jnp.float32) ** block_levels(seeds[16], (2, 2, D, FF), ((2, 8), (3, 4)), -0.2, 0.2)), 7.56211326197187e-12, 3.024845304788748e-11),
        "embed_second": jnp.clip(jnp.exp(math.log(3.024845304788748e-11) - 1.3862944 * jax.random.uniform(seeds[17], (EMB_ROWS, D), jnp.float32) ** block_levels(seeds[17], (EMB_ROWS, D), ((0, 8), (1, 4)), -0.2, 0.2)), 7.56211326197187e-12, 3.024845304788748e-11),
        "vector_second": draw_vector_second(jax.random.fold_in(seeds[23], 71), 0),
        "attn_ema": gaussian(seeds[19], (3, D, 4 * D), D ** -0.5, 0.1875, ((1, 8), (2, 4)), jnp.float32),
        "ffn_ema": gaussian(seeds[20], (2, 2, D, FF), D ** -0.5, 0.1875, ((2, 8), (3, 4)), jnp.float32),
        "embed_ema": gaussian(seeds[21], (EMB_ROWS, D), D ** -0.5, 0.1875, ((0, 8), (1, 4)), jnp.float32),
        "vector_ema": draw_vector_ema(jax.random.fold_in(seeds[23], 71), 0),
    }


HIGHEST = lax.Precision.HIGHEST
EPS_NORM = 1e-06
LEARN_RATE = 0.03
VECTOR_RATE = 0.15
BETA_FIRST = 0.5
BETA_SECOND = 0.5
ADAM_EPSILON = 1e-08
WEIGHT_DECAY = 0.01
EMA_DECAY = 0.9
CLIP_NORM = 0.02
NEG_LARGE = -1e+30

@jax.custom_vjp
def low(v):
    return lax.optimization_barrier(v.astype(jnp.bfloat16)).astype(jnp.float32)

@jax.custom_vjp
def low_back(v):
    return v

def low_keep(v):
    return (low(v), None)

def low_pass(kept, grad):
    return (grad,)

def back_keep(v):
    return (v, None)

def back_low(kept, grad):
    return (low(grad),)
low.defvjp(low_keep, low_pass)
low_back.defvjp(back_keep, back_low)

def vector_parts():
    return [('patch_w', (CIN, D)), ('patch_b', (D,)), ('final_w', (COUT, D)), ('final_b', (COUT,)), ('t_bias_one', (D,)), ('t_bias_two', (D,)), ('t_bias_mod', (6 * D,)), ('c_bias_one', (D,)), ('c_bias_two', (D,)), ('attn_bias', (3, 3, D)), ('ffn_bias_one', (2, FF)), ('ffn_bias_two', (2, D)), ('tables', (2, 6, D)), ('final_table', (2, D))]

def unpack(flat):
    result = {}
    offset = 0
    for label, extent in vector_parts():
        length = math.prod(extent)
        result[label] = flat[offset:offset + length].reshape(extent)
        offset += length
    return result

def waves(position, width):
    half = width // 2
    freqs = jnp.exp(-math.log(10000.0) * jnp.arange(half, dtype=jnp.float32) / half)
    angles = position[..., None] * freqs
    return jnp.concatenate([jnp.sin(angles), jnp.cos(angles)], -1)

def roster():
    betas = 0.0001 + (0.02 - 0.0001) * jnp.arange(1000, dtype=jnp.float32) / 999.0
    return (betas, jnp.exp(jnp.cumsum(jnp.log1p(-betas))))

def modulate(x, shift_vec, scale_vec):
    centered = x - lax.optimization_barrier(jnp.mean(x, -1, keepdims=True))
    normed = centered * lax.rsqrt(lax.optimization_barrier(jnp.mean(centered * centered, -1, keepdims=True)) + EPS_NORM)
    return normed * (1.0 + scale_vec) + shift_vec

def token_losses(output, frozen, latent, noise_part, extra):
    noisy, alpha_bar, alpha_prev, beta_now = extra
    eps = output[:, :CIN]
    var_raw = output[:, CIN:]
    mse = lax.optimization_barrier(jnp.mean((eps - noise_part) ** 2, -1))
    post_var = beta_now * (1.0 - alpha_prev) / (1.0 - alpha_bar)
    log_post = jnp.log(post_var)
    frac = (var_raw + 1.0) / 2.0
    log_var = frac * jnp.log(beta_now) + (1.0 - frac) * log_post
    coef_start = beta_now * jnp.sqrt(alpha_prev) / (1.0 - alpha_bar)
    coef_now = (1.0 - alpha_prev) * jnp.sqrt(1.0 - beta_now) / (1.0 - alpha_bar)
    true_mean = coef_start * latent + coef_now * noisy
    guess = (noisy - jnp.sqrt(1.0 - alpha_bar) * frozen) / jnp.sqrt(alpha_bar)
    model_mean = coef_start * guess + coef_now * noisy
    kl_term = 0.5 * (-1.0 + log_var - log_post + jnp.exp(log_post - log_var) + (true_mean - model_mean) ** 2 * jnp.exp(-log_var))
    return mse + lax.optimization_barrier(jnp.mean(kl_term, -1)) / math.log(2.0)

def attention_forms(kind):
    if kind == 'space':
        return ('fqhe,fkhe->fhqk', 'fhqk,fkhe->fqhe', 'fhqk,fqhe->fkhe')
    if kind == 'time':
        return ('qphe,kphe->phqk', 'phqk,kphe->qphe', 'phqk,qphe->kphe')
    return ('qhe,khe->hqk', 'hqk,khe->qhe', 'hqk,qhe->khe')

def matmul(left, right):
    return jnp.dot(left, right, precision=HIGHEST)

def einsum_high(form, left, right):
    return jnp.einsum(form, left, right, precision=HIGHEST)

def ref_attention(source, weight, biases, kind, keep, context):
    forms = attention_forms(kind)
    rows_from = context if kind == 'cross' else source
    query = low(low_back(einsum_high('td,dhe->the', source, weight[:, :, 0]) + biases[0].reshape(HEADS, HD)))
    key_rows = low(low_back(einsum_high('td,dhe->the', rows_from, weight[:, :, 1])))
    value_rows = low(low_back(einsum_high('td,dhe->the', rows_from, weight[:, :, 2]) + biases[1].reshape(HEADS, HD)))
    if kind != 'cross':
        query = query.reshape(FR, PM, HEADS, HD)
        key_rows = key_rows.reshape(FR, PM, HEADS, HD)
        value_rows = value_rows.reshape(FR, PM, HEADS, HD)
    raw = low_back(einsum_high(forms[0], query, key_rows))
    probs = low(jax.nn.softmax(jnp.where(keep, raw * HD ** (-0.5), NEG_LARGE), axis=-1))
    mixed = low(low_back(einsum_high(forms[1], probs, value_rows).reshape(FR * PM, HEADS, HD)))
    return low_back(einsum_high('the,dhe->td', mixed, weight[:, :, 3]) + biases[2])

def ref_block(x, attn_w, ffn_w, parts, mods, index, kind, keeps, context):
    source = low(modulate(x, mods[0], mods[1]))
    x = x + mods[2] * ref_attention(source, attn_w[index], parts['attn_bias'][index], kind, keeps[kind], None)
    if kind == 'space':
        x = x + ref_attention(low(x), attn_w[2], parts['attn_bias'][2], 'cross', keeps['cross'], context)
    source = low(modulate(x, mods[3], mods[4]))
    pre = low_back(matmul(source, ffn_w[index, 0]) + parts['ffn_bias_one'][index])
    hidden = low(jax.nn.gelu(pre, approximate=True))
    return x + mods[5] * low_back(matmul(hidden, ffn_w[index, 1].T) + parts['ffn_bias_two'][index])

def group_forward(weights, group):
    attn_mats, ffn_mats, embed_mats, vectors = weights
    latent, noise_part, caption_part, cap_len, tstep, height, width_grid, frames = group
    parts = unpack(vectors)
    betas, cumul = roster()
    alpha_bar = cumul[tstep]
    alpha_prev = cumul[tstep - 1]
    beta_now = betas[tstep]
    noisy = jnp.sqrt(alpha_bar) * latent + jnp.sqrt(1.0 - alpha_bar) * noise_part
    embed_low = low(embed_mats)
    t_one = embed_low[:TFREQ]
    c_one = embed_low[TFREQ:TFREQ + TXT]
    t_two = embed_low[TFREQ + TXT:TFREQ + TXT + D]
    c_two = embed_low[TFREQ + TXT + D:TFREQ + TXT + 2 * D]
    t_mod = embed_low[TFREQ + TXT + 2 * D:]
    freq = low(waves(tstep.astype(jnp.float32), TFREQ))
    t_hidden = low(jax.nn.silu(matmul(freq, t_one) + parts['t_bias_one']))
    t_emb = matmul(t_two, t_hidden) + parts['t_bias_two']
    t_mod_vec = matmul(t_mod, low(jax.nn.silu(t_emb))) + parts['t_bias_mod']
    c_hidden = low(jax.nn.gelu(low_back(matmul(caption_part, c_one) + parts['c_bias_one']), approximate=True))
    context = low(low_back(matmul(c_hidden, c_two.T) + parts['c_bias_two']))
    token_ids = jnp.arange(FR * PM, dtype=jnp.int32)
    frame_slot = token_ids // PM
    patch_slot = token_ids % PM
    area = height * width_grid
    shifted = patch_slot - (PM - area)
    valid = (frame_slot >= FR - frames) & (patch_slot >= PM - area)
    position = jnp.concatenate([waves((shifted // width_grid).astype(jnp.float32), D // 2), waves((shifted % width_grid).astype(jnp.float32), D // 2)], -1)
    keeps = {'space': (jnp.arange(PM, dtype=jnp.int32) >= PM - area).reshape(1, 1, 1, PM), 'time': (jnp.arange(FR, dtype=jnp.int32) >= FR - frames).reshape(1, 1, 1, FR), 'cross': (jnp.arange(CAP, dtype=jnp.int32) < cap_len).reshape(1, 1, CAP)}
    x = low_back(matmul(low(noisy), low(parts['patch_w'])) + parts['patch_b']) + position
    attn_w = low(attn_mats).reshape(3, D, HEADS, 4, HD)
    ffn_w = low(ffn_mats)
    mods = parts['tables'] + t_mod_vec.reshape(1, 6, D)
    x = ref_block(x, attn_w, ffn_w, parts, mods[0], 0, 'space', keeps, context)
    x = x + waves((frame_slot - (FR - frames)).astype(jnp.float32), D)
    x = ref_block(x, attn_w, ffn_w, parts, mods[1], 1, 'time', keeps, context)
    final_mods = parts['final_table'] + t_emb
    source = low(modulate(x, final_mods[0], final_mods[1]))
    output = low_back(matmul(source, low(parts['final_w']).T) + parts['final_b'])
    return (output, valid, (noisy, alpha_bar, alpha_prev, beta_now))

def adam_update(weight, first, second, ema, grad, rate):
    first_new = BETA_FIRST * first + (1.0 - BETA_FIRST) * grad
    second_new = BETA_SECOND * second + (1.0 - BETA_SECOND) * grad * grad
    corr_one = 1.0 - BETA_FIRST ** STEP
    corr_two = 1.0 - BETA_SECOND ** STEP
    weight_new = weight - rate * (first_new / corr_one / (jnp.sqrt(second_new / corr_two) + ADAM_EPSILON) + WEIGHT_DECAY * weight)
    return (first_new, second_new, weight_new, EMA_DECAY * ema + (1.0 - EMA_DECAY) * weight_new)

def reference(latents, noise, caption, caption_lens, timesteps, grid_hw, frame_counts, attn_mats, ffn_mats, embed_mats, vectors, attn_first, ffn_first, embed_first, vector_first, attn_second, ffn_second, embed_second, vector_second, attn_ema, ffn_ema, embed_ema, vector_ema):
    weights = (attn_mats, ffn_mats, embed_mats, vectors)
    groups = (latents, noise, caption.astype(jnp.float32), caption_lens, timesteps, grid_hw[:, 0], grid_hw[:, 1], frame_counts)
    frozen = lax.map(lambda group: group_forward(weights, group)[0][:, :CIN], groups)
    count = jnp.sum(frame_counts * grid_hw[:, 0] * grid_hw[:, 1]).astype(jnp.float32)

    def summed(weight_set):

        def one(total, item):
            group, fixed = item
            output, valid, extra = group_forward(weight_set, group)
            losses = token_losses(output, fixed, group[0], group[1], extra)
            return (total + jnp.sum(jnp.where(valid, losses, 0.0)), None)
        total, unused = lax.scan(jax.checkpoint(one), jnp.zeros((), jnp.float32), (groups, frozen))
        return total
    loss_sum, pullback = jax.vjp(summed, weights)
    grads = pullback(1.0 / count)[0]
    squares = sum((jnp.sum(grad * grad) for grad in grads))
    grad_norm = jnp.sqrt(squares)
    factor = CLIP_NORM / (grad_norm + 1e-06)
    firsts = (attn_first, ffn_first, embed_first, vector_first)
    seconds = (attn_second, ffn_second, embed_second, vector_second)
    emas = (attn_ema, ffn_ema, embed_ema, vector_ema)
    rates = (LEARN_RATE, LEARN_RATE, LEARN_RATE, VECTOR_RATE)
    updated = [adam_update(weights[i], firsts[i], seconds[i], emas[i], grads[i] * factor, rates[i]) for i in range(4)]
    return (loss_sum, count, grad_norm, updated[0][0], updated[1][0], updated[2][0], updated[3][0], updated[0][1], updated[1][1], updated[2][1], updated[3][1], updated[0][2], updated[1][2], updated[2][2], updated[3][2], updated[0][3], updated[1][3], updated[2][3], updated[3][3])
```

```python
import functools
import math

import jax
import jax.numpy as jnp
from jax import lax
from jax.experimental import pallas as pl
from jax.experimental.pallas import tpu as pltpu
from jax.sharding import PartitionSpec as P

D = 1152
HEADS = 16
HD = 72
FF = 4608
TFREQ = 256
TXT = 4096
CIN = 16
COUT = 32
CAP = 120
FR = 4
PM = 448
STEP = 5


EPS_NORM = 1e-06
LEARN_RATE = 0.03
VECTOR_RATE = 0.15
BETA_FIRST = 0.5
BETA_SECOND = 0.5
ADAM_EPSILON = 1e-08
WEIGHT_DECAY = 0.01
EMA_DECAY = 0.9
CLIP_NORM = 0.02
NEG_LARGE = -1e30
CONTRACT_ROWS = (((0,), (0,)), ((), ()))
CONTRACT_LAST = (((1,), (1,)), ((), ()))


def vector_parts():
    return [
        ("patch_w", (CIN, D)),
        ("patch_b", (D,)),
        ("final_w", (COUT, D)),
        ("final_b", (COUT,)),
        ("t_bias_one", (D,)),
        ("t_bias_two", (D,)),
        ("t_bias_mod", (6 * D,)),
        ("c_bias_one", (D,)),
        ("c_bias_two", (D,)),
        ("attn_bias", (3, 3, D)),
        ("ffn_bias_one", (2, FF)),
        ("ffn_bias_two", (2, D)),
        ("tables", (2, 6, D)),
        ("final_table", (2, D)),
    ]


def unpack(flat):
    result = {}
    offset = 0
    for label, extent in vector_parts():
        length = math.prod(extent)
        result[label] = flat[offset : offset + length].reshape(extent)
        offset += length
    return result


def waves(position, width):
    half = width // 2
    freqs = jnp.exp(-math.log(10000.0) * jnp.arange(half, dtype=jnp.float32) / half)
    angles = position[..., None] * freqs
    return jnp.concatenate([jnp.sin(angles), jnp.cos(angles)], -1)


def roster():
    betas = 0.0001 + (0.02 - 0.0001) * jnp.arange(1000, dtype=jnp.float32) / 999.0
    return (betas, jnp.exp(jnp.cumsum(jnp.log1p(-betas))))


def modulate(x, shift_vec, scale_vec):
    centered = x - jnp.mean(x, -1, keepdims=True)
    normed = centered * lax.rsqrt(jnp.mean(centered * centered, -1, keepdims=True) + EPS_NORM)
    return normed * (1.0 + scale_vec) + shift_vec


def gelu_tanh(values):
    return jax.nn.gelu(values, approximate=True)


def token_losses(output, frozen, latent, noise_part, extra):
    noisy, alpha_bar, alpha_prev, beta_now = extra
    eps = output[:, :CIN]
    var_raw = output[:, CIN:]
    mse = jnp.mean((eps - noise_part) ** 2, -1)
    post_var = beta_now * (1.0 - alpha_prev) / (1.0 - alpha_bar)
    log_post = jnp.log(post_var)
    frac = (var_raw + 1.0) / 2.0
    log_var = frac * jnp.log(beta_now) + (1.0 - frac) * log_post
    coef_start = beta_now * jnp.sqrt(alpha_prev) / (1.0 - alpha_bar)
    coef_now = (1.0 - alpha_prev) * jnp.sqrt(1.0 - beta_now) / (1.0 - alpha_bar)
    true_mean = coef_start * latent + coef_now * noisy
    guess = (noisy - jnp.sqrt(1.0 - alpha_bar) * frozen) / jnp.sqrt(alpha_bar)
    model_mean = coef_start * guess + coef_now * noisy
    kl_term = 0.5 * (
        -1.0
        + log_var
        - log_post
        + jnp.exp(log_post - log_var)
        + (true_mean - model_mean) ** 2 * jnp.exp(-log_var)
    )
    return mse + jnp.mean(kl_term, -1) / math.log(2.0)


def attention_forms(kind):
    if kind == "space":
        return ("fqhe,fkhe->fhqk", "fhqk,fkhe->fqhe", "fhqk,fqhe->fkhe")
    if kind == "time":
        return ("qphe,kphe->phqk", "phqk,kphe->qphe", "phqk,qphe->kphe")
    return ("qhe,khe->hqk", "hqk,khe->qhe", "hqk,qhe->khe")


def own_slice(vector, part, width):
    return lax.dynamic_slice_in_dim(vector, part * width, width, 0)


def placed(piece, part, full):
    return lax.dynamic_update_slice_in_dim(
        jnp.zeros((full,), jnp.float32), piece, part * piece.shape[0], 0
    )


def project_in(shard_rows, weight):
    piece = lax.all_gather(shard_rows, "mp", axis=0, tiled=True)
    product = jnp.dot(piece, weight, preferred_element_type=jnp.float32)
    return (product, piece)


def project_out(full_rows, weight_t):
    return lax.psum_scatter(
        lax.dot_general(
            full_rows, weight_t, CONTRACT_LAST, preferred_element_type=jnp.float32
        ).astype(jnp.bfloat16),
        "mp",
        scatter_dimension=0,
        tiled=True,
    ).astype(jnp.float32)


def back_out(grad_rows, full_rows, weight_t):
    piece = lax.all_gather(grad_rows, "mp", axis=0, tiled=True)
    product = jnp.dot(piece, weight_t, preferred_element_type=jnp.float32)
    d_weight = lax.dot_general(piece, full_rows, CONTRACT_ROWS, preferred_element_type=jnp.float32)
    return (product, d_weight)


def back_in(d_full, weight):
    return lax.psum_scatter(
        lax.dot_general(d_full, weight, CONTRACT_LAST, preferred_element_type=jnp.float32).astype(
            jnp.bfloat16
        ),
        "mp",
        scatter_dimension=0,
        tiled=True,
    ).astype(jnp.float32)


def attend_forward(query, key_rows, value_rows, keep, forms):
    scores = jnp.einsum(forms[0], query, key_rows, preferred_element_type=jnp.float32) * HD ** (
        -0.5
    )
    scores = jnp.where(keep, scores, NEG_LARGE)
    peak = jnp.max(scores, -1, keepdims=True)
    expd = jnp.exp(scores - peak)
    total = jnp.sum(expd, -1, keepdims=True)
    probs = (expd / total).astype(jnp.bfloat16)
    mixed = jnp.einsum(forms[1], probs, value_rows, preferred_element_type=jnp.float32)
    return (mixed, peak + jnp.log(total))


def attend_backward(query, key_rows, value_rows, keep, forms, logsum, d_mixed):
    scores = jnp.einsum(forms[0], query, key_rows, preferred_element_type=jnp.float32) * HD ** (
        -0.5
    )
    scores = jnp.where(keep, scores, NEG_LARGE)
    probs_full = jnp.exp(scores - logsum)
    probs = probs_full.astype(jnp.bfloat16)
    d_value = jnp.einsum(forms[2], probs, d_mixed, preferred_element_type=jnp.float32)
    d_probs = jnp.einsum(forms[0], d_mixed, value_rows, preferred_element_type=jnp.float32)
    offset = jnp.sum(d_probs * probs_full, -1, keepdims=True)
    d_scores = (probs_full * (d_probs - offset) * HD ** (-0.5)).astype(jnp.bfloat16)
    d_query = jnp.einsum(forms[1], d_scores, key_rows, preferred_element_type=jnp.float32)
    d_key = jnp.einsum(forms[2], d_scores, query, preferred_element_type=jnp.float32)
    return (d_query, d_key, d_value)


def attention_forward(x, index, mods, kind, setup):
    weight = setup["attn"][index]
    heads = weight.shape[1]
    width_local = heads * HD
    biases = setup["parts"]["attn_bias"][index]
    part = setup["part"]
    forms = attention_forms(kind)
    query_bias = own_slice(biases[0], part, width_local).reshape(heads, HD)
    value_bias = own_slice(biases[1], part, width_local).reshape(heads, HD)
    if kind == "cross":
        projected, gathered = project_in(
            x.astype(jnp.bfloat16), weight[:, :, 0, :].reshape(D, width_local)
        )
        query = projected.reshape(-1, heads, HD) + query_bias
        context = setup["context"]
        key_rows = jnp.einsum(
            "cd,dhe->che", context, weight[:, :, 1, :], preferred_element_type=jnp.float32
        )
        value_rows = (
            jnp.einsum(
                "cd,dhe->che", context, weight[:, :, 2, :], preferred_element_type=jnp.float32
            )
            + value_bias
        )
    else:
        source = modulate(x, mods[0], mods[1])
        projected, gathered = project_in(
            source.astype(jnp.bfloat16), weight[:, :, :3, :].reshape(D, 3 * width_local)
        )
        projected = projected.reshape(FR, PM, heads, 3, HD)
        query = projected[:, :, :, 0] + query_bias
        key_rows = projected[:, :, :, 1]
        value_rows = projected[:, :, :, 2] + value_bias
    query = query.astype(jnp.bfloat16)
    key_rows = key_rows.astype(jnp.bfloat16)
    value_rows = value_rows.astype(jnp.bfloat16)
    mixed, logsum = attend_forward(query, key_rows, value_rows, setup["keep"][kind], forms)
    mixed = mixed.reshape(-1, width_local).astype(jnp.bfloat16)
    branch = project_out(mixed, weight[:, :, 3, :].reshape(D, width_local)) + biases[2]
    saved = {
        "input": x,
        "gathered": gathered,
        "query": query,
        "key_rows": key_rows,
        "value_rows": value_rows,
        "logsum": logsum,
        "mixed": mixed,
        "branch": branch,
    }
    if kind == "cross":
        return (x + branch, saved)
    return (x + mods[2] * branch, saved)


def attention_backward(grad_x, index, mods, kind, saved, setup):
    weight = setup["attn"][index]
    heads = weight.shape[1]
    width_local = heads * HD
    part = setup["part"]
    forms = attention_forms(kind)
    query = saved["query"]
    if kind == "cross":
        gate_vec = 1.0
        d_gate = None
    else:
        gate_vec = mods[2]
        d_gate = jnp.sum(grad_x * saved["branch"], 0)
    d_branch = (gate_vec * grad_x).astype(jnp.bfloat16)
    d_out_bias = jnp.sum(d_branch.astype(jnp.float32), 0)
    d_mixed, d_out_weight = back_out(
        d_branch, saved["mixed"], weight[:, :, 3, :].reshape(D, width_local)
    )
    d_mixed = d_mixed.astype(jnp.bfloat16).reshape(query.shape)
    d_query, d_key, d_value = attend_backward(
        query,
        saved["key_rows"],
        saved["value_rows"],
        setup["keep"][kind],
        forms,
        saved["logsum"],
        d_mixed,
    )
    d_query = d_query.reshape(-1, heads, HD).astype(jnp.bfloat16)
    d_key = d_key.reshape(-1, heads, HD).astype(jnp.bfloat16)
    d_value = d_value.reshape(-1, heads, HD).astype(jnp.bfloat16)
    d_query_bias = jnp.sum(d_query.astype(jnp.float32), 0).reshape(-1)
    d_value_bias = jnp.sum(d_value.astype(jnp.float32), 0).reshape(-1)
    if kind == "cross":
        context = setup["context"]
        d_query_weight = lax.dot_general(
            saved["gathered"],
            d_query.reshape(-1, width_local),
            CONTRACT_ROWS,
            preferred_element_type=jnp.float32,
        ).reshape(D, heads, 1, HD)
        d_key_weight = jnp.einsum("cd,che->dhe", context, d_key, preferred_element_type=jnp.float32)
        d_value_weight = jnp.einsum(
            "cd,che->dhe", context, d_value, preferred_element_type=jnp.float32
        )
        d_in = jnp.concatenate(
            [d_query_weight, d_key_weight[:, :, None], d_value_weight[:, :, None]], 2
        )
        d_context = jnp.einsum(
            "che,dhe->cd", d_key, weight[:, :, 1, :], preferred_element_type=jnp.float32
        ) + jnp.einsum(
            "che,dhe->cd", d_value, weight[:, :, 2, :], preferred_element_type=jnp.float32
        )
        grad_x = grad_x + back_in(
            d_query.reshape(-1, width_local), weight[:, :, 0, :].reshape(D, width_local)
        )
        mod_grads = None
    else:
        d_proj = jnp.stack([d_query, d_key, d_value], 2).reshape(-1, 3 * width_local)
        d_in = lax.dot_general(
            saved["gathered"], d_proj, CONTRACT_ROWS, preferred_element_type=jnp.float32
        ).reshape(D, heads, 3, HD)
        d_source = back_in(d_proj, weight[:, :, :3, :].reshape(D, 3 * width_local))
        unused, norm_pull = jax.vjp(modulate, saved["input"], mods[0], mods[1])
        d_input, d_shift, d_scale = norm_pull(d_source)
        grad_x = grad_x + d_input
        mod_grads = (d_shift, d_scale, d_gate)
        d_context = None
    d_weight = jnp.concatenate([d_in, d_out_weight.reshape(D, heads, 1, HD)], 2)
    d_bias = jnp.stack([placed(d_query_bias, part, D), placed(d_value_bias, part, D), d_out_bias])
    return (grad_x, d_weight, d_bias, mod_grads, d_context)


def ffn_forward(x, index, mods, setup):
    weight_in = setup["ffn"][index, 0]
    weight_out = setup["ffn"][index, 1]
    source = modulate(x, mods[3], mods[4])
    pre, gathered = project_in(source.astype(jnp.bfloat16), weight_in)
    pre = pre + own_slice(setup["parts"]["ffn_bias_one"][index], setup["part"], weight_in.shape[1])
    hidden = gelu_tanh(pre).astype(jnp.bfloat16)
    branch = project_out(hidden, weight_out) + setup["parts"]["ffn_bias_two"][index]
    saved = {"input": x, "gathered": gathered, "pre": pre, "hidden": hidden, "branch": branch}
    return (x + mods[5] * branch, saved)


def ffn_backward(grad_x, index, mods, saved, setup):
    weight_in = setup["ffn"][index, 0]
    weight_out = setup["ffn"][index, 1]
    d_gate = jnp.sum(grad_x * saved["branch"], 0)
    d_branch = (mods[5] * grad_x).astype(jnp.bfloat16)
    d_bias_two = jnp.sum(d_branch.astype(jnp.float32), 0)
    d_hidden, d_weight_out = back_out(d_branch, saved["hidden"], weight_out)
    unused, gelu_pull = jax.vjp(gelu_tanh, saved["pre"])
    d_pre = gelu_pull(d_hidden)[0].astype(jnp.bfloat16)
    d_bias_one = jnp.sum(d_pre.astype(jnp.float32), 0)
    d_weight_in = lax.dot_general(
        saved["gathered"], d_pre, CONTRACT_ROWS, preferred_element_type=jnp.float32
    )
    d_source = back_in(d_pre, weight_in)
    unused, norm_pull = jax.vjp(modulate, saved["input"], mods[3], mods[4])
    d_input, d_shift, d_scale = norm_pull(d_source)
    biases = (placed(d_bias_one, setup["part"], FF), d_bias_two)
    return (
        grad_x + d_input,
        jnp.stack([d_weight_in, d_weight_out]),
        biases,
        (d_shift, d_scale, d_gate),
    )


def block_forward(x, kind, mods, setup):
    index = 0 if kind == "space" else 1
    x, first = attention_forward(x, index, mods, kind, setup)
    second = None
    if kind == "space":
        x, second = attention_forward(x, 2, mods, "cross", setup)
    x, third = ffn_forward(x, index, mods, setup)
    return (x, (first, second, third))


def block_backward(grad_x, kind, mods, saved, setup):
    index = 0 if kind == "space" else 1
    first, second, third = saved
    grad_x, d_ffn, d_ffn_bias, ffn_mods = ffn_backward(grad_x, index, mods, third, setup)
    cross_part = None
    if kind == "space":
        grad_x, d_cross, d_cross_bias, unused, d_context = attention_backward(
            grad_x, 2, mods, "cross", second, setup
        )
        cross_part = (d_cross, d_cross_bias, d_context)
    grad_x, d_attn, d_attn_bias, attn_mods, unused = attention_backward(
        grad_x, index, mods, kind, first, setup
    )
    d_mods = jnp.stack(list(attn_mods) + list(ffn_mods))
    return (grad_x, (d_attn, d_attn_bias, d_ffn, d_ffn_bias, d_mods), cross_part)


def adam_update(weight, first, second, ema, grad, rate):
    first_new = BETA_FIRST * first + (1.0 - BETA_FIRST) * grad
    second_new = BETA_SECOND * second + (1.0 - BETA_SECOND) * grad * grad
    corr_one = 1.0 - BETA_FIRST**STEP
    corr_two = 1.0 - BETA_SECOND**STEP
    weight_new = weight - rate * (
        first_new / corr_one / (jnp.sqrt(second_new / corr_two) + ADAM_EPSILON)
        + WEIGHT_DECAY * weight
    )
    return (first_new, second_new, weight_new, EMA_DECAY * ema + (1.0 - EMA_DECAY) * weight_new)


def per_device(
    latents,
    noise,
    caption,
    caption_lens,
    timesteps,
    grid_hw,
    frame_counts,
    attn_mats,
    ffn_mats,
    embed_mats,
    vectors,
    attn_first,
    ffn_first,
    embed_first,
    vector_first,
    attn_second,
    ffn_second,
    embed_second,
    vector_second,
    attn_ema,
    ffn_ema,
    embed_ema,
    vector_ema,
):
    group = lax.axis_index("dp")
    part = lax.axis_index("mp")
    mp_size = lax.axis_size("mp")
    rows = latents.shape[1]
    heads = HEADS // mp_size
    width_local = D // mp_size
    attn_all, ffn_all, embed_all = (
        lax.all_gather(attn_mats.astype(jnp.bfloat16), "dp", axis=1, tiled=True),
        lax.all_gather(ffn_mats.astype(jnp.bfloat16), "dp", axis=2, tiled=True),
        lax.all_gather(embed_mats.astype(jnp.bfloat16), "dp", axis=0, tiled=True),
    )
    parts = unpack(vectors)
    pick = jnp.arange(timesteps.shape[0], dtype=jnp.int32) == group

    def select(values):
        return jnp.sum(jnp.where(pick, values, 0))

    tstep = select(timesteps)
    cap_len = select(caption_lens)
    height = select(grid_hw[:, 0])
    width_grid = select(grid_hw[:, 1])
    frames = select(frame_counts)
    count = jnp.sum(frame_counts * grid_hw[:, 0] * grid_hw[:, 1]).astype(jnp.float32)
    betas, cumul = roster()
    step_ids = jnp.arange(1000, dtype=jnp.int32)
    alpha_bar = jnp.sum(jnp.where(step_ids == tstep, cumul, 0.0))
    alpha_prev = jnp.sum(jnp.where(step_ids == tstep - 1, cumul, 0.0))
    beta_now = jnp.sum(jnp.where(step_ids == tstep, betas, 0.0))
    t_one = embed_all[:TFREQ]
    c_one = embed_all[TFREQ : TFREQ + TXT]
    t_two = embed_all[TFREQ + TXT : TFREQ + TXT + D]
    c_two = embed_all[TFREQ + TXT + D : TFREQ + TXT + 2 * D]
    t_mod = embed_all[TFREQ + TXT + 2 * D :]
    freq = waves(tstep.astype(jnp.float32), TFREQ).astype(jnp.bfloat16)
    t_pre = jnp.dot(freq, t_one, preferred_element_type=jnp.float32) + own_slice(
        parts["t_bias_one"], part, width_local
    )
    t_hidden = jax.nn.silu(t_pre).astype(jnp.bfloat16)
    t_part = jnp.dot(t_two, t_hidden, preferred_element_type=jnp.float32)
    caption_rows = caption[0]
    c_pre = jnp.dot(caption_rows, c_one, preferred_element_type=jnp.float32) + own_slice(
        parts["c_bias_one"], part, width_local
    )
    c_hidden = gelu_tanh(c_pre).astype(jnp.bfloat16)
    c_part = lax.dot_general(c_hidden, c_two, CONTRACT_LAST, preferred_element_type=jnp.float32)
    t_sum, c_sum = (
        lax.psum(t_part.astype(jnp.bfloat16), "mp").astype(jnp.float32),
        lax.psum(c_part.astype(jnp.bfloat16), "mp").astype(jnp.float32),
    )
    t_emb = t_sum + parts["t_bias_two"]
    context = (c_sum + parts["c_bias_two"]).astype(jnp.bfloat16)
    t_emb_local = own_slice(t_emb, part, width_local)
    silu_local = jax.nn.silu(t_emb_local).astype(jnp.bfloat16)
    t_mod_vec = (
        lax.psum(jnp.dot(t_mod, silu_local, preferred_element_type=jnp.float32), "mp")
        + parts["t_bias_mod"]
    )
    token_ids = part * rows + jnp.arange(rows, dtype=jnp.int32)
    frame_slot = token_ids // PM
    patch_slot = token_ids % PM
    area = height * width_grid
    shifted = patch_slot - (PM - area)
    valid = (frame_slot >= FR - frames) & (patch_slot >= PM - area)
    setup = {
        "attn": attn_all.reshape(3, D, heads, 4, HD),
        "ffn": ffn_all,
        "parts": parts,
        "part": part,
        "context": context,
        "keep": {
            "space": (jnp.arange(PM, dtype=jnp.int32) >= PM - area).reshape(1, 1, 1, PM),
            "time": (jnp.arange(FR, dtype=jnp.int32) >= FR - frames).reshape(1, 1, 1, FR),
            "cross": (jnp.arange(CAP, dtype=jnp.int32) < cap_len).reshape(1, 1, CAP),
        },
    }
    noisy = jnp.sqrt(alpha_bar) * latents[0] + jnp.sqrt(1.0 - alpha_bar) * noise[0]
    noisy_low = noisy.astype(jnp.bfloat16)
    position = jnp.concatenate(
        [
            waves((shifted // width_grid).astype(jnp.float32), D // 2),
            waves((shifted % width_grid).astype(jnp.float32), D // 2),
        ],
        -1,
    )
    x = jnp.dot(
        noisy_low, parts["patch_w"].astype(jnp.bfloat16), preferred_element_type=jnp.float32
    )
    x = x + parts["patch_b"] + position
    tables = parts["tables"] + t_mod_vec.reshape(1, 6, D)
    x, saved_space = block_forward(x, "space", tables[0], setup)
    x = x + waves((frame_slot - (FR - frames)).astype(jnp.float32), D)
    x, saved_time = block_forward(x, "time", tables[1], setup)
    final_mods = parts["final_table"] + t_emb
    final_source = modulate(x, final_mods[0], final_mods[1]).astype(jnp.bfloat16)
    final_low = parts["final_w"].astype(jnp.bfloat16)
    output = (
        lax.dot_general(final_source, final_low, CONTRACT_LAST, preferred_element_type=jnp.float32)
        + parts["final_b"]
    )
    frozen = output[:, :CIN]

    def shard_loss(values):
        losses = token_losses(
            values, frozen, latents[0], noise[0], (noisy, alpha_bar, alpha_prev, beta_now)
        )
        return jnp.sum(jnp.where(valid, losses, 0.0))

    loss_part, loss_pull = jax.vjp(shard_loss, output)
    loss_total = lax.psum(loss_part, ("dp", "mp"))
    d_output = loss_pull(1.0 / count)[0].astype(jnp.bfloat16)
    d_final_w = lax.dot_general(
        d_output, final_source, CONTRACT_ROWS, preferred_element_type=jnp.float32
    )
    d_final_b = jnp.sum(d_output.astype(jnp.float32), 0)
    d_final_source = jnp.dot(d_output, final_low, preferred_element_type=jnp.float32)
    unused, final_pull = jax.vjp(modulate, x, final_mods[0], final_mods[1])
    grad_x, d_final_shift, d_final_scale = final_pull(d_final_source)
    grad_x, time_grads, unused = block_backward(grad_x, "time", tables[1], saved_time, setup)
    grad_x, space_grads, cross_grads = block_backward(
        grad_x, "space", tables[0], saved_space, setup
    )
    d_patch = grad_x.astype(jnp.bfloat16)
    d_patch_b = jnp.sum(d_patch.astype(jnp.float32), 0)
    d_patch_w = lax.dot_general(
        noisy_low, d_patch, CONTRACT_ROWS, preferred_element_type=jnp.float32
    )
    d_mod_part = space_grads[4].reshape(-1) + time_grads[4].reshape(-1)
    d_temb_part = d_final_shift + d_final_scale
    d_mod_vec, d_temb_sum, d_context = (
        lax.psum(d_mod_part.astype(jnp.bfloat16), "mp").astype(jnp.float32),
        lax.psum(d_temb_part.astype(jnp.bfloat16), "mp").astype(jnp.float32),
        lax.psum(cross_grads[2].astype(jnp.bfloat16), "mp").astype(jnp.float32),
    )
    d_t_mod = jnp.outer(d_mod_vec, silu_local.astype(jnp.float32))
    d_silu_local = jnp.dot(d_mod_vec, t_mod, preferred_element_type=jnp.float32)
    unused, silu_pull = jax.vjp(jax.nn.silu, t_emb_local)
    d_temb_local = silu_pull(d_silu_local)[0]
    d_temb = d_temb_sum + lax.all_gather(d_temb_local, "mp", axis=0, tiled=True)
    d_t_two = jnp.outer(d_temb, t_hidden.astype(jnp.float32))
    d_t_hidden = jnp.dot(d_temb, t_two, preferred_element_type=jnp.float32)
    unused, pre_pull = jax.vjp(jax.nn.silu, t_pre)
    d_t_pre = pre_pull(d_t_hidden)[0]
    d_t_one = jnp.outer(freq.astype(jnp.float32), d_t_pre)
    d_context = d_context.astype(jnp.bfloat16)
    d_c_bias_two = jnp.sum(d_context.astype(jnp.float32), 0) * (part == 0).astype(jnp.float32)
    d_c_two = lax.dot_general(
        d_context, c_hidden, CONTRACT_ROWS, preferred_element_type=jnp.float32
    )
    d_c_hidden = jnp.dot(d_context, c_two, preferred_element_type=jnp.float32)
    unused, cap_pull = jax.vjp(gelu_tanh, c_pre)
    d_c_pre = cap_pull(d_c_hidden)[0].astype(jnp.bfloat16)
    d_c_one = lax.dot_general(
        caption_rows, d_c_pre, CONTRACT_ROWS, preferred_element_type=jnp.float32
    )
    d_c_bias_one = jnp.sum(d_c_pre.astype(jnp.float32), 0)
    d_attn = jnp.stack([space_grads[0], time_grads[0], cross_grads[0]]).reshape(
        3, D, heads * 4 * HD
    )
    d_ffn = jnp.stack([space_grads[2], time_grads[2]])
    d_embed = jnp.concatenate([d_t_one, d_c_one, d_t_two, d_c_two, d_t_mod], 0)
    vector_grads = {
        "patch_w": d_patch_w,
        "patch_b": d_patch_b,
        "final_w": d_final_w,
        "final_b": d_final_b,
        "t_bias_one": placed(d_t_pre, part, D),
        "t_bias_two": d_temb_part + placed(d_temb_local, part, D),
        "t_bias_mod": d_mod_part,
        "c_bias_one": placed(d_c_bias_one, part, D),
        "c_bias_two": d_c_bias_two,
        "attn_bias": jnp.stack([space_grads[1], time_grads[1], cross_grads[1]]),
        "ffn_bias_one": jnp.stack([space_grads[3][0], time_grads[3][0]]),
        "ffn_bias_two": jnp.stack([space_grads[3][1], time_grads[3][1]]),
        "tables": jnp.stack([space_grads[4], time_grads[4]]),
        "final_table": jnp.stack([d_final_shift, d_final_scale]),
    }
    vector_grad = jnp.concatenate(
        [vector_grads[label].reshape(-1) for label, extent in vector_parts()]
    )
    g_attn, g_ffn, g_embed = (
        lax.psum_scatter(d_attn.astype(jnp.bfloat16), "dp", scatter_dimension=1, tiled=True).astype(
            jnp.float32
        ),
        lax.psum_scatter(d_ffn.astype(jnp.bfloat16), "dp", scatter_dimension=2, tiled=True).astype(
            jnp.float32
        ),
        lax.psum_scatter(
            d_embed.astype(jnp.bfloat16), "dp", scatter_dimension=0, tiled=True
        ).astype(jnp.float32),
    )
    g_vector = lax.psum(vector_grad, ("dp", "mp"))
    matrix_squares = jnp.sum(g_attn * g_attn) + jnp.sum(g_ffn * g_ffn) + jnp.sum(g_embed * g_embed)
    squares = lax.psum(matrix_squares, ("dp", "mp")) + jnp.sum(g_vector * g_vector)
    grad_norm = jnp.sqrt(squares)
    factor = CLIP_NORM / (grad_norm + 1e-06)
    new_attn = adam_update(
        attn_mats, attn_first, attn_second, attn_ema, g_attn * factor, LEARN_RATE
    )
    new_ffn = adam_update(ffn_mats, ffn_first, ffn_second, ffn_ema, g_ffn * factor, LEARN_RATE)
    new_embed = adam_update(
        embed_mats, embed_first, embed_second, embed_ema, g_embed * factor, LEARN_RATE
    )
    new_vector = adam_update(
        vectors, vector_first, vector_second, vector_ema, g_vector * factor, VECTOR_RATE
    )
    return (
        loss_total,
        count,
        grad_norm,
        new_attn[0],
        new_ffn[0],
        new_embed[0],
        new_vector[0],
        new_attn[1],
        new_ffn[1],
        new_embed[1],
        new_vector[1],
        new_attn[2],
        new_ffn[2],
        new_embed[2],
        new_vector[2],
        new_attn[3],
        new_ffn[3],
        new_embed[3],
        new_vector[3],
    )


SPAN = 4 * HD
EMB_ALL = TFREQ + TXT + 8 * D
EMB_LOCAL = EMB_ALL // 8
MESH = pl.DeviceIdType.MESH
BLOCK = 144


class Chips:
    def __init__(self):
        dp = lax.axis_index("dp")
        mp = lax.axis_index("mp")
        self.z, self.x = dp // 2, dp % 2
        self.y, self.c = mp // 2, mp % 2

    def z_at(self, j):
        z = self.z
        return (z, z + 1 - 2 * (z % 2), z + 2 - 4 * (z // 2), 3 - z)[j]

    def dp_at(self, jz, jx):
        return self.z_at(jz) * 2 + (1 - self.x if jx else self.x)

    def mp_at(self, jy, jc):
        return (1 - self.y if jy else self.y) * 2 + (1 - self.c if jc else self.c)

    def peer_x(self):
        return {"dp": self.dp_at(0, 1)}

    def peer_y(self):
        return {"mp": self.mp_at(1, 0)}

    def peer_core(self):
        return {"mp": self.mp_at(0, 1)}

    def peer_z(self, j):
        return {"dp": self.dp_at(j, 0)}

    def greet(self):
        barrier = pltpu.get_barrier_semaphore()
        peers = [self.peer_x(), self.peer_y(), self.peer_core()]
        peers += [self.peer_z(j) for j in (1, 2, 3)]
        for peer in peers:
            pl.semaphore_signal(barrier, inc=1, device_id=peer, device_id_type=MESH)
        pl.semaphore_wait(barrier, len(peers))


class Gather:
    def __init__(self, chips, shard, full, send, recv, local):
        self.chips, self.shard, self.full = chips, shard, full
        self.send, self.recv, self.local = send, recv, local
        self.started = []

    def block(self, jy, jz, jx, jc=0):
        chips = self.chips
        return self.full.at[:, chips.mp_at(jy, jc), chips.dp_at(jz, jx)]

    def start(self, src, dst, slot, peer):
        copy = pltpu.make_async_remote_copy(
            src_ref=src,
            dst_ref=dst,
            send_sem=self.send.at[slot],
            recv_sem=self.recv.at[slot],
            device_id=peer,
            device_id_type=MESH,
        )
        copy.start()
        self.started.append(copy)

    def arrive(self, jy, jz, jx, jc=0):
        slot = jc * 16 + jy * 8 + jz * 2 + jx
        block = self.block(jy, jz, jx, jc)
        pltpu.make_async_remote_copy(
            src_ref=block,
            dst_ref=block,
            send_sem=self.send.at[slot],
            recv_sem=self.recv.at[slot],
            device_id=self.chips.peer_core(),
            device_id_type=MESH,
        ).wait_recv()

    def core(self, jy, jz, jx, src=None):
        block = self.block(jy, jz, jx)
        self.start(block if src is None else src, block, 16 + jy * 8 + jz * 2 + jx, self.chips.peer_core())

    def first(self):
        chips, own = self.chips, self.block(0, 0, 0)
        self.start(self.shard, own, 1, chips.peer_x())
        self.start(self.shard, own, 8, chips.peer_y())
        for j in (1, 2, 3):
            self.start(self.shard, own, 2 * j, chips.peer_z(j))
        self.core(0, 0, 0, self.shard)
        self.own = pltpu.make_async_copy(self.shard, own, self.local)
        self.own.start()

    def second(self, jz):
        self.arrive(0, jz, 0)
        block = self.block(0, jz, 0)
        self.start(block, block, jz * 2 + 1, self.chips.peer_x())
        self.start(block, block, jz * 2 + 8, self.chips.peer_y())
        self.core(0, jz, 0)

    def third(self, jz):
        if jz < 2:
            self.arrive(0, jz, 1)
            block, peer = self.block(0, jz, 1), self.chips.peer_y()
        else:
            self.arrive(1, jz, 0)
            block, peer = self.block(1, jz, 0), self.chips.peer_x()
        self.start(block, block, 8 + jz * 2 + 1, peer)
        self.core(0 if jz < 2 else 1, jz, 1 if jz < 2 else 0)

    def fourth(self, jz):
        if jz < 2:
            self.arrive(1, jz, 0)
            self.core(1, jz, 0)
        else:
            self.arrive(0, jz, 1)
            self.core(0, jz, 1)

    def fifth(self, jz):
        self.arrive(1, jz, 1)
        self.core(1, jz, 1)

    def last(self):
        self.own.wait()
        for jy in range(2):
            for jz in range(4):
                for jx in range(2):
                    self.arrive(jy, jz, jx, 1)
        for copy in self.started:
            copy.wait_send()

    def steps(self):
        order = (0, 2, 1, 3)
        parts = [[self.first]]
        parts.append([functools.partial(self.second, j) for j in (1, 2, 3)])
        parts.append([functools.partial(self.third, j) for j in order])
        parts.append([functools.partial(self.fourth, j) for j in order])
        parts.append([functools.partial(self.fifth, j) for j in order])
        parts.append([self.last])
        return parts


GATHER_SEMS = [
    pltpu.SemaphoreType.DMA((32,)),
    pltpu.SemaphoreType.DMA((32,)),
    pltpu.SemaphoreType.DMA,
]


def gather_kernel(count, *refs):
    shards, fulls, sems = refs[:count], refs[count : 2 * count], refs[2 * count :]
    chips = Chips()
    chips.greet()
    plans = [Gather(chips, shards[i], fulls[i], *sems[3 * i : 3 * i + 3]).steps() for i in range(count)]
    for turn in range(count + 5):
        for i in range(count):
            phase = turn - i
            if 0 <= phase < 6:
                for step in plans[i][phase]:
                    step()


def gather_all(shards, ident):
    count = len(shards)
    return pl.pallas_call(
        functools.partial(gather_kernel, count),
        out_shape=[jax.ShapeDtypeStruct((s.shape[0], 4, 8) + s.shape[1:], s.dtype) for s in shards],
        in_specs=[pl.BlockSpec(memory_space=pl.ANY)] * count,
        out_specs=[pl.BlockSpec(memory_space=pl.ANY)] * count,
        scratch_shapes=GATHER_SEMS * count,
        compiler_params=pltpu.CompilerParams(collective_id=ident, has_side_effects=True),
    )(*shards)


class Scatter:
    def __init__(self, chips, full, total, own, near, far, send, recv, load):
        self.chips, self.full, self.total = chips, full, total
        self.own, self.near, self.far = own, near, far
        self.send, self.recv, self.load = send, recv, load
        self.started = []

    def start(self, src, dst, slot, peer):
        copy = pltpu.make_async_remote_copy(
            src_ref=src,
            dst_ref=dst,
            send_sem=self.send.at[slot],
            recv_sem=self.recv.at[slot],
            device_id=peer,
            device_id_type=MESH,
        )
        copy.start()
        self.started.append(copy)

    def arrive(self, dst, slot):
        pltpu.make_async_remote_copy(
            src_ref=dst,
            dst_ref=dst,
            send_sem=self.send.at[slot],
            recv_sem=self.recv.at[slot],
            device_id=self.chips.peer_core(),
            device_id_type=MESH,
        ).wait_recv()

    def order(self):
        out = [(1, jz, 1) for jz in (0, 2, 1, 3)]
        out += [(1 - (jz < 2), jz, 0 + (jz < 2)) for jz in (0, 2, 1, 3)]
        out += [(0 + (jz < 2), jz, 1 - (jz < 2)) for jz in (0, 2, 1, 3)]
        return out + [(0, jz, 0) for jz in (1, 2, 3, 0)]

    def first(self):
        chips = self.chips
        self.loads = {}
        for jy, jz, jx in self.order():
            slot = jy * 8 + jz * 2 + jx
            dp = chips.dp_at(jz, jx)
            self.start(self.full.at[:, chips.mp_at(jy, 1), dp], self.near.at[slot], slot, chips.peer_core())
            copy = pltpu.make_async_copy(
                self.full.at[:, chips.mp_at(jy, 0), dp], self.own.at[slot], self.load.at[slot]
            )
            copy.start()
            self.loads[slot] = copy

    def add(self, slot, others):
        own = self.own

        def rows(i, carry):
            at = pl.ds(pl.multiple_of(i * 16, 16), 16)
            for m in range(own.shape[1]):
                value = own[slot, m, at].astype(jnp.float32)
                for ref, index in others:
                    value += ref[index, m, at].astype(jnp.float32)
                own[slot, m, at] = value.astype(jnp.bfloat16)
            return carry

        lax.fori_loop(0, BLOCK // 16, rows, 0)

    def pair(self, slot):
        self.loads[slot].wait()
        self.arrive(self.near.at[slot], slot)

    def diagonal(self, jz):
        slot = 8 + jz * 2 + 1
        self.pair(slot)
        self.add(slot, [(self.near, slot)])
        peer = self.chips.peer_y() if jz < 2 else self.chips.peer_x()
        self.start(self.own.at[slot], self.far.at[jz], 16 + jz, peer)

    def straight(self, jz):
        slot = jz * 2 + (8 if jz < 2 else 1)
        self.pair(slot)
        self.add(slot, [(self.near, slot)])
        if jz < 2:
            self.start(self.own.at[slot], self.far.at[8 + jz], 24 + jz, self.chips.peer_y())
        else:
            self.start(self.own.at[slot], self.far.at[4 + jz], 20 + jz, self.chips.peer_x())

    def bent(self, jz):
        slot = jz * 2 + (1 if jz < 2 else 8)
        self.pair(slot)
        self.arrive(self.far.at[jz], 16 + jz)
        self.add(slot, [(self.near, slot), (self.far, jz)])
        if jz < 2:
            self.start(self.own.at[slot], self.far.at[4 + jz], 20 + jz, self.chips.peer_x())
        else:
            self.start(self.own.at[slot], self.far.at[8 + jz], 24 + jz, self.chips.peer_y())

    def column(self, jz):
        slot = jz * 2
        self.pair(slot)
        self.arrive(self.far.at[4 + jz], 20 + jz)
        self.arrive(self.far.at[8 + jz], 24 + jz)
        if jz:
            self.add(slot, [(self.near, slot), (self.far, 4 + jz), (self.far, 8 + jz)])
            self.start(self.own.at[slot], self.far.at[11 + jz], 27 + jz, self.chips.peer_z(jz))

    def last(self):
        for jz in (1, 2, 3):
            self.arrive(self.far.at[11 + jz], 27 + jz)
        own, near, far, total = self.own, self.near, self.far, self.total

        def rows(i, carry):
            at = pl.ds(pl.multiple_of(i * 16, 16), 16)
            for m in range(own.shape[1]):
                value = own[0, m, at].astype(jnp.float32) + near[0, m, at].astype(jnp.float32)
                for index in (4, 8, 12, 13, 14):
                    value += far[index, m, at].astype(jnp.float32)
                total[m, at] = value
            return carry

        lax.fori_loop(0, BLOCK // 16, rows, 0)
        for copy in self.started:
            copy.wait_send()

    def steps(self):
        order = (0, 2, 1, 3)
        parts = [self.first]
        parts += [functools.partial(self.diagonal, j) for j in order]
        parts += [functools.partial(self.straight, j) for j in order]
        parts += [functools.partial(self.bent, j) for j in order]
        parts += [functools.partial(self.column, j) for j in (1, 2, 3, 0)]
        return parts + [self.last]


def scatter_scratch(k):
    return [
        pltpu.VMEM((16, k, BLOCK, 1152), jnp.bfloat16),
        pltpu.VMEM((16, k, BLOCK, 1152), jnp.bfloat16),
        pltpu.VMEM((15, k, BLOCK, 1152), jnp.bfloat16),
        pltpu.SemaphoreType.DMA((31,)),
        pltpu.SemaphoreType.DMA((31,)),
        pltpu.SemaphoreType.DMA((16,)),
    ]


def scatter_kernel(full, total, *scratch):
    chips = Chips()
    chips.greet()
    for step in Scatter(chips, full, total, *scratch).steps():
        step()


def scatter_one(full, ident):
    k = full.shape[0]
    return pl.pallas_call(
        scatter_kernel,
        out_shape=jax.ShapeDtypeStruct((k,) + full.shape[3:], jnp.float32),
        in_specs=[pl.BlockSpec(memory_space=pl.ANY)],
        out_specs=pl.BlockSpec(memory_space=pltpu.VMEM),
        scratch_shapes=scatter_scratch(k),
        compiler_params=pltpu.CompilerParams(
            collective_id=ident, has_side_effects=True, vmem_limit_bytes=56 * 2**20
        ),
    )(full)


def chip_forward_attention(source, panels, biases, keep, forms, rows):
    query, key_rows, value_rows = [], [], []
    for m in range(4):
        product = jnp.dot(source, panels[m][:, : 3 * SPAN], preferred_element_type=jnp.float32)
        query.append(product[:, :SPAN])
        key_rows.append(product[:, SPAN : 2 * SPAN])
        value_rows.append(product[:, 2 * SPAN :])
    query = (jnp.concatenate(query, 1) + biases[0]).astype(jnp.bfloat16).reshape(rows + (HEADS, HD))
    key_rows = jnp.concatenate(key_rows, 1).astype(jnp.bfloat16).reshape(rows + (HEADS, HD))
    value_rows = (jnp.concatenate(value_rows, 1) + biases[1]).astype(jnp.bfloat16)
    value_rows = value_rows.reshape(rows + (HEADS, HD))
    mixed, logsum = attend_forward(query, key_rows, value_rows, keep, forms)
    mixed = mixed.astype(jnp.bfloat16).reshape(-1, D)
    branch = out_product(mixed, panels) + biases[2]
    return branch, (query, key_rows, value_rows, logsum, mixed)


def out_product(mixed, panels):
    branch = 0.0
    for m in range(4):
        branch += lax.dot_general(
            mixed[:, m * SPAN : (m + 1) * SPAN],
            panels[m][:, 3 * SPAN :],
            CONTRACT_LAST,
            preferred_element_type=jnp.float32,
        )
    return branch


def chip_backward_attention(d_branch, source, panels, keep, forms, saved):
    query, key_rows, value_rows, logsum, mixed = saved
    d_mixed = jnp.concatenate(
        [jnp.dot(d_branch, panels[m][:, 3 * SPAN :], preferred_element_type=jnp.float32) for m in range(4)],
        1,
    )
    d_mixed = d_mixed.astype(jnp.bfloat16).reshape(query.shape)
    d_query, d_key, d_value = attend_backward(
        query, key_rows, value_rows, keep, forms, logsum, d_mixed
    )
    flat = lambda value: value.astype(jnp.bfloat16).reshape(-1, D)
    d_query, d_key, d_value = flat(d_query), flat(d_key), flat(d_value)
    sums = [jnp.sum(value.astype(jnp.float32), 0) for value in (d_query, d_value, d_branch)]
    grads, d_source = [], 0.0
    for m in range(4):
        at = slice(m * SPAN, (m + 1) * SPAN)
        d_proj = jnp.concatenate([d_query[:, at], d_key[:, at], d_value[:, at]], 1)
        d_source += lax.dot_general(
            d_proj, panels[m][:, : 3 * SPAN], CONTRACT_LAST, preferred_element_type=jnp.float32
        )
        d_in = lax.dot_general(source, d_proj, CONTRACT_ROWS, preferred_element_type=jnp.float32)
        d_out = lax.dot_general(
            d_branch, mixed[:, at], CONTRACT_ROWS, preferred_element_type=jnp.float32
        )
        grads.append(jnp.concatenate([d_in, d_out], 1).astype(jnp.bfloat16))
    return d_source, jnp.stack(grads), jnp.stack(sums)


def chip_ffn_forward(source, w_in, w_out, bias_one, bias_two):
    pre, hidden, branch = [], [], bias_two
    for m in range(4):
        value = jnp.dot(source, w_in[m], preferred_element_type=jnp.float32)
        value = value + bias_one[m * D : (m + 1) * D]
        pre.append(value)
        hidden.append(gelu_tanh(value).astype(jnp.bfloat16))
        branch = branch + lax.dot_general(
            hidden[m], w_out[m], CONTRACT_LAST, preferred_element_type=jnp.float32
        )
    return branch, (pre, hidden)


def chip_ffn_backward(d_branch, source, w_in, w_out, saved):
    pre, hidden = saved
    d_source, d_win, d_wout, d_bias = 0.0, [], [], []
    for m in range(4):
        d_hidden = jnp.dot(d_branch, w_out[m], preferred_element_type=jnp.float32)
        unused, gelu_pull = jax.vjp(gelu_tanh, pre[m])
        d_pre = gelu_pull(d_hidden)[0].astype(jnp.bfloat16)
        d_bias.append(jnp.sum(d_pre.astype(jnp.float32), 0))
        d_source += lax.dot_general(
            d_pre, w_in[m], CONTRACT_LAST, preferred_element_type=jnp.float32
        )
        d_win.append(
            lax.dot_general(
                source, d_pre, CONTRACT_ROWS, preferred_element_type=jnp.float32
            ).astype(jnp.bfloat16)
        )
        d_wout.append(
            lax.dot_general(
                d_branch, hidden[m], CONTRACT_ROWS, preferred_element_type=jnp.float32
            ).astype(jnp.bfloat16)
        )
    return d_source, jnp.stack([jnp.stack(d_win), jnp.stack(d_wout)]), jnp.concatenate(d_bias)


def modulate_back(x, shift_vec, scale_vec, grad):
    unused, pull = jax.vjp(modulate, x, shift_vec, scale_vec)
    return pull(grad)


def local_rows(full, group):
    return lax.dynamic_slice_in_dim(full, group * EMB_LOCAL, EMB_LOCAL, 1)


def per_device_chips(
    latents,
    noise,
    caption,
    caption_lens,
    timesteps,
    grid_hw,
    frame_counts,
    attn_mats,
    ffn_mats,
    embed_mats,
    vectors,
    attn_first,
    ffn_first,
    embed_first,
    vector_first,
    attn_second,
    ffn_second,
    embed_second,
    vector_second,
    attn_ema,
    ffn_ema,
    embed_ema,
    vector_ema,
):
    group = lax.axis_index("dp")
    part = lax.axis_index("mp")
    clips = timesteps.shape[0]
    parts = unpack(vectors)
    bf16 = jnp.bfloat16
    f32 = jnp.float32

    attn_low = attn_mats.astype(bf16).reshape(3, BLOCK, 4, 4, HD).swapaxes(2, 3).reshape(3, BLOCK, D)
    ffn_low = ffn_mats.astype(bf16)
    fulls = gather_all([attn_low[0:1], attn_low[2:3], ffn_low[0], attn_low[1:2], ffn_low[1]], 0)
    w_space, w_cross, w_ffn0, w_time, w_ffn1 = [f.reshape(f.shape[:2] + (D, D)) for f in fulls]
    w_space, w_cross, w_time = w_space[0], w_cross[0], w_time[0]

    pick = jnp.arange(clips, dtype=jnp.int32) == group

    def select(values):
        return jnp.sum(jnp.where(pick, values, 0))

    tstep = select(timesteps)
    cap_len = select(caption_lens)
    height = select(grid_hw[:, 0])
    width_grid = select(grid_hw[:, 1])
    frames = select(frame_counts)
    count = jnp.sum(frame_counts * grid_hw[:, 0] * grid_hw[:, 1]).astype(f32)
    betas, cumul = roster()
    step_ids = jnp.arange(1000, dtype=jnp.int32)
    alpha_bar = jnp.sum(jnp.where(step_ids == tstep, cumul, 0.0))
    alpha_prev = jnp.sum(jnp.where(step_ids == tstep - 1, cumul, 0.0))
    beta_now = jnp.sum(jnp.where(step_ids == tstep, betas, 0.0))

    embed_low = embed_mats.astype(bf16)
    width_local = embed_low.shape[1]
    captions = lax.all_gather(caption[0], "dp", axis=0, tiled=True)
    lead = TFREQ + TXT
    cap_rows = local_rows(jnp.pad(captions, ((0, 0), (TFREQ, EMB_ALL - lead))), group)
    freq = waves(timesteps.astype(f32), TFREQ).astype(bf16)
    freq_rows = local_rows(jnp.pad(freq, ((0, 0), (0, EMB_ALL - TFREQ))), group)

    def from_rows(local):
        whole = lax.all_gather(lax.psum(local, "mp"), "dp", axis=0)
        return whole.swapaxes(0, 1).reshape(clips, EMB_ALL)

    t_pre = lax.psum(jnp.dot(freq_rows, embed_low, preferred_element_type=f32), "dp")
    t_pre = t_pre + own_slice(parts["t_bias_one"], part, width_local)
    t_hidden = jax.nn.silu(t_pre).astype(bf16)
    t_sum = from_rows(lax.dot_general(t_hidden, embed_low, CONTRACT_LAST, preferred_element_type=f32))
    t_emb_all = t_sum[:, lead : lead + D] + parts["t_bias_two"]
    t_emb_local = lax.dynamic_slice_in_dim(t_emb_all, part * width_local, width_local, 1)
    silu_local = jax.nn.silu(t_emb_local).astype(bf16)
    mod_sum = from_rows(
        lax.dot_general(silu_local, embed_low, CONTRACT_LAST, preferred_element_type=f32)
    )[:, lead + 2 * D :]
    t_mod_vec = jnp.sum(jnp.where(pick[:, None], mod_sum, 0.0), 0) + parts["t_bias_mod"]
    t_emb = jnp.sum(jnp.where(pick[:, None], t_emb_all, 0.0), 0)

    c_two_row = lead + D - group * EMB_LOCAL
    c_row_ids = c_two_row + jnp.arange(D, dtype=jnp.int32)
    c_held = (c_two_row >= 0) & (c_two_row + D <= EMB_LOCAL)
    c_two = lax.dynamic_slice_in_dim(embed_low, jnp.clip(c_two_row, 0, EMB_LOCAL - D), D, 0)
    c_two = lax.psum(jnp.where(c_held, c_two, jnp.zeros_like(c_two)), "dp")
    c_pre = lax.psum_scatter(
        jnp.dot(cap_rows, embed_low, preferred_element_type=f32), "dp", scatter_dimension=0, tiled=True
    ) + own_slice(parts["c_bias_one"], part, width_local)
    c_hidden = gelu_tanh(c_pre).astype(bf16)
    c_part = lax.dot_general(c_hidden, c_two, CONTRACT_LAST, preferred_element_type=f32)
    c_sum = lax.psum(c_part.astype(bf16), "mp").astype(f32)
    context = (c_sum + parts["c_bias_two"]).astype(bf16)

    area = height * width_grid
    patch_ids = jnp.arange(PM, dtype=jnp.int32)
    shifted = patch_ids - (PM - area)
    noisy = jnp.sqrt(alpha_bar) * latents[0] + jnp.sqrt(1.0 - alpha_bar) * noise[0]
    noisy_low = noisy.astype(bf16)
    position = jnp.concatenate(
        [
            waves((shifted // width_grid).astype(f32), D // 2),
            waves((shifted % width_grid).astype(f32), D // 2),
        ],
        -1,
    )
    x = jnp.dot(noisy_low, parts["patch_w"].astype(bf16), preferred_element_type=f32)
    x = x + parts["patch_b"] + position
    tables = parts["tables"] + t_mod_vec.reshape(1, 6, D)
    mods0, mods1 = tables[0], tables[1]
    keep_space = (patch_ids >= PM - area).reshape(1, 1, PM)
    keep_cross = (jnp.arange(CAP, dtype=jnp.int32) < cap_len).reshape(1, 1, CAP)
    keep_time = (jnp.arange(FR, dtype=jnp.int32) >= FR - frames).reshape(1, 1, 1, FR)
    flat_forms, time_forms = attention_forms("cross"), attention_forms("time")
    biases = parts["attn_bias"]

    x0 = x
    source0 = modulate(x0, mods0[0], mods0[1]).astype(bf16)
    branch0, saved0 = chip_forward_attention(
        source0, w_space, biases[0], keep_space, flat_forms, (PM,)
    )
    x1 = x0 + mods0[2] * branch0
    x1_low = x1.astype(bf16)
    cross_q, cross_k, cross_v = [], [], []
    for m in range(4):
        cross_q.append(jnp.dot(x1_low, w_cross[m][:, :SPAN], preferred_element_type=f32))
        both = jnp.dot(context, w_cross[m][:, SPAN : 3 * SPAN], preferred_element_type=f32)
        cross_k.append(both[:, :SPAN])
        cross_v.append(both[:, SPAN:])
    cross_q = (jnp.concatenate(cross_q, 1) + biases[2, 0]).astype(bf16).reshape(PM, HEADS, HD)
    cross_k = jnp.concatenate(cross_k, 1).astype(bf16).reshape(CAP, HEADS, HD)
    cross_v = (jnp.concatenate(cross_v, 1) + biases[2, 1]).astype(bf16).reshape(CAP, HEADS, HD)
    cross_mixed, cross_log = attend_forward(cross_q, cross_k, cross_v, keep_cross, flat_forms)
    cross_mixed = cross_mixed.astype(bf16).reshape(PM, D)
    x2 = x1 + out_product(cross_mixed, w_cross) + biases[2, 2]
    source2 = modulate(x2, mods0[3], mods0[4]).astype(bf16)
    branch2, saved2 = chip_ffn_forward(
        source2, w_ffn0[0], w_ffn0[1], parts["ffn_bias_one"][0], parts["ffn_bias_two"][0]
    )
    x3 = x2 + mods0[5] * branch2
    x3 = x3 + waves((part - (FR - frames)).astype(f32)[None], D)

    share = PM // FR

    def to_time(value):
        return lax.all_to_all(value.reshape(FR, share, -1), "mp", 0, 0, tiled=True).reshape(PM, -1)

    x4 = to_time(x3)
    noise_time = to_time(jnp.concatenate([latents[0], noise[0]], 1))
    latent_time, noise_time = noise_time[:, :CIN], noise_time[:, CIN:]
    source4 = modulate(x4, mods1[0], mods1[1]).astype(bf16)
    branch4, saved4 = chip_forward_attention(
        source4, w_time, biases[1], keep_time, time_forms, (FR, share)
    )
    x5 = x4 + mods1[2] * branch4
    source5 = modulate(x5, mods1[3], mods1[4]).astype(bf16)
    branch5, saved5 = chip_ffn_forward(
        source5, w_ffn1[0], w_ffn1[1], parts["ffn_bias_one"][1], parts["ffn_bias_two"][1]
    )
    x6 = x5 + mods1[5] * branch5

    final_mods = parts["final_table"] + t_emb
    final_source = modulate(x6, final_mods[0], final_mods[1]).astype(bf16)
    final_low = parts["final_w"].astype(bf16)
    output = (
        lax.dot_general(final_source, final_low, CONTRACT_LAST, preferred_element_type=f32)
        + parts["final_b"]
    )
    frozen = output[:, :CIN]
    noisy_time = jnp.sqrt(alpha_bar) * latent_time + jnp.sqrt(1.0 - alpha_bar) * noise_time
    row_ids = jnp.arange(PM, dtype=jnp.int32)
    valid = (row_ids // share >= FR - frames) & (part * share + row_ids % share >= PM - area)

    def shard_loss(values):
        losses = token_losses(
            values, frozen, latent_time, noise_time, (noisy_time, alpha_bar, alpha_prev, beta_now)
        )
        return jnp.sum(jnp.where(valid, losses, 0.0))

    loss_part, loss_pull = jax.vjp(shard_loss, output)
    d_output = loss_pull(1.0 / count)[0].astype(bf16)
    d_final_w = lax.dot_general(d_output, final_source, CONTRACT_ROWS, preferred_element_type=f32)
    d_final_b = jnp.sum(d_output.astype(f32), 0)
    d_final_source = jnp.dot(d_output, final_low, preferred_element_type=f32)
    grad_x, d_final_shift, d_final_scale = modulate_back(
        x6, final_mods[0], final_mods[1], d_final_source
    )

    d_gate5 = jnp.sum(grad_x * branch5, 0)
    d_branch = (mods1[5] * grad_x).astype(bf16)
    d_bias5 = jnp.sum(d_branch.astype(f32), 0)
    d_source, d_ffn1, d_ffn1_bias = chip_ffn_backward(
        d_branch, source5, w_ffn1[0], w_ffn1[1], saved5
    )
    d_input, d_shift5, d_scale5 = modulate_back(x5, mods1[3], mods1[4], d_source)
    grad_x = grad_x + d_input
    g_ffn1 = scatter_one(d_ffn1.reshape(2, 4, 8, BLOCK, D), 2)
    d_gate4 = jnp.sum(grad_x * branch4, 0)
    d_branch = (mods1[2] * grad_x).astype(bf16)
    d_source, d_time, d_time_bias = chip_backward_attention(
        d_branch, source4, w_time, keep_time, time_forms, saved4
    )
    d_input, d_shift4, d_scale4 = modulate_back(x4, mods1[0], mods1[1], d_source)
    grad_x = grad_x + d_input
    g_time = scatter_one(d_time.reshape(1, 4, 8, BLOCK, D), 1)
    d_mods1 = jnp.stack([d_shift4, d_scale4, d_gate4, d_shift5, d_scale5, d_gate5])
    grad_x = to_time(grad_x)

    d_gate2 = jnp.sum(grad_x * branch2, 0)
    d_branch = (mods0[5] * grad_x).astype(bf16)
    d_bias2 = jnp.sum(d_branch.astype(f32), 0)
    d_source, d_ffn0, d_ffn0_bias = chip_ffn_backward(
        d_branch, source2, w_ffn0[0], w_ffn0[1], saved2
    )
    d_input, d_shift2, d_scale2 = modulate_back(x2, mods0[3], mods0[4], d_source)
    grad_x = grad_x + d_input
    g_ffn0 = scatter_one(d_ffn0.reshape(2, 4, 8, BLOCK, D), 2)

    d_branch = grad_x.astype(bf16)
    d_mixed = jnp.concatenate(
        [
            jnp.dot(d_branch, w_cross[m][:, 3 * SPAN :], preferred_element_type=f32)
            for m in range(4)
        ],
        1,
    )
    d_mixed = d_mixed.astype(bf16).reshape(PM, HEADS, HD)
    d_query, d_key, d_value = attend_backward(
        cross_q, cross_k, cross_v, keep_cross, flat_forms, cross_log, d_mixed
    )
    d_query = d_query.astype(bf16).reshape(PM, D)
    d_both = jnp.concatenate([d_key.reshape(CAP, D), d_value.reshape(CAP, D)], 1)
    d_both = lax.psum(d_both, "mp").astype(bf16)
    first_part = (part == 0).astype(f32)
    d_cross_bias = jnp.stack(
        [
            jnp.sum(d_query.astype(f32), 0),
            jnp.sum(d_both[:, D:].astype(f32), 0) * first_part,
            jnp.sum(d_branch.astype(f32), 0),
        ]
    )
    own_both = jnp.where(part == 0, d_both, jnp.zeros_like(d_both))
    d_cross, d_context, back = [], 0.0, 0.0
    for m in range(4):
        at = slice(m * SPAN, (m + 1) * SPAN)
        d_pair = jnp.concatenate([d_both[:, :D][:, at], d_both[:, D:][:, at]], 1)
        own_pair = jnp.concatenate([own_both[:, :D][:, at], own_both[:, D:][:, at]], 1)
        back += lax.dot_general(
            d_query[:, at], w_cross[m][:, :SPAN], CONTRACT_LAST, preferred_element_type=f32
        )
        d_context += lax.dot_general(
            d_pair, w_cross[m][:, SPAN : 3 * SPAN], CONTRACT_LAST, preferred_element_type=f32
        )
        d_cross.append(
            jnp.concatenate(
                [
                    lax.dot_general(x1_low, d_query[:, at], CONTRACT_ROWS, preferred_element_type=f32),
                    lax.dot_general(context, own_pair, CONTRACT_ROWS, preferred_element_type=f32),
                    lax.dot_general(
                        d_branch, cross_mixed[:, at], CONTRACT_ROWS, preferred_element_type=f32
                    ),
                ],
                1,
            ).astype(bf16)
        )
    grad_x = grad_x + back
    g_cross = scatter_one(jnp.stack(d_cross).reshape(1, 4, 8, BLOCK, D), 1)

    d_context = d_context.astype(bf16)
    d_c_bias_two = jnp.sum(d_context.astype(f32), 0) * first_part
    d_c_hidden = jnp.dot(d_context, c_two, preferred_element_type=f32)
    unused, cap_pull = jax.vjp(gelu_tanh, c_pre)
    d_c_pre = cap_pull(d_c_hidden)[0].astype(bf16)
    d_c_bias_one = jnp.sum(d_c_pre.astype(f32), 0)
    d_c_pre_all = lax.all_gather(d_c_pre, "dp", axis=0, tiled=True)
    c_hidden_all = lax.all_gather(c_hidden, "dp", axis=0, tiled=True)
    d_context_all = lax.all_gather(d_context, "dp", axis=0, tiled=True)
    d_c_one = lax.dot_general(cap_rows, d_c_pre_all, CONTRACT_ROWS, preferred_element_type=f32)
    d_c_two = lax.dot_general(d_context_all, c_hidden_all, CONTRACT_ROWS, preferred_element_type=f32)

    d_gate0 = jnp.sum(grad_x * branch0, 0)
    d_branch = (mods0[2] * grad_x).astype(bf16)
    d_source, d_space, d_space_bias = chip_backward_attention(
        d_branch, source0, w_space, keep_space, flat_forms, saved0
    )
    d_input, d_shift0, d_scale0 = modulate_back(x0, mods0[0], mods0[1], d_source)
    grad_x = grad_x + d_input
    g_space = scatter_one(d_space.reshape(1, 4, 8, BLOCK, D), 1)
    d_mods0 = jnp.stack([d_shift0, d_scale0, d_gate0, d_shift2, d_scale2, d_gate2])

    d_patch = grad_x.astype(bf16)
    d_patch_b = jnp.sum(d_patch.astype(f32), 0)
    d_patch_w = lax.dot_general(noisy_low, d_patch, CONTRACT_ROWS, preferred_element_type=f32)

    d_mod_part = (d_mods0 + d_mods1).reshape(-1)
    d_temb_part = d_final_shift + d_final_scale
    d_mod_all = lax.all_gather(
        lax.psum(jnp.concatenate([d_mod_part, d_temb_part]), "mp"), "dp", axis=0
    )
    d_temb_sum = d_mod_all[:, 6 * D :]
    d_mod_low = d_mod_all[:, : 6 * D].astype(bf16)
    d_mod_rows = local_rows(jnp.pad(d_mod_low, ((0, 0), (lead + 2 * D, 0))), group)
    d_silu = lax.psum(jnp.dot(d_mod_rows, embed_low, preferred_element_type=f32), "dp")
    unused, silu_pull = jax.vjp(jax.nn.silu, t_emb_local)
    d_temb_local = silu_pull(d_silu)[0]
    d_temb = lax.all_gather(d_temb_local, "mp", axis=1, tiled=True) + d_temb_sum
    d_temb_rows = local_rows(jnp.pad(d_temb, ((0, 0), (lead, EMB_ALL - lead - D))), group)
    d_t_hidden = lax.psum(
        jnp.dot(d_temb_rows, embed_low.astype(f32), precision=lax.Precision.HIGHEST), "dp"
    )
    unused, pre_pull = jax.vjp(jax.nn.silu, t_pre)
    d_t_pre = pre_pull(d_t_hidden)[0]

    def outer(left, right):
        return lax.dot_general(
            left.astype(f32), right.astype(f32), CONTRACT_ROWS, precision=lax.Precision.HIGHEST
        )

    g_embed = (
        lax.dot_general(d_mod_rows, silu_local, CONTRACT_ROWS, preferred_element_type=f32)
        + outer(jnp.concatenate([d_temb_rows, freq_rows.astype(f32)]), jnp.concatenate([t_hidden.astype(f32), d_t_pre]))
        + d_c_one
    )
    here = lax.dynamic_slice_in_dim(g_embed, jnp.clip(c_two_row, 0, EMB_LOCAL - D), D, 0)
    g_embed = lax.dynamic_update_slice_in_dim(
        g_embed, jnp.where(c_held, d_c_two, here), jnp.clip(c_two_row, 0, EMB_LOCAL - D), 0
    )

    first_clip = pick.astype(f32) * first_part
    vector_grads = {
        "patch_w": d_patch_w,
        "patch_b": d_patch_b,
        "final_w": d_final_w,
        "final_b": d_final_b,
        "t_bias_one": placed(jnp.sum(d_t_pre * pick.astype(f32)[:, None], 0), part, D),
        "t_bias_two": d_temb_part
        + placed(jnp.sum(d_temb_local * pick.astype(f32)[:, None], 0), part, D),
        "t_bias_mod": d_mod_part,
        "c_bias_one": placed(d_c_bias_one, part, D),
        "c_bias_two": d_c_bias_two,
        "attn_bias": jnp.stack([d_space_bias, d_time_bias, d_cross_bias]),
        "ffn_bias_one": jnp.stack([d_ffn0_bias, d_ffn1_bias]),
        "ffn_bias_two": jnp.stack([d_bias2, d_bias5]),
        "tables": jnp.stack([d_mods0, d_mods1]),
        "final_table": jnp.stack([d_final_shift, d_final_scale]),
    }
    vector_grad = jnp.concatenate(
        [vector_grads[label].reshape(-1) for label, extent in vector_parts()]
    )
    g_vector = lax.psum(vector_grad, ("dp", "mp"))
    g_attn = jnp.stack([g_space[0], g_time[0], g_cross[0]])
    g_attn = g_attn.reshape(3, BLOCK, 4, 4, HD).swapaxes(2, 3).reshape(3, BLOCK, D)
    g_ffn = jnp.stack([g_ffn0, g_ffn1])
    matrix_squares = jnp.sum(g_attn * g_attn) + jnp.sum(g_ffn * g_ffn) + jnp.sum(g_embed * g_embed)
    totals = lax.psum(jnp.stack([matrix_squares, loss_part]), ("dp", "mp"))
    loss_total = totals[1]
    squares = totals[0] + jnp.sum(g_vector * g_vector)
    grad_norm = jnp.sqrt(squares)
    factor = CLIP_NORM / (grad_norm + 1e-06)
    new_attn = adam_update(
        attn_mats, attn_first, attn_second, attn_ema, g_attn * factor, LEARN_RATE
    )
    new_ffn = adam_update(ffn_mats, ffn_first, ffn_second, ffn_ema, g_ffn * factor, LEARN_RATE)
    new_embed = adam_update(
        embed_mats, embed_first, embed_second, embed_ema, g_embed * factor, LEARN_RATE
    )
    new_vector = adam_update(
        vectors, vector_first, vector_second, vector_ema, g_vector * factor, VECTOR_RATE
    )
    return (loss_total, count, grad_norm) + tuple(
        group_new[kind]
        for kind in range(4)
        for group_new in (new_attn, new_ffn, new_embed, new_vector)
    )


def solution(mesh):
    fits = dict(mesh.shape) == {"dp": 8, "mp": FR}
    program = per_device_chips if fits else per_device
    return jax.shard_map(
        program,
        mesh=mesh,
        in_specs=(
            P("dp", "mp", None),
            P("dp", "mp", None),
            P("dp", None, None),
            P(),
            P(),
            P(),
            P(),
            P(None, "dp", "mp"),
            P(None, None, "dp", "mp"),
            P("dp", "mp"),
            P(),
            P(None, "dp", "mp"),
            P(None, None, "dp", "mp"),
            P("dp", "mp"),
            P(),
            P(None, "dp", "mp"),
            P(None, None, "dp", "mp"),
            P("dp", "mp"),
            P(),
            P(None, "dp", "mp"),
            P(None, None, "dp", "mp"),
            P("dp", "mp"),
            P(),
        ),
        out_specs=(
            P(),
            P(),
            P(),
            P(None, "dp", "mp"),
            P(None, None, "dp", "mp"),
            P("dp", "mp"),
            P(),
            P(None, "dp", "mp"),
            P(None, None, "dp", "mp"),
            P("dp", "mp"),
            P(),
            P(None, "dp", "mp"),
            P(None, None, "dp", "mp"),
            P("dp", "mp"),
            P(),
            P(None, "dp", "mp"),
            P(None, None, "dp", "mp"),
            P("dp", "mp"),
            P(),
        ),
        check_vma=False,
    )
```

```python
import functools
import math

import jax
import jax.numpy as jnp
from jax import lax
from jax.experimental import pallas as pl
from jax.experimental.pallas import tpu as pltpu
from jax.sharding import PartitionSpec as P

D = 1152
HEADS = 16
HD = 72
FF = 4608
TFREQ = 256
TXT = 4096
CIN = 16
COUT = 32
CAP = 120
FR = 4
PM = 448
STEP = 5
DP, MP = "dp", "mp"
AT_SPACE = 0
AT_TIME = 1
AT_CROSS = 2
AT_ATTN = 3
AT_FFN = 4
AT_PARTS = 5
AT_PART = 6
AT_CONTEXT = 7
AT_KEEP = 8
AT_INPUT = 9
AT_GATHERED = 10
AT_QUERY = 11
AT_KEY_ROWS = 12
AT_VALUE_ROWS = 13
AT_LOGSUM = 14
AT_MIXED = 15
AT_BRANCH = 16
AT_PRE = 17
AT_HIDDEN = 18
PATCH_W = 0
PATCH_B = 1
FINAL_W = 2
FINAL_B = 3
T_BIAS_ONE = 4
T_BIAS_TWO = 5
T_BIAS_MOD = 6
C_BIAS_ONE = 7
C_BIAS_TWO = 8
ATTN_BIAS = 9
FFN_BIAS_ONE = 10
FFN_BIAS_TWO = 11
TABLES = 12
FINAL_TABLE = 13


EPS_NORM = 1e-06
LEARN_RATE = 0.03
VECTOR_RATE = 0.15
BETA_FIRST = 0.5
BETA_SECOND = 0.5
ADAM_EPSILON = 1e-08
WEIGHT_DECAY = 0.01
EMA_DECAY = 0.9
CLIP_NORM = 0.02
NEG_LARGE = -1e30
CONTRACT_ROWS = (((0,), (0,)), ((), ()))
CONTRACT_LAST = (((1,), (1,)), ((), ()))


def vector_parts():
    return [
        (PATCH_W, (CIN, D)),
        (PATCH_B, (D,)),
        (FINAL_W, (COUT, D)),
        (FINAL_B, (COUT,)),
        (T_BIAS_ONE, (D,)),
        (T_BIAS_TWO, (D,)),
        (T_BIAS_MOD, (6 * D,)),
        (C_BIAS_ONE, (D,)),
        (C_BIAS_TWO, (D,)),
        (ATTN_BIAS, (3, 3, D)),
        (FFN_BIAS_ONE, (2, FF)),
        (FFN_BIAS_TWO, (2, D)),
        (TABLES, (2, 6, D)),
        (FINAL_TABLE, (2, D)),
    ]


def unpack(flat):
    result = {}
    offset = 0
    for label, extent in vector_parts():
        length = math.prod(extent)
        result[label] = flat[offset : offset + length].reshape(extent)
        offset += length
    return result


def waves(position, width):
    half = width // 2
    freqs = jnp.exp(-math.log(10000.0) * jnp.arange(half, dtype=jnp.float32) / half)
    angles = position[..., None] * freqs
    return jnp.concatenate([jnp.sin(angles), jnp.cos(angles)], -1)


def roster():
    betas = 0.0001 + (0.02 - 0.0001) * jnp.arange(1000, dtype=jnp.float32) / 999.0
    return (betas, jnp.exp(jnp.cumsum(jnp.log1p(-betas))))


def modulate(x, shift_vec, scale_vec):
    centered = x - jnp.mean(x, -1, keepdims=True)
    normed = centered * lax.rsqrt(jnp.mean(centered * centered, -1, keepdims=True) + EPS_NORM)
    return normed * (1.0 + scale_vec) + shift_vec


def gelu_tanh(values):
    return jax.nn.gelu(values, approximate=True)


def token_losses(output, frozen, latent, noise_part, extra):
    noisy, alpha_bar, alpha_prev, beta_now = extra
    eps = output[:, :CIN]
    var_raw = output[:, CIN:]
    mse = jnp.mean((eps - noise_part) ** 2, -1)
    post_var = beta_now * (1.0 - alpha_prev) / (1.0 - alpha_bar)
    log_post = jnp.log(post_var)
    frac = (var_raw + 1.0) / 2.0
    log_var = frac * jnp.log(beta_now) + (1.0 - frac) * log_post
    coef_start = beta_now * jnp.sqrt(alpha_prev) / (1.0 - alpha_bar)
    coef_now = (1.0 - alpha_prev) * jnp.sqrt(1.0 - beta_now) / (1.0 - alpha_bar)
    true_mean = coef_start * latent + coef_now * noisy
    guess = (noisy - jnp.sqrt(1.0 - alpha_bar) * frozen) / jnp.sqrt(alpha_bar)
    model_mean = coef_start * guess + coef_now * noisy
    kl_term = 0.5 * (
        -1.0
        + log_var
        - log_post
        + jnp.exp(log_post - log_var)
        + (true_mean - model_mean) ** 2 * jnp.exp(-log_var)
    )
    return mse + jnp.mean(kl_term, -1) / math.log(2.0)


def attention_forms(kind):
    if kind == AT_SPACE:
        return ("fqhe,fkhe->fhqk", "fhqk,fkhe->fqhe", "fhqk,fqhe->fkhe")
    if kind == AT_TIME:
        return ("qphe,kphe->phqk", "phqk,kphe->qphe", "phqk,qphe->kphe")
    return ("qhe,khe->hqk", "hqk,khe->qhe", "hqk,qhe->khe")


def own_slice(vector, part, width):
    return lax.dynamic_slice_in_dim(vector, part * width, width, 0)


def placed(piece, part, full):
    return lax.dynamic_update_slice_in_dim(
        jnp.zeros((full,), jnp.float32), piece, part * piece.shape[0], 0
    )


def project_in(shard_rows, weight):
    piece = lax.all_gather(shard_rows, MP, axis=0, tiled=True)
    product = jnp.dot(piece, weight, preferred_element_type=jnp.float32)
    return (product, piece)


def project_out(full_rows, weight_t):
    return lax.psum_scatter(
        lax.dot_general(
            full_rows, weight_t, CONTRACT_LAST, preferred_element_type=jnp.float32
        ).astype(jnp.bfloat16),
        MP,
        scatter_dimension=0,
        tiled=True,
    ).astype(jnp.float32)


def back_out(grad_rows, full_rows, weight_t):
    piece = lax.all_gather(grad_rows, MP, axis=0, tiled=True)
    product = jnp.dot(piece, weight_t, preferred_element_type=jnp.float32)
    d_weight = lax.dot_general(piece, full_rows, CONTRACT_ROWS, preferred_element_type=jnp.float32)
    return (product, d_weight)


def back_in(d_full, weight):
    return lax.psum_scatter(
        lax.dot_general(d_full, weight, CONTRACT_LAST, preferred_element_type=jnp.float32).astype(
            jnp.bfloat16
        ),
        MP,
        scatter_dimension=0,
        tiled=True,
    ).astype(jnp.float32)


def attend_forward(query, key_rows, value_rows, keep, forms):
    scores = jnp.einsum(forms[0], query, key_rows, preferred_element_type=jnp.float32) * HD ** (
        -0.5
    )
    scores = jnp.where(keep, scores, NEG_LARGE)
    peak = jnp.max(scores, -1, keepdims=True)
    expd = jnp.exp(scores - peak)
    total = jnp.sum(expd, -1, keepdims=True)
    probs = (expd / total).astype(jnp.bfloat16)
    mixed = jnp.einsum(forms[1], probs, value_rows, preferred_element_type=jnp.float32)
    return (mixed, peak + jnp.log(total))


def attend_backward(query, key_rows, value_rows, keep, forms, logsum, d_mixed):
    scores = jnp.einsum(forms[0], query, key_rows, preferred_element_type=jnp.float32) * HD ** (
        -0.5
    )
    scores = jnp.where(keep, scores, NEG_LARGE)
    probs_full = jnp.exp(scores - logsum)
    probs = probs_full.astype(jnp.bfloat16)
    d_value = jnp.einsum(forms[2], probs, d_mixed, preferred_element_type=jnp.float32)
    d_probs = jnp.einsum(forms[0], d_mixed, value_rows, preferred_element_type=jnp.float32)
    offset = jnp.sum(d_probs * probs_full, -1, keepdims=True)
    d_scores = (probs_full * (d_probs - offset) * HD ** (-0.5)).astype(jnp.bfloat16)
    d_query = jnp.einsum(forms[1], d_scores, key_rows, preferred_element_type=jnp.float32)
    d_key = jnp.einsum(forms[2], d_scores, query, preferred_element_type=jnp.float32)
    return (d_query, d_key, d_value)


def attention_forward(x, index, mods, kind, setup):
    weight = setup[AT_ATTN][index]
    heads = weight.shape[1]
    width_local = heads * HD
    biases = setup[AT_PARTS][ATTN_BIAS][index]
    part = setup[AT_PART]
    forms = attention_forms(kind)
    query_bias = own_slice(biases[0], part, width_local).reshape(heads, HD)
    value_bias = own_slice(biases[1], part, width_local).reshape(heads, HD)
    if kind == AT_CROSS:
        projected, gathered = project_in(
            x.astype(jnp.bfloat16), weight[:, :, 0, :].reshape(D, width_local)
        )
        query = projected.reshape(-1, heads, HD) + query_bias
        context = setup[AT_CONTEXT]
        key_rows = jnp.einsum(
            "cd,dhe->che", context, weight[:, :, 1, :], preferred_element_type=jnp.float32
        )
        value_rows = (
            jnp.einsum(
                "cd,dhe->che", context, weight[:, :, 2, :], preferred_element_type=jnp.float32
            )
            + value_bias
        )
    else:
        source = modulate(x, mods[0], mods[1])
        projected, gathered = project_in(
            source.astype(jnp.bfloat16), weight[:, :, :3, :].reshape(D, 3 * width_local)
        )
        projected = projected.reshape(FR, PM, heads, 3, HD)
        query = projected[:, :, :, 0] + query_bias
        key_rows = projected[:, :, :, 1]
        value_rows = projected[:, :, :, 2] + value_bias
    query = query.astype(jnp.bfloat16)
    key_rows = key_rows.astype(jnp.bfloat16)
    value_rows = value_rows.astype(jnp.bfloat16)
    mixed, logsum = attend_forward(query, key_rows, value_rows, setup[AT_KEEP][kind], forms)
    mixed = mixed.reshape(-1, width_local).astype(jnp.bfloat16)
    branch = project_out(mixed, weight[:, :, 3, :].reshape(D, width_local)) + biases[2]
    saved = {
        AT_INPUT: x,
        AT_GATHERED: gathered,
        AT_QUERY: query,
        AT_KEY_ROWS: key_rows,
        AT_VALUE_ROWS: value_rows,
        AT_LOGSUM: logsum,
        AT_MIXED: mixed,
        AT_BRANCH: branch,
    }
    if kind == AT_CROSS:
        return (x + branch, saved)
    return (x + mods[2] * branch, saved)


def attention_backward(grad_x, index, mods, kind, saved, setup):
    weight = setup[AT_ATTN][index]
    heads = weight.shape[1]
    width_local = heads * HD
    part = setup[AT_PART]
    forms = attention_forms(kind)
    query = saved[AT_QUERY]
    if kind == AT_CROSS:
        gate_vec = 1.0
        d_gate = None
    else:
        gate_vec = mods[2]
        d_gate = jnp.sum(grad_x * saved[AT_BRANCH], 0)
    d_branch = (gate_vec * grad_x).astype(jnp.bfloat16)
    d_out_bias = jnp.sum(d_branch.astype(jnp.float32), 0)
    d_mixed, d_out_weight = back_out(
        d_branch, saved[AT_MIXED], weight[:, :, 3, :].reshape(D, width_local)
    )
    d_mixed = d_mixed.astype(jnp.bfloat16).reshape(query.shape)
    d_query, d_key, d_value = attend_backward(
        query,
        saved[AT_KEY_ROWS],
        saved[AT_VALUE_ROWS],
        setup[AT_KEEP][kind],
        forms,
        saved[AT_LOGSUM],
        d_mixed,
    )
    d_query = d_query.reshape(-1, heads, HD).astype(jnp.bfloat16)
    d_key = d_key.reshape(-1, heads, HD).astype(jnp.bfloat16)
    d_value = d_value.reshape(-1, heads, HD).astype(jnp.bfloat16)
    d_query_bias = jnp.sum(d_query.astype(jnp.float32), 0).reshape(-1)
    d_value_bias = jnp.sum(d_value.astype(jnp.float32), 0).reshape(-1)
    if kind == AT_CROSS:
        context = setup[AT_CONTEXT]
        d_query_weight = lax.dot_general(
            saved[AT_GATHERED],
            d_query.reshape(-1, width_local),
            CONTRACT_ROWS,
            preferred_element_type=jnp.float32,
        ).reshape(D, heads, 1, HD)
        d_key_weight = jnp.einsum("cd,che->dhe", context, d_key, preferred_element_type=jnp.float32)
        d_value_weight = jnp.einsum(
            "cd,che->dhe", context, d_value, preferred_element_type=jnp.float32
        )
        d_in = jnp.concatenate(
            [d_query_weight, d_key_weight[:, :, None], d_value_weight[:, :, None]], 2
        )
        d_context = jnp.einsum(
            "che,dhe->cd", d_key, weight[:, :, 1, :], preferred_element_type=jnp.float32
        ) + jnp.einsum(
            "che,dhe->cd", d_value, weight[:, :, 2, :], preferred_element_type=jnp.float32
        )
        grad_x = grad_x + back_in(
            d_query.reshape(-1, width_local), weight[:, :, 0, :].reshape(D, width_local)
        )
        mod_grads = None
    else:
        d_proj = jnp.stack([d_query, d_key, d_value], 2).reshape(-1, 3 * width_local)
        d_in = lax.dot_general(
            saved[AT_GATHERED], d_proj, CONTRACT_ROWS, preferred_element_type=jnp.float32
        ).reshape(D, heads, 3, HD)
        d_source = back_in(d_proj, weight[:, :, :3, :].reshape(D, 3 * width_local))
        unused, norm_pull = jax.vjp(modulate, saved[AT_INPUT], mods[0], mods[1])
        d_input, d_shift, d_scale = norm_pull(d_source)
        grad_x = grad_x + d_input
        mod_grads = (d_shift, d_scale, d_gate)
        d_context = None
    d_weight = jnp.concatenate([d_in, d_out_weight.reshape(D, heads, 1, HD)], 2)
    d_bias = jnp.stack([placed(d_query_bias, part, D), placed(d_value_bias, part, D), d_out_bias])
    return (grad_x, d_weight, d_bias, mod_grads, d_context)


def ffn_forward(x, index, mods, setup):
    weight_in = setup[AT_FFN][index, 0]
    weight_out = setup[AT_FFN][index, 1]
    source = modulate(x, mods[3], mods[4])
    pre, gathered = project_in(source.astype(jnp.bfloat16), weight_in)
    pre = pre + own_slice(setup[AT_PARTS][FFN_BIAS_ONE][index], setup[AT_PART], weight_in.shape[1])
    hidden = gelu_tanh(pre).astype(jnp.bfloat16)
    branch = project_out(hidden, weight_out) + setup[AT_PARTS][FFN_BIAS_TWO][index]
    saved = {AT_INPUT: x, AT_GATHERED: gathered, AT_PRE: pre, AT_HIDDEN: hidden, AT_BRANCH: branch}
    return (x + mods[5] * branch, saved)


def ffn_backward(grad_x, index, mods, saved, setup):
    weight_in = setup[AT_FFN][index, 0]
    weight_out = setup[AT_FFN][index, 1]
    d_gate = jnp.sum(grad_x * saved[AT_BRANCH], 0)
    d_branch = (mods[5] * grad_x).astype(jnp.bfloat16)
    d_bias_two = jnp.sum(d_branch.astype(jnp.float32), 0)
    d_hidden, d_weight_out = back_out(d_branch, saved[AT_HIDDEN], weight_out)
    unused, gelu_pull = jax.vjp(gelu_tanh, saved[AT_PRE])
    d_pre = gelu_pull(d_hidden)[0].astype(jnp.bfloat16)
    d_bias_one = jnp.sum(d_pre.astype(jnp.float32), 0)
    d_weight_in = lax.dot_general(
        saved[AT_GATHERED], d_pre, CONTRACT_ROWS, preferred_element_type=jnp.float32
    )
    d_source = back_in(d_pre, weight_in)
    unused, norm_pull = jax.vjp(modulate, saved[AT_INPUT], mods[3], mods[4])
    d_input, d_shift, d_scale = norm_pull(d_source)
    biases = (placed(d_bias_one, setup[AT_PART], FF), d_bias_two)
    return (
        grad_x + d_input,
        jnp.stack([d_weight_in, d_weight_out]),
        biases,
        (d_shift, d_scale, d_gate),
    )


def block_forward(x, kind, mods, setup):
    index = 0 if kind == AT_SPACE else 1
    x, first = attention_forward(x, index, mods, kind, setup)
    second = None
    if kind == AT_SPACE:
        x, second = attention_forward(x, 2, mods, AT_CROSS, setup)
    x, third = ffn_forward(x, index, mods, setup)
    return (x, (first, second, third))


def block_backward(grad_x, kind, mods, saved, setup):
    index = 0 if kind == AT_SPACE else 1
    first, second, third = saved
    grad_x, d_ffn, d_ffn_bias, ffn_mods = ffn_backward(grad_x, index, mods, third, setup)
    cross_part = None
    if kind == AT_SPACE:
        grad_x, d_cross, d_cross_bias, unused, d_context = attention_backward(
            grad_x, 2, mods, AT_CROSS, second, setup
        )
        cross_part = (d_cross, d_cross_bias, d_context)
    grad_x, d_attn, d_attn_bias, attn_mods, unused = attention_backward(
        grad_x, index, mods, kind, first, setup
    )
    d_mods = jnp.stack(list(attn_mods) + list(ffn_mods))
    return (grad_x, (d_attn, d_attn_bias, d_ffn, d_ffn_bias, d_mods), cross_part)


def adam_update(weight, first, second, ema, grad, rate):
    first_new = BETA_FIRST * first + (1.0 - BETA_FIRST) * grad
    second_new = BETA_SECOND * second + (1.0 - BETA_SECOND) * grad * grad
    corr_one = 1.0 - BETA_FIRST**STEP
    corr_two = 1.0 - BETA_SECOND**STEP
    weight_new = weight - rate * (
        first_new / corr_one / (jnp.sqrt(second_new / corr_two) + ADAM_EPSILON)
        + WEIGHT_DECAY * weight
    )
    return (first_new, second_new, weight_new, EMA_DECAY * ema + (1.0 - EMA_DECAY) * weight_new)


def per_device(
    latents,
    noise,
    caption,
    caption_lens,
    timesteps,
    grid_hw,
    frame_counts,
    attn_mats,
    ffn_mats,
    embed_mats,
    vectors,
    attn_first,
    ffn_first,
    embed_first,
    vector_first,
    attn_second,
    ffn_second,
    embed_second,
    vector_second,
    attn_ema,
    ffn_ema,
    embed_ema,
    vector_ema,
):
    group = lax.axis_index(DP)
    part = lax.axis_index(MP)
    mp_size = lax.axis_size(MP)
    rows = latents.shape[1]
    heads = HEADS // mp_size
    width_local = D // mp_size
    attn_all, ffn_all, embed_all = (
        lax.all_gather(attn_mats.astype(jnp.bfloat16), DP, axis=1, tiled=True),
        lax.all_gather(ffn_mats.astype(jnp.bfloat16), DP, axis=2, tiled=True),
        lax.all_gather(embed_mats.astype(jnp.bfloat16), DP, axis=0, tiled=True),
    )
    parts = unpack(vectors)
    pick = jnp.arange(timesteps.shape[0], dtype=jnp.int32) == group

    def select(values):
        return jnp.sum(jnp.where(pick, values, 0))

    tstep = select(timesteps)
    cap_len = select(caption_lens)
    height = select(grid_hw[:, 0])
    width_grid = select(grid_hw[:, 1])
    frames = select(frame_counts)
    count = jnp.sum(frame_counts * grid_hw[:, 0] * grid_hw[:, 1]).astype(jnp.float32)
    betas, cumul = roster()
    step_ids = jnp.arange(1000, dtype=jnp.int32)
    alpha_bar = jnp.sum(jnp.where(step_ids == tstep, cumul, 0.0))
    alpha_prev = jnp.sum(jnp.where(step_ids == tstep - 1, cumul, 0.0))
    beta_now = jnp.sum(jnp.where(step_ids == tstep, betas, 0.0))
    t_one = embed_all[:TFREQ]
    c_one = embed_all[TFREQ : TFREQ + TXT]
    t_two = embed_all[TFREQ + TXT : TFREQ + TXT + D]
    c_two = embed_all[TFREQ + TXT + D : TFREQ + TXT + 2 * D]
    t_mod = embed_all[TFREQ + TXT + 2 * D :]
    freq = waves(tstep.astype(jnp.float32), TFREQ).astype(jnp.bfloat16)
    t_pre = jnp.dot(freq, t_one, preferred_element_type=jnp.float32) + own_slice(
        parts[T_BIAS_ONE], part, width_local
    )
    t_hidden = jax.nn.silu(t_pre).astype(jnp.bfloat16)
    t_part = jnp.dot(t_two, t_hidden, preferred_element_type=jnp.float32)
    caption_rows = caption[0]
    c_pre = jnp.dot(caption_rows, c_one, preferred_element_type=jnp.float32) + own_slice(
        parts[C_BIAS_ONE], part, width_local
    )
    c_hidden = gelu_tanh(c_pre).astype(jnp.bfloat16)
    c_part = lax.dot_general(c_hidden, c_two, CONTRACT_LAST, preferred_element_type=jnp.float32)
    t_sum, c_sum = (
        lax.psum(t_part.astype(jnp.bfloat16), MP).astype(jnp.float32),
        lax.psum(c_part.astype(jnp.bfloat16), MP).astype(jnp.float32),
    )
    t_emb = t_sum + parts[T_BIAS_TWO]
    context = (c_sum + parts[C_BIAS_TWO]).astype(jnp.bfloat16)
    t_emb_local = own_slice(t_emb, part, width_local)
    silu_local = jax.nn.silu(t_emb_local).astype(jnp.bfloat16)
    t_mod_vec = (
        lax.psum(jnp.dot(t_mod, silu_local, preferred_element_type=jnp.float32), MP)
        + parts[T_BIAS_MOD]
    )
    token_ids = part * rows + jnp.arange(rows, dtype=jnp.int32)
    frame_slot = token_ids // PM
    patch_slot = token_ids % PM
    area = height * width_grid
    shifted = patch_slot - (PM - area)
    valid = (frame_slot >= FR - frames) & (patch_slot >= PM - area)
    setup = {
        AT_ATTN: attn_all.reshape(3, D, heads, 4, HD),
        AT_FFN: ffn_all,
        AT_PARTS: parts,
        AT_PART: part,
        AT_CONTEXT: context,
        AT_KEEP: {
            AT_SPACE: (jnp.arange(PM, dtype=jnp.int32) >= PM - area).reshape(1, 1, 1, PM),
            AT_TIME: (jnp.arange(FR, dtype=jnp.int32) >= FR - frames).reshape(1, 1, 1, FR),
            AT_CROSS: (jnp.arange(CAP, dtype=jnp.int32) < cap_len).reshape(1, 1, CAP),
        },
    }
    noisy = jnp.sqrt(alpha_bar) * latents[0] + jnp.sqrt(1.0 - alpha_bar) * noise[0]
    noisy_low = noisy.astype(jnp.bfloat16)
    position = jnp.concatenate(
        [
            waves((shifted // width_grid).astype(jnp.float32), D // 2),
            waves((shifted % width_grid).astype(jnp.float32), D // 2),
        ],
        -1,
    )
    x = jnp.dot(
        noisy_low, parts[PATCH_W].astype(jnp.bfloat16), preferred_element_type=jnp.float32
    )
    x = x + parts[PATCH_B] + position
    tables = parts[TABLES] + t_mod_vec.reshape(1, 6, D)
    x, saved_space = block_forward(x, AT_SPACE, tables[0], setup)
    x = x + waves((frame_slot - (FR - frames)).astype(jnp.float32), D)
    x, saved_time = block_forward(x, AT_TIME, tables[1], setup)
    final_mods = parts[FINAL_TABLE] + t_emb
    final_source = modulate(x, final_mods[0], final_mods[1]).astype(jnp.bfloat16)
    final_low = parts[FINAL_W].astype(jnp.bfloat16)
    output = (
        lax.dot_general(final_source, final_low, CONTRACT_LAST, preferred_element_type=jnp.float32)
        + parts[FINAL_B]
    )
    frozen = output[:, :CIN]

    def shard_loss(values):
        losses = token_losses(
            values, frozen, latents[0], noise[0], (noisy, alpha_bar, alpha_prev, beta_now)
        )
        return jnp.sum(jnp.where(valid, losses, 0.0))

    loss_part, loss_pull = jax.vjp(shard_loss, output)
    loss_total = lax.psum(loss_part, (DP, MP))
    d_output = loss_pull(1.0 / count)[0].astype(jnp.bfloat16)
    d_final_w = lax.dot_general(
        d_output, final_source, CONTRACT_ROWS, preferred_element_type=jnp.float32
    )
    d_final_b = jnp.sum(d_output.astype(jnp.float32), 0)
    d_final_source = jnp.dot(d_output, final_low, preferred_element_type=jnp.float32)
    unused, final_pull = jax.vjp(modulate, x, final_mods[0], final_mods[1])
    grad_x, d_final_shift, d_final_scale = final_pull(d_final_source)
    grad_x, time_grads, unused = block_backward(grad_x, AT_TIME, tables[1], saved_time, setup)
    grad_x, space_grads, cross_grads = block_backward(
        grad_x, AT_SPACE, tables[0], saved_space, setup
    )
    d_patch = grad_x.astype(jnp.bfloat16)
    d_patch_b = jnp.sum(d_patch.astype(jnp.float32), 0)
    d_patch_w = lax.dot_general(
        noisy_low, d_patch, CONTRACT_ROWS, preferred_element_type=jnp.float32
    )
    d_mod_part = space_grads[4].reshape(-1) + time_grads[4].reshape(-1)
    d_temb_part = d_final_shift + d_final_scale
    d_mod_vec, d_temb_sum, d_context = (
        lax.psum(d_mod_part.astype(jnp.bfloat16), MP).astype(jnp.float32),
        lax.psum(d_temb_part.astype(jnp.bfloat16), MP).astype(jnp.float32),
        lax.psum(cross_grads[2].astype(jnp.bfloat16), MP).astype(jnp.float32),
    )
    d_t_mod = jnp.outer(d_mod_vec, silu_local.astype(jnp.float32))
    d_silu_local = jnp.dot(d_mod_vec, t_mod, preferred_element_type=jnp.float32)
    unused, silu_pull = jax.vjp(jax.nn.silu, t_emb_local)
    d_temb_local = silu_pull(d_silu_local)[0]
    d_temb = d_temb_sum + lax.all_gather(d_temb_local, MP, axis=0, tiled=True)
    d_t_two = jnp.outer(d_temb, t_hidden.astype(jnp.float32))
    d_t_hidden = jnp.dot(d_temb, t_two, preferred_element_type=jnp.float32)
    unused, pre_pull = jax.vjp(jax.nn.silu, t_pre)
    d_t_pre = pre_pull(d_t_hidden)[0]
    d_t_one = jnp.outer(freq.astype(jnp.float32), d_t_pre)
    d_context = d_context.astype(jnp.bfloat16)
    d_c_bias_two = jnp.sum(d_context.astype(jnp.float32), 0) * (part == 0).astype(jnp.float32)
    d_c_two = lax.dot_general(
        d_context, c_hidden, CONTRACT_ROWS, preferred_element_type=jnp.float32
    )
    d_c_hidden = jnp.dot(d_context, c_two, preferred_element_type=jnp.float32)
    unused, cap_pull = jax.vjp(gelu_tanh, c_pre)
    d_c_pre = cap_pull(d_c_hidden)[0].astype(jnp.bfloat16)
    d_c_one = lax.dot_general(
        caption_rows, d_c_pre, CONTRACT_ROWS, preferred_element_type=jnp.float32
    )
    d_c_bias_one = jnp.sum(d_c_pre.astype(jnp.float32), 0)
    d_attn = jnp.stack([space_grads[0], time_grads[0], cross_grads[0]]).reshape(
        3, D, heads * 4 * HD
    )
    d_ffn = jnp.stack([space_grads[2], time_grads[2]])
    d_embed = jnp.concatenate([d_t_one, d_c_one, d_t_two, d_c_two, d_t_mod], 0)
    vector_grads = {
        PATCH_W: d_patch_w,
        PATCH_B: d_patch_b,
        FINAL_W: d_final_w,
        FINAL_B: d_final_b,
        T_BIAS_ONE: placed(d_t_pre, part, D),
        T_BIAS_TWO: d_temb_part + placed(d_temb_local, part, D),
        T_BIAS_MOD: d_mod_part,
        C_BIAS_ONE: placed(d_c_bias_one, part, D),
        C_BIAS_TWO: d_c_bias_two,
        ATTN_BIAS: jnp.stack([space_grads[1], time_grads[1], cross_grads[1]]),
        FFN_BIAS_ONE: jnp.stack([space_grads[3][0], time_grads[3][0]]),
        FFN_BIAS_TWO: jnp.stack([space_grads[3][1], time_grads[3][1]]),
        TABLES: jnp.stack([space_grads[4], time_grads[4]]),
        FINAL_TABLE: jnp.stack([d_final_shift, d_final_scale]),
    }
    vector_grad = jnp.concatenate(
        [vector_grads[label].reshape(-1) for label, extent in vector_parts()]
    )
    g_attn, g_ffn, g_embed = (
        lax.psum_scatter(d_attn.astype(jnp.bfloat16), DP, scatter_dimension=1, tiled=True).astype(
            jnp.float32
        ),
        lax.psum_scatter(d_ffn.astype(jnp.bfloat16), DP, scatter_dimension=2, tiled=True).astype(
            jnp.float32
        ),
        lax.psum_scatter(
            d_embed.astype(jnp.bfloat16), DP, scatter_dimension=0, tiled=True
        ).astype(jnp.float32),
    )
    g_vector = lax.psum(vector_grad, (DP, MP))
    matrix_squares = jnp.sum(g_attn * g_attn) + jnp.sum(g_ffn * g_ffn) + jnp.sum(g_embed * g_embed)
    squares = lax.psum(matrix_squares, (DP, MP)) + jnp.sum(g_vector * g_vector)
    grad_norm = jnp.sqrt(squares)
    factor = CLIP_NORM / (grad_norm + 1e-06)
    new_attn = adam_update(
        attn_mats, attn_first, attn_second, attn_ema, g_attn * factor, LEARN_RATE
    )
    new_ffn = adam_update(ffn_mats, ffn_first, ffn_second, ffn_ema, g_ffn * factor, LEARN_RATE)
    new_embed = adam_update(
        embed_mats, embed_first, embed_second, embed_ema, g_embed * factor, LEARN_RATE
    )
    new_vector = adam_update(
        vectors, vector_first, vector_second, vector_ema, g_vector * factor, VECTOR_RATE
    )
    return (
        loss_total,
        count,
        grad_norm,
        new_attn[0],
        new_ffn[0],
        new_embed[0],
        new_vector[0],
        new_attn[1],
        new_ffn[1],
        new_embed[1],
        new_vector[1],
        new_attn[2],
        new_ffn[2],
        new_embed[2],
        new_vector[2],
        new_attn[3],
        new_ffn[3],
        new_embed[3],
        new_vector[3],
    )


SPAN = 4 * HD
EMB_ALL = TFREQ + TXT + 8 * D
EMB_LOCAL = EMB_ALL // 8
MESH = pl.DeviceIdType.MESH
BLOCK = 144
BIG = 58 * 2**20
PIECES = {1: 2, 2: 1}


class Chips:
    def __init__(self):
        dp = lax.axis_index(DP)
        mp = lax.axis_index(MP)
        self.z, self.x = dp // 2, dp % 2
        self.y, self.c = mp // 2, mp % 2

    def z_at(self, j):
        z = self.z
        return (z, z + 1 - 2 * (z % 2), z + 2 - 4 * (z // 2), 3 - z)[j]

    def dp_at(self, jz, jx):
        return self.z_at(jz) * 2 + (1 - self.x if jx else self.x)

    def mp_at(self, jy, jc):
        return (1 - self.y if jy else self.y) * 2 + (1 - self.c if jc else self.c)

    def peer_x(self):
        return {DP: self.dp_at(0, 1)}

    def peer_y(self):
        return {MP: self.mp_at(1, 0)}

    def peer_core(self):
        return {MP: self.mp_at(0, 1)}

    def peer_z(self, j):
        return {DP: self.dp_at(j, 0)}

    def greet(self):
        barrier = pltpu.get_barrier_semaphore()
        peers = [self.peer_x(), self.peer_y(), self.peer_core()]
        peers += [self.peer_z(j) for j in (1, 2, 3)]
        for peer in peers:
            pl.semaphore_signal(barrier, inc=1, device_id=peer, device_id_type=MESH)
        pl.semaphore_wait(barrier, len(peers))


class Work:
    def __init__(self, chips, send, recv):
        self.chips, self.send, self.recv = chips, send, recv
        self.started = []

    def start(self, src, dst, slot, peer):
        def copy():
            return pltpu.make_async_remote_copy(
                src_ref=src(),
                dst_ref=dst(),
                send_sem=self.send.at[slot],
                recv_sem=self.recv.at[slot],
                device_id=peer(),
                device_id_type=MESH,
            )

        copy().start()
        self.started.append(copy)

    def arrived(self, dst, slot):
        pltpu.make_async_remote_copy(
            src_ref=dst,
            dst_ref=dst,
            send_sem=self.send.at[slot],
            recv_sem=self.recv.at[slot],
            device_id=self.chips.peer_core(),
            device_id_type=MESH,
        ).wait_recv()

    def finish(self):
        for copy in self.started:
            copy().wait_send()


class Gather(Work):
    def __init__(self, chips, shard, full, send, recv, local):
        super().__init__(chips, send, recv)
        self.shard, self.full, self.local = shard, full, local

    def block(self, jy, jz, jx, jc=0):
        chips = self.chips
        return self.full.at[:, chips.mp_at(jy, jc), chips.dp_at(jz, jx)]

    def arrive(self, jy, jz, jx, jc=0):
        self.arrived(self.block(jy, jz, jx, jc), jc * 16 + jy * 8 + jz * 2 + jx)

    def pass_on(self, place, slot, peer):
        self.start(lambda: self.block(*place), lambda: self.block(*place), slot, peer)

    def core(self, jy, jz, jx):
        self.pass_on((jy, jz, jx), 16 + jy * 8 + jz * 2 + jx, self.chips.peer_core)

    def own(self):
        return pltpu.make_async_copy(self.shard, self.block(0, 0, 0), self.local)

    def begin(self):
        chips = self.chips
        shard, block = (lambda: self.shard), (lambda: self.block(0, 0, 0))
        self.start(shard, block, 1, chips.peer_x)
        self.start(shard, block, 8, chips.peer_y)
        for j in (1, 2, 3):
            self.start(shard, block, 2 * j, functools.partial(chips.peer_z, j))
        self.start(shard, block, 16, chips.peer_core)
        self.own().start()

    def second(self, jz):
        self.arrive(0, jz, 0)
        self.pass_on((0, jz, 0), jz * 2 + 1, self.chips.peer_x)
        self.pass_on((0, jz, 0), jz * 2 + 8, self.chips.peer_y)
        self.core(0, jz, 0)

    def third(self, jz):
        place = (0, jz, 1) if jz < 2 else (1, jz, 0)
        self.arrive(*place)
        self.pass_on(place, 9 + jz * 2, self.chips.peer_y if jz < 2 else self.chips.peer_x)
        self.core(*place)

    def fourth(self, jz):
        place = (1, jz, 0) if jz < 2 else (0, jz, 1)
        self.arrive(*place)
        self.core(*place)

    def fifth(self, jz):
        self.arrive(1, jz, 1)
        self.core(1, jz, 1)

    def last(self):
        self.own().wait()
        for jy in range(2):
            for jz in range(4):
                for jx in range(2):
                    self.arrive(jy, jz, jx, 1)
        self.finish()

    def steps(self):
        order = (0, 2, 1, 3)
        parts = [[self.begin]]
        parts.append([functools.partial(self.second, j) for j in (1, 2, 3)])
        parts.append([functools.partial(self.third, j) for j in order])
        parts.append([functools.partial(self.fourth, j) for j in order])
        parts.append([functools.partial(self.fifth, j) for j in order])
        parts.append([self.last])
        return parts


GATHER_SEMS = [
    pltpu.SemaphoreType.DMA((32,)),
    pltpu.SemaphoreType.DMA((32,)),
    pltpu.SemaphoreType.DMA,
]


class Ticks:
    def __init__(self, steps, spots):
        self.step = pl.program_id(0)
        total = 4 * spots
        self.table = [[] for unused in range(total)]
        count = len(steps)
        for i, step in enumerate(steps):
            at = 0 if i == 0 else total - 1 if i == count - 1 else 1 + (i - 1) * (total - 2) // (count - 2)
            self.table[at].append(step)
        self.spots = spots

    def __call__(self, spot):
        for turn in range(4):
            todo = self.table[turn * self.spots + spot]
            if todo:

                @pl.when(self.step == turn)
                def run(todo=todo):
                    for step in todo:
                        step()


def no_ticks(spot):
    return None


def gather_ticks(refs, spots):
    chips = Chips()
    work = Gather(chips, *refs)
    steps = [step for phase in work.steps() for step in phase]
    begin = steps[0]

    def enter():
        chips.greet()
        begin()

    return Ticks([enter] + steps[1:], spots)


def gather_kernel(count, *refs):
    shards, fulls, sems = refs[:count], refs[count : 2 * count], refs[2 * count :]
    chips = Chips()
    chips.greet()
    plans = [Gather(chips, shards[i], fulls[i], *sems[3 * i : 3 * i + 3]).steps() for i in range(count)]
    for step in woven(plans):
        step()


def gather_all(shards, ident):
    count = len(shards)
    return pl.pallas_call(
        functools.partial(gather_kernel, count),
        out_shape=[jax.ShapeDtypeStruct((s.shape[0], 4, 8) + s.shape[1:], s.dtype) for s in shards],
        in_specs=[pl.BlockSpec(memory_space=pl.ANY)] * count,
        out_specs=[pl.BlockSpec(memory_space=pl.ANY)] * count,
        scratch_shapes=GATHER_SEMS * count,
        compiler_params=pltpu.CompilerParams(collective_id=ident, has_side_effects=True),
    )(*shards)


class Scatter(Work):
    def __init__(self, chips, full, total, m, row, near, far, own, send, recv, load):
        super().__init__(chips, send, recv)
        self.full, self.total = full, total
        self.m, self.row, self.size = m, row, near.shape[1]
        self.near, self.far, self.own, self.load = near, far, own, load
        diagonal = [(1, jz, 1) for jz in (0, 2, 1, 3)]
        straight = [(1, jz, 0) if jz < 2 else (0, jz, 1) for jz in (0, 2, 1, 3)]
        bent = [(0, jz, 1) if jz < 2 else (1, jz, 0) for jz in (0, 2, 1, 3)]
        column = [(0, jz, 0) for jz in (2, 3, 1, 0)]
        self.order = diagonal + straight + bent + column
        self.turns = {jy * 8 + jz * 2 + jx: i for i, (jy, jz, jx) in enumerate(self.order)}

    def block(self, jy, jz, jx, jc):
        chips = self.chips
        return self.full.at[
            self.m, chips.mp_at(jy, jc), chips.dp_at(jz, jx), pl.ds(self.row, self.size)
        ]

    def fetch(self, turn):
        buffer = turn % self.own.shape[0]
        return pltpu.make_async_copy(
            self.block(*self.order[turn], 0), self.own.at[buffer], self.load.at[buffer]
        )

    def begin(self):
        for place in self.order:
            slot = place[0] * 8 + place[1] * 2 + place[2]
            self.start(
                functools.partial(self.block, *place, 1),
                functools.partial(lambda at: self.near.at[at], slot),
                slot,
                self.chips.peer_core,
            )
        for turn in range(self.own.shape[0]):
            self.fetch(turn).start()

    def add(self, slot, others):
        turn, near, own = self.turns[slot], self.near, self.own
        buffer = turn % own.shape[0]
        self.fetch(turn).wait()
        self.arrived(near.at[slot], slot)

        def rows(i, carry):
            at = pl.ds(pl.multiple_of(i * 16, 16), 16)
            value = near[slot, at].astype(jnp.float32) + own[buffer, at].astype(jnp.float32)
            for index in others:
                value += self.far[index, at].astype(jnp.float32)
            near[slot, at] = value.astype(jnp.bfloat16)
            return carry

        lax.fori_loop(0, self.size // 16, rows, 0)
        if turn + own.shape[0] < 16:
            self.fetch(turn + own.shape[0]).start()

    def move(self, slot, index, where, peer):
        self.start(lambda: self.near.at[slot], lambda: self.far.at[index], where, peer)

    def along_x(self, slot, jz):
        self.move(slot, 4 + jz, 20 + jz, self.chips.peer_x)

    def along_y(self, slot, jz):
        self.move(slot, 8 + jz, 24 + jz, self.chips.peer_y)

    def diagonal(self, jz):
        slot = 9 + jz * 2
        self.add(slot, [])
        self.move(slot, jz, 16 + jz, self.chips.peer_y if jz < 2 else self.chips.peer_x)

    def straight(self, jz):
        slot = jz * 2 + (8 if jz < 2 else 1)
        self.add(slot, [])
        (self.along_y if jz < 2 else self.along_x)(slot, jz)

    def bent(self, jz):
        slot = jz * 2 + (1 if jz < 2 else 8)
        self.arrived(self.far.at[jz], 16 + jz)
        self.add(slot, [jz])
        (self.along_x if jz < 2 else self.along_y)(slot, jz)

    def column(self, jz):
        self.arrived(self.far.at[4 + jz], 20 + jz)
        self.arrived(self.far.at[8 + jz], 24 + jz)
        if jz:
            self.add(jz * 2, [4 + jz, 8 + jz])
            self.move(jz * 2, 11 + jz, 27 + jz, functools.partial(self.chips.peer_z, jz))

    def last(self):
        turn, near, own, far = 15, self.near, self.own, self.far
        buffer = turn % own.shape[0]
        self.fetch(turn).wait()
        self.arrived(near.at[0], 0)
        for jz in (2, 3, 1):
            self.arrived(far.at[11 + jz], 27 + jz)

        def rows(i, carry):
            at = pl.ds(pl.multiple_of(i * 16, 16), 16)
            value = near[0, at].astype(jnp.float32) + own[buffer, at].astype(jnp.float32)
            for index in (4, 8, 12, 13, 14):
                value += far[index, at].astype(jnp.float32)
            self.total[self.m, pl.ds(pl.multiple_of(self.row + i * 16, 16), 16)] = value
            return carry

        lax.fori_loop(0, self.size // 16, rows, 0)

    def steps(self):
        order = (0, 2, 1, 3)
        parts = [[self.begin]]
        parts.append([functools.partial(self.diagonal, j) for j in order])
        parts[-1] += [functools.partial(self.straight, j) for j in order]
        parts.append([functools.partial(self.bent, j) for j in order])
        parts.append([functools.partial(self.column, j) for j in (2, 3, 1, 0)])
        parts.append([self.last])
        return parts


def chunks_of(k, pieces):
    sizes = {1: [144], 2: [80, 64], 3: [48, 48, 48]}[pieces]
    return [(m, sum(sizes[:i]), sizes[i]) for m in range(k) for i in range(pieces)]


def scatter_scratch(chunks):
    out = []
    for unused, unused_row, size in chunks:
        out += [
            pltpu.VMEM((16, size, 1152), jnp.bfloat16),
            pltpu.VMEM((15, size, 1152), jnp.bfloat16),
            pltpu.VMEM((4, size, 1152), jnp.bfloat16),
            pltpu.SemaphoreType.DMA((31,)),
            pltpu.SemaphoreType.DMA((31,)),
            pltpu.SemaphoreType.DMA((4,)),
        ]
    return out


def woven(plans):
    order = []
    deep = max(len(plan) for plan in plans)
    for turn in range(len(plans) + deep - 1):
        for i, plan in enumerate(plans):
            if 0 <= turn - i < len(plan):
                order += plan[turn - i]
    return order


def scatter_kernel(chunks, full, total, *scratch):
    chips = Chips()
    chips.greet()
    works = [
        Scatter(chips, full, total, m, row, *scratch[6 * i : 6 * i + 6])
        for i, (m, row, unused) in enumerate(chunks)
    ]
    for step in woven([work.steps() for work in works]):
        step()
    for work in works:
        work.finish()


def scatter_one(full, ident, pieces=PIECES):
    k = full.shape[0]
    chunks = chunks_of(k, pieces[k])
    return pl.pallas_call(
        functools.partial(scatter_kernel, chunks),
        out_shape=jax.ShapeDtypeStruct((k,) + full.shape[3:], jnp.float32),
        in_specs=[pl.BlockSpec(memory_space=pl.ANY)],
        out_specs=pl.BlockSpec(memory_space=pltpu.VMEM),
        scratch_shapes=scatter_scratch(chunks),
        compiler_params=pltpu.CompilerParams(
            collective_id=ident, has_side_effects=True, vmem_limit_bytes=BIG
        ),
    )(full)


CLIPS, PARTS = 8, 4


def all_peers(names):
    peers = []
    for name, size in ((DP, CLIPS), (MP, PARTS)):
        if name in names:
            me = lax.axis_index(name)
            peers += [{name: (me + o) % size} for o in range(1, size)]
    return peers


def greet_all(peers):
    barrier = pltpu.get_barrier_semaphore()
    for peer in peers:
        pl.semaphore_signal(barrier, inc=1, device_id=peer, device_id_type=MESH)
    pl.semaphore_wait(barrier, len(peers))


def trade(name, size, source, target, landing, send, recv, first=0):
    me = lax.axis_index(name)

    def copy(o, src, dst):
        return pltpu.make_async_remote_copy(
            src_ref=src,
            dst_ref=dst,
            send_sem=send.at[first + o],
            recv_sem=recv.at[first + o],
            device_id={name: (me + o) % size},
            device_id_type=MESH,
        )

    out = [copy(o, source((me + o) % size), target()) for o in range(1, size)]
    for one in out:
        one.start()
    for o in range(1, size):
        land = landing((me + size - o) % size)
        copy(o, land, land).wait_recv()
    for one in out:
        one.wait_send()


def exchange_call(kernel, ident, out_shape, scratch, operand, anywhere=False):
    spec = pl.BlockSpec(memory_space=pl.ANY if anywhere else pltpu.VMEM)
    return pl.pallas_call(
        kernel,
        out_shape=out_shape,
        in_specs=[spec],
        out_specs=spec,
        scratch_shapes=scratch + [pltpu.SemaphoreType.DMA((18,)), pltpu.SemaphoreType.DMA((18,))],
        compiler_params=pltpu.CompilerParams(
            collective_id=ident, has_side_effects=True, vmem_limit_bytes=BIG
        ),
    )(operand)


def share_kernel(name, size, x, out, send, recv):
    me = lax.axis_index(name)
    greet_all(all_peers((name,)))
    out[me] = x[...]
    trade(name, size, lambda to: x, lambda: out.at[me], lambda at: out.at[at], send, recv)


def share(x, name, ident):
    size = CLIPS if name == DP else PARTS
    shape = jax.ShapeDtypeStruct((size,) + x.shape, x.dtype)
    return exchange_call(functools.partial(share_kernel, name, size), ident, shape, [], x)


def gathered_sum(refs, count):
    value = refs[0]
    for i in range(1, count):
        value = value + refs[i]
    return value


def part_sum_kernel(x, out, near, one, send, recv):
    part, clip = lax.axis_index(MP), lax.axis_index(DP)
    greet_all(all_peers((DP, MP)))
    near[part] = x[...]
    trade(MP, PARTS, lambda to: x, lambda: near.at[part], lambda at: near.at[at], send, recv, 8)
    one[...] = gathered_sum(near, PARTS)
    out[clip] = one[...]
    trade(DP, CLIPS, lambda to: one, lambda: out.at[clip], lambda at: out.at[at], send, recv)


def part_sum(x, ident):
    scratch = [pltpu.VMEM((PARTS,) + x.shape, x.dtype), pltpu.VMEM(x.shape, x.dtype)]
    shape = jax.ShapeDtypeStruct((CLIPS,) + x.shape, x.dtype)
    return exchange_call(part_sum_kernel, ident, shape, scratch, x)


def whole_sum_kernel(x, out, far, near, one, two, send, recv):
    part, clip = lax.axis_index(MP), lax.axis_index(DP)
    greet_all(all_peers((DP, MP)))
    far[clip] = x[clip]
    trade(DP, CLIPS, lambda to: x.at[to], lambda: far.at[clip], lambda at: far.at[at], send, recv)
    one[...] = gathered_sum(far, CLIPS)
    near[part] = one[...]
    trade(MP, PARTS, lambda to: one, lambda: near.at[part], lambda at: near.at[at], send, recv, 7)
    two[...] = gathered_sum(near, PARTS)
    out[clip] = two[...]
    trade(DP, CLIPS, lambda to: two, lambda: out.at[clip], lambda at: out.at[at], send, recv, 10)


def whole_sum(x, ident):
    row = x.shape[1:]
    scratch = [pltpu.VMEM((n,) + row, x.dtype) for n in (CLIPS, PARTS)]
    scratch += [pltpu.VMEM(row, x.dtype)] * 2
    return exchange_call(whole_sum_kernel, ident, jax.ShapeDtypeStruct(x.shape, x.dtype), scratch, x)


def deal_kernel(x, out, send, recv):
    clip = lax.axis_index(DP)
    greet_all(all_peers((DP,)))
    out[clip] = x[clip]
    trade(DP, CLIPS, lambda to: x.at[to], lambda: out.at[clip], lambda at: out.at[at], send, recv)


def deal(x, ident):
    return exchange_call(deal_kernel, ident, jax.ShapeDtypeStruct(x.shape, x.dtype), [], x)


def to_time_kernel(x, out, local, send, recv):
    part = lax.axis_index(MP)
    greet_all(all_peers((MP,)))
    own = pltpu.make_async_copy(x.at[part], out.at[:, part], local)
    own.start()
    trade(MP, PARTS, lambda to: x.at[to], lambda: out.at[:, part], lambda at: out.at[:, at], send, recv)
    own.wait()


def to_space_kernel(x, out, local, send, recv):
    part = lax.axis_index(MP)
    greet_all(all_peers((MP,)))
    own = pltpu.make_async_copy(x.at[:, part], out.at[part], local)
    own.start()
    trade(MP, PARTS, lambda to: x.at[:, to], lambda: out.at[part], lambda at: out.at[at], send, recv)
    own.wait()


def to_time(x, ident):
    shape = jax.ShapeDtypeStruct((2, FR, PM // 8, D), x.dtype)
    operand = x.reshape(FR, 2, PM // 8, D)
    return exchange_call(
        to_time_kernel, ident, shape, [pltpu.SemaphoreType.DMA], operand, True
    ).reshape(PM, D)


def to_space(x, ident):
    shape = jax.ShapeDtypeStruct((FR, 2, PM // 8, D), x.dtype)
    operand = x.reshape(2, FR, PM // 8, D)
    return exchange_call(
        to_space_kernel, ident, shape, [pltpu.SemaphoreType.DMA], operand, True
    ).reshape(PM, D)


def normal_parts(x):
    centered = x - jnp.mean(x, -1, keepdims=True)
    inverse = lax.rsqrt(jnp.mean(centered * centered, -1, keepdims=True) + EPS_NORM)
    return centered * inverse, inverse


def normal_back(x, scale_vec, grad):
    normed, inverse = normal_parts(x)
    inner = grad * (1.0 + scale_vec)
    d_x = inverse * (
        inner
        - jnp.mean(inner, -1, keepdims=True)
        - normed * jnp.mean(inner * normed, -1, keepdims=True)
    )
    return d_x, jnp.sum(grad, 0, keepdims=True), jnp.sum(grad * normed, 0, keepdims=True)


def mxu(left, right, dims=(((1,), (0,)), ((), ()))):
    return lax.dot_general(left, right, dims, preferred_element_type=jnp.float32)


def padded_heads(pieces, before, after):
    rows = pieces[0].shape[0]
    parts = list(pieces)
    if before:
        parts.insert(0, jnp.zeros((rows, before), pieces[0].dtype))
    if after:
        parts.append(jnp.zeros((rows, after), pieces[0].dtype))
    return jnp.concatenate(parts, 1)


def head_forward(query, key_rows, value_rows, bias):
    scores = mxu(key_rows, query, CONTRACT_LAST) * HD ** (-0.5) + bias
    expd = jnp.exp(scores - jnp.max(scores, 0, keepdims=True))
    probs = (expd / jnp.sum(expd, 0, keepdims=True)).astype(jnp.bfloat16)
    return mxu(probs, value_rows, CONTRACT_ROWS)


def head_backward(query, key_rows, value_rows, bias, d_mixed):
    scores = mxu(key_rows, query, CONTRACT_LAST) * HD ** (-0.5) + bias
    expd = jnp.exp(scores - jnp.max(scores, 0, keepdims=True))
    probs = expd / jnp.sum(expd, 0, keepdims=True)
    d_value = mxu(probs.astype(jnp.bfloat16), d_mixed)
    d_probs = mxu(value_rows, d_mixed, CONTRACT_LAST)
    offset = jnp.sum(d_probs * probs, 0, keepdims=True)
    d_scores = (probs * (d_probs - offset) * HD ** (-0.5)).astype(jnp.bfloat16)
    d_query = mxu(d_scores, key_rows, CONTRACT_ROWS)
    d_key = mxu(d_scores, query)
    return d_query, d_key, d_value


def self_forward_kernel(tiles, tick, x, mods, bias, panel, mask, out, branch, source, proj, mixed, total):
    step = pl.program_id(0)
    rows = PM // tiles
    tick(0)

    @pl.when(step == 0)
    def first():
        normed, unused = normal_parts(x[...])
        source[...] = (normed * (1.0 + mods[1:2]) + mods[0:1]).astype(jnp.bfloat16)
        total[...] = jnp.zeros_like(total)

    values = mxu(source[...], panel[0, :, :896]) + bias[0]
    values = values.astype(jnp.bfloat16)
    proj[0] = values
    heads = []
    for h in range(4):
        tops = []
        for t in range(tiles):
            part = values[t * rows : (t + 1) * rows]
            at = h * HD
            tops.append(
                head_forward(
                    part[:, at : at + HD],
                    part[:, SPAN + at : SPAN + at + HD],
                    part[:, 2 * SPAN + at : 2 * SPAN + at + HD],
                    mask[...],
                )
            )
        heads.append(jnp.concatenate(tops, 0) if tiles > 1 else tops[0])
        tick(h + 1)
    packed = padded_heads(heads, 96, 0).astype(jnp.bfloat16)
    mixed[0] = packed
    total[...] += mxu(packed, panel[0, :, 768:], CONTRACT_LAST)

    @pl.when(step == 3)
    def last():
        value = total[...] + mods[6:7]
        branch[...] = value
        out[...] = x[...] + mods[2:3] * value

    tick(5)


def whole(shape):
    return pl.BlockSpec(shape, lambda i: (0,) * len(shape))


def slab(shape):
    return pl.BlockSpec((1,) + shape, lambda i: (i,) + (0,) * len(shape))


def grid_params(ident=None):
    if ident is None:
        return pltpu.CompilerParams(vmem_limit_bytes=BIG)
    return pltpu.CompilerParams(vmem_limit_bytes=BIG, collective_id=ident, has_side_effects=True)


def with_gather(kernel, spots, inputs, outputs):
    def run(*refs):
        ins, shard = refs[:inputs], refs[inputs]
        outs, full = refs[inputs + 1 : inputs + 1 + outputs], refs[inputs + 1 + outputs]
        scratch, sems = refs[inputs + outputs + 2 : -3], refs[-3:]
        kernel(gather_ticks((shard, full) + sems, spots), *ins, *outs, *scratch)

    return run


def call_with(kernel, spots, operands, in_specs, out_specs, out_shape, scratch, shard, ident):
    if shard is None:
        return pl.pallas_call(
            functools.partial(kernel, no_ticks),
            grid=(4,),
            in_specs=in_specs,
            out_specs=out_specs,
            out_shape=out_shape,
            scratch_shapes=scratch,
            compiler_params=grid_params(),
        )(*operands)
    remote = pl.BlockSpec(memory_space=pl.ANY)
    full = jax.ShapeDtypeStruct((shard.shape[0], 4, 8) + shard.shape[1:], shard.dtype)
    return pl.pallas_call(
        with_gather(kernel, spots, len(in_specs), len(out_specs)),
        grid=(4,),
        in_specs=in_specs + [remote],
        out_specs=out_specs + [remote],
        out_shape=out_shape + [full],
        scratch_shapes=scratch + GATHER_SEMS,
        compiler_params=grid_params(ident),
    )(*operands, shard)


def self_forward(x, mods, bias, panels, mask, tiles, shard=None, ident=None):
    f32, bf16 = jnp.float32, jnp.bfloat16
    rows = PM // tiles
    return call_with(
        functools.partial(self_forward_kernel, tiles),
        6,
        (x, mods, bias, panels, mask),
        [whole((PM, D)), whole((8, D)), slab((1, 896)), slab((D, D)), whole((rows, rows))],
        [whole((PM, D)), whole((PM, D)), whole((PM, D)), slab((PM, 896)), slab((PM, 384))],
        [
            jax.ShapeDtypeStruct((PM, D), f32),
            jax.ShapeDtypeStruct((PM, D), f32),
            jax.ShapeDtypeStruct((PM, D), bf16),
            jax.ShapeDtypeStruct((4, PM, 896), bf16),
            jax.ShapeDtypeStruct((4, PM, 384), bf16),
        ],
        [pltpu.VMEM((PM, D), f32)],
        shard,
        ident,
    )


def self_backward_kernel(
    tiles, x, grad, mods, branch, source, proj, mixed, panel, mask, out, sums, d_bias, d_panel, d_branch, total
):
    step = pl.program_id(0)
    rows = PM // tiles

    @pl.when(step == 0)
    def first():
        value = grad[...]
        low = (mods[2:3] * value).astype(jnp.bfloat16)
        d_branch[...] = low
        sums[2:3] = jnp.sum(value * branch[...], 0, keepdims=True)
        sums[3:4] = jnp.sum(low.astype(jnp.float32), 0, keepdims=True)
        total[...] = jnp.zeros_like(total)

    low = d_branch[...]
    d_mixed = mxu(low, panel[0, :, 768:]).astype(jnp.bfloat16)
    values = proj[0]
    d_query, d_key, d_value = [], [], []
    for h in range(4):
        at = h * HD
        tops = []
        for t in range(tiles):
            part = values[t * rows : (t + 1) * rows]
            tops.append(
                head_backward(
                    part[:, at : at + HD],
                    part[:, SPAN + at : SPAN + at + HD],
                    part[:, 2 * SPAN + at : 2 * SPAN + at + HD],
                    mask[...],
                    d_mixed[t * rows : (t + 1) * rows, 96 + at : 96 + at + HD],
                )
            )
        for store, index in ((d_query, 0), (d_key, 1), (d_value, 2)):
            pieces = [top[index] for top in tops]
            store.append(jnp.concatenate(pieces, 0) if tiles > 1 else pieces[0])
    d_proj = padded_heads(d_query + d_key + d_value, 0, 32).astype(jnp.bfloat16)
    d_bias[0] = jnp.sum(d_proj.astype(jnp.float32), 0, keepdims=True)
    columns = lax.broadcasted_iota(jnp.int32, (1, 896), 1)
    kept = jnp.where(columns < 3 * SPAN, panel[0, :, :896], jnp.zeros((), jnp.bfloat16))
    total[...] += mxu(d_proj, kept, CONTRACT_LAST)
    src = source[...]
    d_panel[0, :, :768] = mxu(src, d_proj[:, :768], CONTRACT_ROWS).astype(jnp.bfloat16)
    packed = mixed[0]
    d_panel[0, :, 768:896] = (
        mxu(src, d_proj[:, 768:], CONTRACT_ROWS) + mxu(low, packed[:, :128], CONTRACT_ROWS)
    ).astype(jnp.bfloat16)
    d_panel[0, :, 896:] = mxu(low, packed[:, 128:], CONTRACT_ROWS).astype(jnp.bfloat16)

    @pl.when(step == 3)
    def last():
        d_x, d_shift, d_scale = normal_back(x[...], mods[1:2], total[...])
        sums[0:1] = d_shift
        sums[1:2] = d_scale
        out[...] = grad[...] + d_x


def self_backward(x, grad, mods, branch, source, proj, mixed, panels, mask, tiles):
    f32, bf16 = jnp.float32, jnp.bfloat16
    rows = PM // tiles
    return pl.pallas_call(
        functools.partial(self_backward_kernel, tiles),
        grid=(4,),
        in_specs=[
            whole((PM, D)),
            whole((PM, D)),
            whole((8, D)),
            whole((PM, D)),
            whole((PM, D)),
            slab((PM, 896)),
            slab((PM, 384)),
            slab((D, D)),
            whole((rows, rows)),
        ],
        out_specs=[whole((PM, D)), whole((8, D)), slab((1, 896)), slab((D, D))],
        out_shape=[
            jax.ShapeDtypeStruct((PM, D), f32),
            jax.ShapeDtypeStruct((8, D), f32),
            jax.ShapeDtypeStruct((4, 1, 896), f32),
            jax.ShapeDtypeStruct((4, D, D), bf16),
        ],
        scratch_shapes=[pltpu.VMEM((PM, D), bf16), pltpu.VMEM((PM, D), f32)],
        compiler_params=grid_params(),
    )(x, grad, mods, branch, source, proj, mixed, panels, mask)


def cross_forward_kernel(tick, x, mods, bias, context, panel, mask, out, proj, pair, mixed, total):
    step = pl.program_id(0)
    tick(0)

    @pl.when(step == 0)
    def first():
        total[...] = jnp.zeros_like(total)

    query = (mxu(x[...].astype(jnp.bfloat16), panel[0, :, :384]) + bias[0, :, :384]).astype(jnp.bfloat16)
    both = (mxu(context[...], panel[0, :, 256:896]) + bias[0, :, 256:896]).astype(jnp.bfloat16)
    proj[0] = query
    pair[0] = both
    heads = []
    for h in range(4):
        at = h * HD
        heads.append(
            head_forward(
                query[:, at : at + HD],
                both[:, 32 + at : 32 + at + HD],
                both[:, 32 + SPAN + at : 32 + SPAN + at + HD],
                mask[...],
            )
        )
        tick(h + 1)
    packed = padded_heads(heads, 96, 0).astype(jnp.bfloat16)
    mixed[0] = packed
    total[...] += mxu(packed, panel[0, :, 768:], CONTRACT_LAST)

    @pl.when(step == 3)
    def last():
        out[...] = x[...] + total[...] + mods[6:7]

    tick(5)


def cross_forward(x, mods, bias, context, panels, mask, shard=None, ident=None):
    f32, bf16 = jnp.float32, jnp.bfloat16
    return call_with(
        cross_forward_kernel,
        6,
        (x, mods, bias, context, panels, mask),
        [
            whole((PM, D)),
            whole((8, D)),
            slab((1, 896)),
            whole((128, D)),
            slab((D, D)),
            whole((128, 1)),
        ],
        [whole((PM, D)), slab((PM, 384)), slab((128, 640)), slab((PM, 384))],
        [
            jax.ShapeDtypeStruct((PM, D), f32),
            jax.ShapeDtypeStruct((4, PM, 384), bf16),
            jax.ShapeDtypeStruct((4, 128, 640), bf16),
            jax.ShapeDtypeStruct((4, PM, 384), bf16),
        ],
        [pltpu.VMEM((PM, D), f32)],
        shard,
        ident,
    )


def cross_backward_kernel(
    x, grad, context, proj, pair, mixed, panel, mask, out, d_context, sums, d_bias, d_panel, total
):
    step = pl.program_id(0)

    @pl.when(step == 0)
    def first():
        low = grad[...].astype(jnp.bfloat16)
        sums[0:1] = jnp.sum(low.astype(jnp.float32), 0, keepdims=True)
        total[...] = jnp.zeros_like(total)
        d_context[...] = jnp.zeros_like(d_context)

    low = grad[...].astype(jnp.bfloat16)
    d_mixed = mxu(low, panel[0, :, 768:]).astype(jnp.bfloat16)
    query, both = proj[0], pair[0]
    d_query, d_key, d_value = [], [], []
    for h in range(4):
        at = h * HD
        one = head_backward(
            query[:, at : at + HD],
            both[:, 32 + at : 32 + at + HD],
            both[:, 32 + SPAN + at : 32 + SPAN + at + HD],
            mask[...],
            d_mixed[:, 96 + at : 96 + at + HD],
        )
        d_query.append(one[0])
        d_key.append(one[1])
        d_value.append(one[2])
    d_ask = padded_heads(d_query, 0, 96).astype(jnp.bfloat16)
    d_both = padded_heads(d_key + d_value, 32, 32).astype(jnp.bfloat16)
    sum_both = jnp.sum(d_both.astype(jnp.float32), 0, keepdims=True)
    d_bias[0, :, :384] = jnp.sum(d_ask.astype(jnp.float32), 0, keepdims=True)
    d_bias[0, :, 384:] = sum_both
    total[...] += mxu(d_ask, panel[0, :, :384], CONTRACT_LAST)
    d_context[...] += mxu(d_both, panel[0, :, 256:896], CONTRACT_LAST)
    src, ctx, packed = x[...].astype(jnp.bfloat16), context[...], mixed[0]
    d_panel[0, :, :256] = mxu(src, d_ask[:, :256], CONTRACT_ROWS).astype(jnp.bfloat16)
    d_panel[0, :, 256:384] = (
        mxu(src, d_ask[:, 256:], CONTRACT_ROWS) + mxu(ctx, d_both[:, :128], CONTRACT_ROWS)
    ).astype(jnp.bfloat16)
    d_panel[0, :, 384:768] = mxu(ctx, d_both[:, 128:512], CONTRACT_ROWS).astype(jnp.bfloat16)
    d_panel[0, :, 768:896] = (
        mxu(ctx, d_both[:, 512:], CONTRACT_ROWS) + mxu(low, packed[:, :128], CONTRACT_ROWS)
    ).astype(jnp.bfloat16)
    d_panel[0, :, 896:] = mxu(low, packed[:, 128:], CONTRACT_ROWS).astype(jnp.bfloat16)

    @pl.when(step == 3)
    def last():
        out[...] = grad[...] + total[...]


def cross_backward(x, grad, context, proj, pair, mixed, panels, mask):
    f32, bf16 = jnp.float32, jnp.bfloat16
    return pl.pallas_call(
        cross_backward_kernel,
        grid=(4,),
        in_specs=[
            whole((PM, D)),
            whole((PM, D)),
            whole((128, D)),
            slab((PM, 384)),
            slab((128, 640)),
            slab((PM, 384)),
            slab((D, D)),
            whole((128, 1)),
        ],
        out_specs=[whole((PM, D)), whole((128, D)), whole((8, D)), slab((1, 1024)), slab((D, D))],
        out_shape=[
            jax.ShapeDtypeStruct((PM, D), f32),
            jax.ShapeDtypeStruct((128, D), f32),
            jax.ShapeDtypeStruct((8, D), f32),
            jax.ShapeDtypeStruct((4, 1, 1024), f32),
            jax.ShapeDtypeStruct((4, D, D), bf16),
        ],
        scratch_shapes=[pltpu.VMEM((PM, D), f32)],
        compiler_params=grid_params(),
    )(x, grad, context, proj, pair, mixed, panels, mask)


GELU_A = math.sqrt(2.0 / math.pi)
GELU_B = 0.044715


def ffn_forward_kernel(tick, x, mods, bias, w_in, w_out, out, branch, source, pre, total):
    step = pl.program_id(0)
    tick(0)

    @pl.when(step == 0)
    def first():
        normed, unused = normal_parts(x[...])
        source[...] = (normed * (1.0 + mods[4:5]) + mods[3:4]).astype(jnp.bfloat16)
        total[...] = jnp.zeros_like(total)

    value = mxu(source[...], w_in[0, 0]) + bias[0]
    pre[0] = value
    tick(1)
    hidden = 0.5 * value * (1.0 + jnp.tanh(GELU_A * (value + GELU_B * value * value * value)))
    tick(2)
    total[...] += mxu(hidden.astype(jnp.bfloat16), w_out[0, 0], CONTRACT_LAST)

    @pl.when(step == 3)
    def last():
        result = total[...] + mods[6:7]
        branch[...] = result
        out[...] = x[...] + mods[5:6] * result

    tick(3)


def half(index):
    return pl.BlockSpec((1, 1, D, D), lambda i: (index, i, 0, 0))


def ffn_forward_chip(x, mods, bias, panels, shard=None, ident=None):
    f32, bf16 = jnp.float32, jnp.bfloat16
    return call_with(
        ffn_forward_kernel,
        4,
        (x, mods, bias, panels, panels),
        [whole((PM, D)), whole((8, D)), slab((1, D)), half(0), half(1)],
        [whole((PM, D)), whole((PM, D)), whole((PM, D)), slab((PM, D))],
        [
            jax.ShapeDtypeStruct((PM, D), f32),
            jax.ShapeDtypeStruct((PM, D), f32),
            jax.ShapeDtypeStruct((PM, D), bf16),
            jax.ShapeDtypeStruct((4, PM, D), f32),
        ],
        [pltpu.VMEM((PM, D), f32)],
        shard,
        ident,
    )


def ffn_backward_kernel(
    x, grad, mods, branch, source, pre, w_in, w_out, out, sums, d_bias, d_panel, d_branch, total
):
    step = pl.program_id(0)

    @pl.when(step == 0)
    def first():
        value = grad[...]
        low = (mods[5:6] * value).astype(jnp.bfloat16)
        d_branch[...] = low
        sums[2:3] = jnp.sum(value * branch[...], 0, keepdims=True)
        sums[3:4] = jnp.sum(low.astype(jnp.float32), 0, keepdims=True)
        total[...] = jnp.zeros_like(total)

    low = d_branch[...]
    value = pre[0]
    square = value * value
    bent = jnp.tanh(GELU_A * (value + GELU_B * value * square))
    slope = 0.5 * (1.0 + bent) + 0.5 * value * (1.0 - bent * bent) * GELU_A * (
        1.0 + 3.0 * GELU_B * square
    )
    hidden = (0.5 * value * (1.0 + bent)).astype(jnp.bfloat16)
    d_pre = (mxu(low, w_out[0, 0]) * slope).astype(jnp.bfloat16)
    d_bias[0] = jnp.sum(d_pre.astype(jnp.float32), 0, keepdims=True)
    total[...] += mxu(d_pre, w_in[0, 0], CONTRACT_LAST)
    d_panel[0, 0] = mxu(source[...], d_pre, CONTRACT_ROWS).astype(jnp.bfloat16)
    d_panel[1, 0] = mxu(low, hidden, CONTRACT_ROWS).astype(jnp.bfloat16)

    @pl.when(step == 3)
    def last():
        d_x, d_shift, d_scale = normal_back(x[...], mods[4:5], total[...])
        sums[0:1] = d_shift
        sums[1:2] = d_scale
        out[...] = grad[...] + d_x


def ffn_backward_chip(x, grad, mods, branch, source, pre, panels):
    f32, bf16 = jnp.float32, jnp.bfloat16
    return pl.pallas_call(
        ffn_backward_kernel,
        grid=(4,),
        in_specs=[
            whole((PM, D)),
            whole((PM, D)),
            whole((8, D)),
            whole((PM, D)),
            whole((PM, D)),
            slab((PM, D)),
            half(0),
            half(1),
        ],
        out_specs=[
            whole((PM, D)),
            whole((8, D)),
            slab((1, D)),
            pl.BlockSpec((2, 1, D, D), lambda i: (0, i, 0, 0)),
        ],
        out_shape=[
            jax.ShapeDtypeStruct((PM, D), f32),
            jax.ShapeDtypeStruct((8, D), f32),
            jax.ShapeDtypeStruct((4, 1, D), f32),
            jax.ShapeDtypeStruct((2, 4, D, D), bf16),
        ],
        scratch_shapes=[pltpu.VMEM((PM, D), bf16), pltpu.VMEM((PM, D), f32)],
        compiler_params=grid_params(),
    )(x, grad, mods, branch, source, pre, panels, panels)


def modulate_back(x, shift_vec, scale_vec, grad):
    unused, pull = jax.vjp(modulate, x, shift_vec, scale_vec)
    return pull(grad)


def padded_rows(value):
    return jnp.pad(value, ((0, 128 - value.shape[0]), (0, 0)))


def local_rows(full, group):
    return lax.dynamic_slice_in_dim(full, group * EMB_LOCAL, EMB_LOCAL, 1)


def per_device_chips(
    latents,
    noise,
    caption,
    caption_lens,
    timesteps,
    grid_hw,
    frame_counts,
    attn_mats,
    ffn_mats,
    embed_mats,
    vectors,
    attn_first,
    ffn_first,
    embed_first,
    vector_first,
    attn_second,
    ffn_second,
    embed_second,
    vector_second,
    attn_ema,
    ffn_ema,
    embed_ema,
    vector_ema,
):
    group = lax.axis_index(DP)
    part = lax.axis_index(MP)
    clips = timesteps.shape[0]
    parts = unpack(vectors)
    bf16 = jnp.bfloat16
    f32 = jnp.float32

    attn_low = attn_mats.astype(bf16).reshape(3, BLOCK, 4, 4, HD).swapaxes(2, 3).reshape(3, BLOCK, D)
    ffn_low = ffn_mats.astype(bf16)

    def panels(full):
        full = full.reshape(full.shape[:2] + (D, D))
        return full if full.shape[0] > 1 else full[0]

    w_space = panels(gather_all([attn_low[0:1]], 0)[0])

    pick = jnp.arange(clips, dtype=jnp.int32) == group

    def select(values):
        return jnp.sum(jnp.where(pick, values, 0))

    tstep = select(timesteps)
    cap_len = select(caption_lens)
    height = select(grid_hw[:, 0])
    width_grid = select(grid_hw[:, 1])
    frames = select(frame_counts)
    count = jnp.sum(frame_counts * grid_hw[:, 0] * grid_hw[:, 1]).astype(f32)
    betas, cumul = roster()
    step_ids = jnp.arange(1000, dtype=jnp.int32)
    alpha_bar = jnp.sum(jnp.where(step_ids == tstep, cumul, 0.0))
    alpha_prev = jnp.sum(jnp.where(step_ids == tstep - 1, cumul, 0.0))
    beta_now = jnp.sum(jnp.where(step_ids == tstep, betas, 0.0))

    embed_low = embed_mats.astype(bf16)
    width_local = embed_low.shape[1]
    captions = lax.all_gather(caption[0], DP, axis=0, tiled=True)
    lead = TFREQ + TXT
    cap_rows = local_rows(jnp.pad(captions, ((0, 0), (TFREQ, EMB_ALL - lead))), group)
    freq = waves(timesteps.astype(f32), TFREQ).astype(bf16)
    freq_rows = local_rows(jnp.pad(freq, ((0, 0), (0, EMB_ALL - TFREQ))), group)

    def from_rows(local):
        return part_sum(local, 1).swapaxes(0, 1).reshape(clips, EMB_ALL)

    def over_clips(value):
        return jnp.sum(share(value, DP, 2), 0)

    t_pre = over_clips(jnp.dot(freq_rows, embed_low, preferred_element_type=f32))
    t_pre = t_pre + own_slice(parts[T_BIAS_ONE], part, width_local)
    t_hidden = jax.nn.silu(t_pre).astype(bf16)
    t_sum = from_rows(lax.dot_general(t_hidden, embed_low, CONTRACT_LAST, preferred_element_type=f32))
    t_emb_all = t_sum[:, lead : lead + D] + parts[T_BIAS_TWO]
    t_emb_local = lax.dynamic_slice_in_dim(t_emb_all, part * width_local, width_local, 1)
    silu_local = jax.nn.silu(t_emb_local).astype(bf16)
    mod_sum = from_rows(
        lax.dot_general(silu_local, embed_low, CONTRACT_LAST, preferred_element_type=f32)
    )[:, lead + 2 * D :]
    t_mod_vec = jnp.sum(jnp.where(pick[:, None], mod_sum, 0.0), 0) + parts[T_BIAS_MOD]
    t_emb = jnp.sum(jnp.where(pick[:, None], t_emb_all, 0.0), 0)

    c_two_row = lead + D - group * EMB_LOCAL
    c_row_ids = c_two_row + jnp.arange(D, dtype=jnp.int32)
    c_held = (c_two_row >= 0) & (c_two_row + D <= EMB_LOCAL)
    c_two = lax.dynamic_slice_in_dim(embed_low, jnp.clip(c_two_row, 0, EMB_LOCAL - D), D, 0)
    c_two = lax.psum(jnp.where(c_held, c_two, jnp.zeros_like(c_two)), DP)
    c_product = jnp.dot(cap_rows, embed_low, preferred_element_type=f32)
    c_pre = jnp.sum(deal(c_product.reshape(clips, CAP, width_local), 3), 0)
    c_pre = c_pre + own_slice(parts[C_BIAS_ONE], part, width_local)
    c_hidden = gelu_tanh(c_pre).astype(bf16)
    c_part = lax.dot_general(c_hidden, c_two, CONTRACT_LAST, preferred_element_type=f32)

    def over_parts(value):
        return jnp.sum(share(padded_rows(value.astype(bf16)), MP, 4).astype(f32), 0)

    context = padded_rows((over_parts(c_part)[:CAP] + parts[C_BIAS_TWO]).astype(bf16))

    area = height * width_grid
    patch_ids = jnp.arange(PM, dtype=jnp.int32)
    shifted = patch_ids - (PM - area)
    noisy = jnp.sqrt(alpha_bar) * latents[0] + jnp.sqrt(1.0 - alpha_bar) * noise[0]
    noisy_low = noisy.astype(bf16)
    position = jnp.concatenate(
        [
            waves((shifted // width_grid).astype(f32), D // 2),
            waves((shifted % width_grid).astype(f32), D // 2),
        ],
        -1,
    )
    x = jnp.dot(noisy_low, parts[PATCH_W].astype(bf16), preferred_element_type=f32)
    x = x + parts[PATCH_B] + position
    tables = parts[TABLES] + t_mod_vec.reshape(1, 6, D)
    mods0, mods1 = tables[0], tables[1]
    mask_space = jnp.where(patch_ids >= PM - area, 0.0, NEG_LARGE)[:, None]
    mask_space = jnp.broadcast_to(mask_space, (PM, PM))
    mask_cross = jnp.where(jnp.arange(128, dtype=jnp.int32) < cap_len, 0.0, NEG_LARGE)[:, None]
    half_ids = jnp.arange(PM // 2, dtype=jnp.int32)
    frame_ids, place_ids = half_ids // (PM // 8), half_ids % (PM // 8)
    mask_time = jnp.where(
        (place_ids[:, None] == place_ids[None]) & (frame_ids[:, None] >= FR - frames), 0.0, NEG_LARGE
    )
    biases = parts[ATTN_BIAS]

    def side(values):
        blank = jnp.zeros((4, SPAN), f32)
        rows = [values[0].reshape(4, SPAN), blank, values[1].reshape(4, SPAN), blank[:, :32]]
        return jnp.concatenate(rows, 1)[:, None]

    def vectors_of(mods, out_bias):
        return jnp.concatenate([mods, out_bias[None], jnp.zeros((1, D), f32)])

    x0 = x
    m_space, m_ffn0 = vectors_of(mods0, biases[0, 2]), vectors_of(mods0, parts[FFN_BIAS_TWO][0])
    x1, branch0, source0, proj0, mixed0, full = self_forward(
        x0, m_space, side(biases[0]), w_space, mask_space, 1, attn_low[2:3], 5
    )
    w_cross = panels(full)
    m_cross = vectors_of(mods0, biases[2, 2])
    x2, cross_q, cross_kv, mixed1, full = cross_forward(
        x1, m_cross, side(biases[2]), context, w_cross, mask_cross, ffn_low[0], 6
    )
    w_ffn0 = panels(full)
    bias_ffn = parts[FFN_BIAS_ONE].reshape(2, 4, 1, D)
    x3, branch2, source2, pre2, full = ffn_forward_chip(
        x2, m_ffn0, bias_ffn[0], w_ffn0, attn_low[1:2], 7
    )
    w_time = panels(full)
    x3 = x3 + waves((part - (FR - frames)).astype(f32)[None], D)

    share_rows = PM // FR
    pixels = jnp.concatenate([latents[0], noise[0]], 1).reshape(FR, share_rows, -1)
    pixels = lax.all_to_all(pixels, MP, 0, 0, tiled=True).reshape(FR, 2, PM // 8, -1)
    pixels = pixels.swapaxes(0, 1).reshape(PM, -1)
    latent_time, noise_time = pixels[:, :CIN], pixels[:, CIN:]
    x4 = to_time(x3, 8)
    m_time, m_ffn1 = vectors_of(mods1, biases[1, 2]), vectors_of(mods1, parts[FFN_BIAS_TWO][1])
    x5, branch4, source4, proj4, mixed4, full = self_forward(
        x4, m_time, side(biases[1]), w_time, mask_time, 2, ffn_low[1], 9
    )
    w_ffn1 = panels(full)
    x6, branch5, source5, pre5 = ffn_forward_chip(x5, m_ffn1, bias_ffn[1], w_ffn1)

    final_mods = parts[FINAL_TABLE] + t_emb
    final_source = modulate(x6, final_mods[0], final_mods[1]).astype(bf16)
    final_low = parts[FINAL_W].astype(bf16)
    output = (
        lax.dot_general(final_source, final_low, CONTRACT_LAST, preferred_element_type=f32)
        + parts[FINAL_B]
    )
    frozen = output[:, :CIN]
    noisy_time = jnp.sqrt(alpha_bar) * latent_time + jnp.sqrt(1.0 - alpha_bar) * noise_time
    row_ids = jnp.arange(PM, dtype=jnp.int32)
    row_frames = (row_ids % (PM // 2)) // (PM // 8)
    row_patches = part * share_rows + (row_ids // (PM // 2)) * (PM // 8) + row_ids % (PM // 8)
    valid = (row_frames >= FR - frames) & (row_patches >= PM - area)

    def shard_loss(values):
        losses = token_losses(
            values, frozen, latent_time, noise_time, (noisy_time, alpha_bar, alpha_prev, beta_now)
        )
        return jnp.sum(jnp.where(valid, losses, 0.0))

    loss_part, loss_pull = jax.vjp(shard_loss, output)
    d_output = loss_pull(1.0 / count)[0].astype(bf16)
    d_final_w = lax.dot_general(d_output, final_source, CONTRACT_ROWS, preferred_element_type=f32)
    d_final_b = jnp.sum(d_output.astype(f32), 0)
    d_final_source = jnp.dot(d_output, final_low, preferred_element_type=f32)
    grad_x, d_final_shift, d_final_scale = modulate_back(
        x6, final_mods[0], final_mods[1], d_final_source
    )

    def blocks(grads):
        return grads.reshape((-1, 4, 8, BLOCK, D))

    grad_x, sums5, bias5, d_ffn1 = ffn_backward_chip(
        x5, grad_x, m_ffn1, branch5, source5, pre5, w_ffn1
    )
    g_ffn1 = scatter_one(blocks(d_ffn1), 10)
    grad_x, sums4, bias4, d_time = self_backward(
        x4, grad_x, m_time, branch4, source4, proj4, mixed4, w_time, mask_time, 2
    )
    g_time = scatter_one(blocks(d_time), 11)
    d_mods1 = jnp.concatenate([sums4[:3], sums5[:3]])
    grad_x = to_space(grad_x, 12)

    grad_x, sums2, bias2, d_ffn0 = ffn_backward_chip(
        x2, grad_x, m_ffn0, branch2, source2, pre2, w_ffn0
    )
    g_ffn0 = scatter_one(blocks(d_ffn0), 10)
    grad_x, d_context, sums1, bias1, d_cross = cross_backward(
        x1, grad_x, context, cross_q, cross_kv, mixed1, w_cross, mask_cross
    )
    g_cross = scatter_one(blocks(d_cross), 11)

    first_part = (part == 0).astype(f32)
    d_context = over_parts(d_context)[:CAP].astype(bf16)
    d_c_bias_two = jnp.sum(d_context.astype(f32), 0) * first_part
    d_c_hidden = jnp.dot(d_context, c_two, preferred_element_type=f32)
    unused, cap_pull = jax.vjp(gelu_tanh, c_pre)
    d_c_pre = cap_pull(d_c_hidden)[0].astype(bf16)
    d_c_bias_one = jnp.sum(d_c_pre.astype(f32), 0)
    caption_all = lax.all_gather(
        jnp.concatenate([d_context, c_hidden, d_c_pre], 1), DP, axis=0, tiled=True
    )
    d_context_all = caption_all[:, :D]
    c_hidden_all = caption_all[:, D : D + width_local]
    d_c_pre_all = caption_all[:, D + width_local :]
    d_c_one = lax.dot_general(cap_rows, d_c_pre_all, CONTRACT_ROWS, preferred_element_type=f32)
    d_c_two = lax.dot_general(d_context_all, c_hidden_all, CONTRACT_ROWS, preferred_element_type=f32)

    grad_x, sums0, bias0, d_space = self_backward(
        x0, grad_x, m_space, branch0, source0, proj0, mixed0, w_space, mask_space, 1
    )
    g_space = scatter_one(blocks(d_space), 11)
    d_mods0 = jnp.concatenate([sums0[:3], sums2[:3]])

    def side_sums(values, at_query, at_value, out_bias):
        rows = [values[:, 0, at : at + SPAN].reshape(-1) for at in (at_query, at_value)]
        return jnp.stack(rows + [out_bias])

    d_patch = grad_x.astype(bf16)
    d_patch_b = jnp.sum(d_patch.astype(f32), 0)
    d_patch_w = lax.dot_general(noisy_low, d_patch, CONTRACT_ROWS, preferred_element_type=f32)

    d_mod_part = (d_mods0 + d_mods1).reshape(-1)
    d_temb_part = d_final_shift + d_final_scale
    d_mod_all = part_sum(jnp.concatenate([d_mod_part, d_temb_part]).reshape(8, 7 * D // 8), 13)
    d_mod_all = d_mod_all.reshape(clips, 7 * D)
    d_temb_sum = d_mod_all[:, 6 * D :]
    d_mod_low = d_mod_all[:, : 6 * D].astype(bf16)
    d_mod_rows = local_rows(jnp.pad(d_mod_low, ((0, 0), (lead + 2 * D, 0))), group)
    d_silu = over_clips(jnp.dot(d_mod_rows, embed_low, preferred_element_type=f32))
    unused, silu_pull = jax.vjp(jax.nn.silu, t_emb_local)
    d_temb_local = silu_pull(d_silu)[0]
    d_temb = share(d_temb_local, MP, 14).swapaxes(0, 1).reshape(clips, D) + d_temb_sum
    d_temb_rows = local_rows(jnp.pad(d_temb, ((0, 0), (lead, EMB_ALL - lead - D))), group)
    d_t_hidden = over_clips(
        jnp.dot(d_temb_rows, embed_low.astype(f32), precision=lax.Precision.HIGHEST)
    )
    unused, pre_pull = jax.vjp(jax.nn.silu, t_pre)
    d_t_pre = pre_pull(d_t_hidden)[0]

    def outer(left, right):
        return lax.dot_general(
            left.astype(f32), right.astype(f32), CONTRACT_ROWS, precision=lax.Precision.HIGHEST
        )

    g_embed = (
        lax.dot_general(d_mod_rows, silu_local, CONTRACT_ROWS, preferred_element_type=f32)
        + outer(jnp.concatenate([d_temb_rows, freq_rows.astype(f32)]), jnp.concatenate([t_hidden.astype(f32), d_t_pre]))
        + d_c_one
    )
    here = lax.dynamic_slice_in_dim(g_embed, jnp.clip(c_two_row, 0, EMB_LOCAL - D), D, 0)
    g_embed = lax.dynamic_update_slice_in_dim(
        g_embed, jnp.where(c_held, d_c_two, here), jnp.clip(c_two_row, 0, EMB_LOCAL - D), 0
    )

    first_clip = pick.astype(f32) * first_part
    vector_grads = {
        PATCH_W: d_patch_w,
        PATCH_B: d_patch_b,
        FINAL_W: d_final_w,
        FINAL_B: d_final_b,
        T_BIAS_ONE: placed(jnp.sum(d_t_pre * pick.astype(f32)[:, None], 0), part, D),
        T_BIAS_TWO: d_temb_part
        + placed(jnp.sum(d_temb_local * pick.astype(f32)[:, None], 0), part, D),
        T_BIAS_MOD: d_mod_part,
        C_BIAS_ONE: placed(d_c_bias_one, part, D),
        C_BIAS_TWO: d_c_bias_two,
        ATTN_BIAS: jnp.stack(
            [
                side_sums(bias0, 0, 2 * SPAN, sums0[3]),
                side_sums(bias4, 0, 2 * SPAN, sums4[3]),
                side_sums(bias1, 0, 416 + SPAN, sums1[0]),
            ]
        ),
        FFN_BIAS_ONE: jnp.stack([bias2, bias5]),
        FFN_BIAS_TWO: jnp.stack([sums2[3], sums5[3]]),
        TABLES: jnp.stack([d_mods0, d_mods1]),
        FINAL_TABLE: jnp.stack([d_final_shift, d_final_scale]),
    }
    vector_grad = jnp.concatenate(
        [vector_grads[label].reshape(-1) for label, extent in vector_parts()]
    )
    g_attn = jnp.stack([g_space[0], g_time[0], g_cross[0]])
    g_attn = g_attn.reshape(3, BLOCK, 4, 4, HD).swapaxes(2, 3).reshape(3, BLOCK, D)
    g_ffn = jnp.stack([g_ffn0, g_ffn1])
    matrix_squares = jnp.sum(g_attn * g_attn) + jnp.sum(g_ffn * g_ffn) + jnp.sum(g_embed * g_embed)
    length = vector_grad.shape[0]
    spare = -(length + 2) % (8 * 8 * 128)
    totals = jnp.concatenate([vector_grad, matrix_squares[None], loss_part[None], jnp.zeros((spare,), f32)])
    totals = whole_sum(totals.reshape(8, -1, 128), 15).reshape(-1)
    g_vector = totals[:length]
    loss_total = totals[length + 1]
    squares = totals[length] + jnp.sum(g_vector * g_vector)
    grad_norm = jnp.sqrt(squares)
    factor = CLIP_NORM / (grad_norm + 1e-06)
    new_attn = adam_update(
        attn_mats, attn_first, attn_second, attn_ema, g_attn * factor, LEARN_RATE
    )
    new_ffn = adam_update(ffn_mats, ffn_first, ffn_second, ffn_ema, g_ffn * factor, LEARN_RATE)
    new_embed = adam_update(
        embed_mats, embed_first, embed_second, embed_ema, g_embed * factor, LEARN_RATE
    )
    new_vector = adam_update(
        vectors, vector_first, vector_second, vector_ema, g_vector * factor, VECTOR_RATE
    )
    return (loss_total, count, grad_norm) + tuple(
        group_new[kind]
        for kind in range(4)
        for group_new in (new_attn, new_ffn, new_embed, new_vector)
    )


def solution(mesh):
    fits = dict(mesh.shape) == {DP: CLIPS, MP: FR}
    program = per_device_chips if fits else per_device
    return jax.shard_map(
        program,
        mesh=mesh,
        in_specs=(
            P(DP, MP, None),
            P(DP, MP, None),
            P(DP, None, None),
            P(),
            P(),
            P(),
            P(),
            P(None, DP, MP),
            P(None, None, DP, MP),
            P(DP, MP),
            P(),
            P(None, DP, MP),
            P(None, None, DP, MP),
            P(DP, MP),
            P(),
            P(None, DP, MP),
            P(None, None, DP, MP),
            P(DP, MP),
            P(),
            P(None, DP, MP),
            P(None, None, DP, MP),
            P(DP, MP),
            P(),
        ),
        out_specs=(
            P(),
            P(),
            P(),
            P(None, DP, MP),
            P(None, None, DP, MP),
            P(DP, MP),
            P(),
            P(None, DP, MP),
            P(None, None, DP, MP),
            P(DP, MP),
            P(),
            P(None, DP, MP),
            P(None, None, DP, MP),
            P(DP, MP),
            P(),
            P(None, DP, MP),
            P(None, None, DP, MP),
            P(DP, MP),
            P(),
        ),
        check_vma=False,
    )
```

```python
import functools
import math

import jax
import jax.numpy as jnp
from jax import lax
from jax.experimental import pallas as pl
from jax.experimental.pallas import tpu as pltpu
from jax.sharding import PartitionSpec as P

D = 1152
HEADS = 16
HD = 72
FF = 4608
TFREQ = 256
TXT = 4096
CIN = 16
COUT = 32
CAP = 120
FR = 4
PM = 448
STEP = 5
DP, MP = "dp", "mp"
AT_SPACE = 0
AT_TIME = 1
AT_CROSS = 2
AT_ATTN = 3
AT_FFN = 4
AT_PARTS = 5
AT_PART = 6
AT_CONTEXT = 7
AT_KEEP = 8
AT_INPUT = 9
AT_GATHERED = 10
AT_QUERY = 11
AT_KEY_ROWS = 12
AT_VALUE_ROWS = 13
AT_LOGSUM = 14
AT_MIXED = 15
AT_BRANCH = 16
AT_PRE = 17
AT_HIDDEN = 18
PATCH_W = 0
PATCH_B = 1
FINAL_W = 2
FINAL_B = 3
T_BIAS_ONE = 4
T_BIAS_TWO = 5
T_BIAS_MOD = 6
C_BIAS_ONE = 7
C_BIAS_TWO = 8
ATTN_BIAS = 9
FFN_BIAS_ONE = 10
FFN_BIAS_TWO = 11
TABLES = 12
FINAL_TABLE = 13


EPS_NORM = 1e-06
LEARN_RATE = 0.03
VECTOR_RATE = 0.15
BETA_FIRST = 0.5
BETA_SECOND = 0.5
ADAM_EPSILON = 1e-08
WEIGHT_DECAY = 0.01
EMA_DECAY = 0.9
CLIP_NORM = 0.02
NEG_LARGE = -1e30
CONTRACT_ROWS = (((0,), (0,)), ((), ()))
CONTRACT_LAST = (((1,), (1,)), ((), ()))


def vector_parts():
    return [
        (PATCH_W, (CIN, D)),
        (PATCH_B, (D,)),
        (FINAL_W, (COUT, D)),
        (FINAL_B, (COUT,)),
        (T_BIAS_ONE, (D,)),
        (T_BIAS_TWO, (D,)),
        (T_BIAS_MOD, (6 * D,)),
        (C_BIAS_ONE, (D,)),
        (C_BIAS_TWO, (D,)),
        (ATTN_BIAS, (3, 3, D)),
        (FFN_BIAS_ONE, (2, FF)),
        (FFN_BIAS_TWO, (2, D)),
        (TABLES, (2, 6, D)),
        (FINAL_TABLE, (2, D)),
    ]


def unpack(flat):
    result = {}
    offset = 0
    for label, extent in vector_parts():
        length = math.prod(extent)
        result[label] = flat[offset : offset + length].reshape(extent)
        offset += length
    return result


def waves(position, width):
    half = width // 2
    freqs = jnp.exp(-math.log(10000.0) * jnp.arange(half, dtype=jnp.float32) / half)
    angles = position[..., None] * freqs
    return jnp.concatenate([jnp.sin(angles), jnp.cos(angles)], -1)


def roster():
    betas = 0.0001 + (0.02 - 0.0001) * jnp.arange(1000, dtype=jnp.float32) / 999.0
    return (betas, jnp.exp(jnp.cumsum(jnp.log1p(-betas))))


def modulate(x, shift_vec, scale_vec):
    centered = x - jnp.mean(x, -1, keepdims=True)
    normed = centered * lax.rsqrt(jnp.mean(centered * centered, -1, keepdims=True) + EPS_NORM)
    return normed * (1.0 + scale_vec) + shift_vec


def gelu_tanh(values):
    return jax.nn.gelu(values, approximate=True)


def token_losses(output, frozen, latent, noise_part, extra):
    noisy, alpha_bar, alpha_prev, beta_now = extra
    eps = output[:, :CIN]
    var_raw = output[:, CIN:]
    mse = jnp.mean((eps - noise_part) ** 2, -1)
    post_var = beta_now * (1.0 - alpha_prev) / (1.0 - alpha_bar)
    log_post = jnp.log(post_var)
    frac = (var_raw + 1.0) / 2.0
    log_var = frac * jnp.log(beta_now) + (1.0 - frac) * log_post
    coef_start = beta_now * jnp.sqrt(alpha_prev) / (1.0 - alpha_bar)
    coef_now = (1.0 - alpha_prev) * jnp.sqrt(1.0 - beta_now) / (1.0 - alpha_bar)
    true_mean = coef_start * latent + coef_now * noisy
    guess = (noisy - jnp.sqrt(1.0 - alpha_bar) * frozen) / jnp.sqrt(alpha_bar)
    model_mean = coef_start * guess + coef_now * noisy
    kl_term = 0.5 * (
        -1.0
        + log_var
        - log_post
        + jnp.exp(log_post - log_var)
        + (true_mean - model_mean) ** 2 * jnp.exp(-log_var)
    )
    return mse + jnp.mean(kl_term, -1) / math.log(2.0)


def attention_forms(kind):
    if kind == AT_SPACE:
        return ("fqhe,fkhe->fhqk", "fhqk,fkhe->fqhe", "fhqk,fqhe->fkhe")
    if kind == AT_TIME:
        return ("qphe,kphe->phqk", "phqk,kphe->qphe", "phqk,qphe->kphe")
    return ("qhe,khe->hqk", "hqk,khe->qhe", "hqk,qhe->khe")


def own_slice(vector, part, width):
    return lax.dynamic_slice_in_dim(vector, part * width, width, 0)


def placed(piece, part, full):
    return lax.dynamic_update_slice_in_dim(
        jnp.zeros((full,), jnp.float32), piece, part * piece.shape[0], 0
    )


def project_in(shard_rows, weight):
    piece = lax.all_gather(shard_rows, MP, axis=0, tiled=True)
    product = jnp.dot(piece, weight, preferred_element_type=jnp.float32)
    return (product, piece)


def project_out(full_rows, weight_t):
    return lax.psum_scatter(
        lax.dot_general(
            full_rows, weight_t, CONTRACT_LAST, preferred_element_type=jnp.float32
        ).astype(jnp.bfloat16),
        MP,
        scatter_dimension=0,
        tiled=True,
    ).astype(jnp.float32)


def back_out(grad_rows, full_rows, weight_t):
    piece = lax.all_gather(grad_rows, MP, axis=0, tiled=True)
    product = jnp.dot(piece, weight_t, preferred_element_type=jnp.float32)
    d_weight = lax.dot_general(piece, full_rows, CONTRACT_ROWS, preferred_element_type=jnp.float32)
    return (product, d_weight)


def back_in(d_full, weight):
    return lax.psum_scatter(
        lax.dot_general(d_full, weight, CONTRACT_LAST, preferred_element_type=jnp.float32).astype(
            jnp.bfloat16
        ),
        MP,
        scatter_dimension=0,
        tiled=True,
    ).astype(jnp.float32)


def attend_forward(query, key_rows, value_rows, keep, forms):
    scores = jnp.einsum(forms[0], query, key_rows, preferred_element_type=jnp.float32) * HD ** (
        -0.5
    )
    scores = jnp.where(keep, scores, NEG_LARGE)
    peak = jnp.max(scores, -1, keepdims=True)
    expd = jnp.exp(scores - peak)
    total = jnp.sum(expd, -1, keepdims=True)
    probs = (expd / total).astype(jnp.bfloat16)
    mixed = jnp.einsum(forms[1], probs, value_rows, preferred_element_type=jnp.float32)
    return (mixed, peak + jnp.log(total))


def attend_backward(query, key_rows, value_rows, keep, forms, logsum, d_mixed):
    scores = jnp.einsum(forms[0], query, key_rows, preferred_element_type=jnp.float32) * HD ** (
        -0.5
    )
    scores = jnp.where(keep, scores, NEG_LARGE)
    probs_full = jnp.exp(scores - logsum)
    probs = probs_full.astype(jnp.bfloat16)
    d_value = jnp.einsum(forms[2], probs, d_mixed, preferred_element_type=jnp.float32)
    d_probs = jnp.einsum(forms[0], d_mixed, value_rows, preferred_element_type=jnp.float32)
    offset = jnp.sum(d_probs * probs_full, -1, keepdims=True)
    d_scores = (probs_full * (d_probs - offset) * HD ** (-0.5)).astype(jnp.bfloat16)
    d_query = jnp.einsum(forms[1], d_scores, key_rows, preferred_element_type=jnp.float32)
    d_key = jnp.einsum(forms[2], d_scores, query, preferred_element_type=jnp.float32)
    return (d_query, d_key, d_value)


def attention_forward(x, index, mods, kind, setup):
    weight = setup[AT_ATTN][index]
    heads = weight.shape[1]
    width_local = heads * HD
    biases = setup[AT_PARTS][ATTN_BIAS][index]
    part = setup[AT_PART]
    forms = attention_forms(kind)
    query_bias = own_slice(biases[0], part, width_local).reshape(heads, HD)
    value_bias = own_slice(biases[1], part, width_local).reshape(heads, HD)
    if kind == AT_CROSS:
        projected, gathered = project_in(
            x.astype(jnp.bfloat16), weight[:, :, 0, :].reshape(D, width_local)
        )
        query = projected.reshape(-1, heads, HD) + query_bias
        context = setup[AT_CONTEXT]
        key_rows = jnp.einsum(
            "cd,dhe->che", context, weight[:, :, 1, :], preferred_element_type=jnp.float32
        )
        value_rows = (
            jnp.einsum(
                "cd,dhe->che", context, weight[:, :, 2, :], preferred_element_type=jnp.float32
            )
            + value_bias
        )
    else:
        source = modulate(x, mods[0], mods[1])
        projected, gathered = project_in(
            source.astype(jnp.bfloat16), weight[:, :, :3, :].reshape(D, 3 * width_local)
        )
        projected = projected.reshape(FR, PM, heads, 3, HD)
        query = projected[:, :, :, 0] + query_bias
        key_rows = projected[:, :, :, 1]
        value_rows = projected[:, :, :, 2] + value_bias
    query = query.astype(jnp.bfloat16)
    key_rows = key_rows.astype(jnp.bfloat16)
    value_rows = value_rows.astype(jnp.bfloat16)
    mixed, logsum = attend_forward(query, key_rows, value_rows, setup[AT_KEEP][kind], forms)
    mixed = mixed.reshape(-1, width_local).astype(jnp.bfloat16)
    branch = project_out(mixed, weight[:, :, 3, :].reshape(D, width_local)) + biases[2]
    saved = {
        AT_INPUT: x,
        AT_GATHERED: gathered,
        AT_QUERY: query,
        AT_KEY_ROWS: key_rows,
        AT_VALUE_ROWS: value_rows,
        AT_LOGSUM: logsum,
        AT_MIXED: mixed,
        AT_BRANCH: branch,
    }
    if kind == AT_CROSS:
        return (x + branch, saved)
    return (x + mods[2] * branch, saved)


def attention_backward(grad_x, index, mods, kind, saved, setup):
    weight = setup[AT_ATTN][index]
    heads = weight.shape[1]
    width_local = heads * HD
    part = setup[AT_PART]
    forms = attention_forms(kind)
    query = saved[AT_QUERY]
    if kind == AT_CROSS:
        gate_vec = 1.0
        d_gate = None
    else:
        gate_vec = mods[2]
        d_gate = jnp.sum(grad_x * saved[AT_BRANCH], 0)
    d_branch = (gate_vec * grad_x).astype(jnp.bfloat16)
    d_out_bias = jnp.sum(d_branch.astype(jnp.float32), 0)
    d_mixed, d_out_weight = back_out(
        d_branch, saved[AT_MIXED], weight[:, :, 3, :].reshape(D, width_local)
    )
    d_mixed = d_mixed.astype(jnp.bfloat16).reshape(query.shape)
    d_query, d_key, d_value = attend_backward(
        query,
        saved[AT_KEY_ROWS],
        saved[AT_VALUE_ROWS],
        setup[AT_KEEP][kind],
        forms,
        saved[AT_LOGSUM],
        d_mixed,
    )
    d_query = d_query.reshape(-1, heads, HD).astype(jnp.bfloat16)
    d_key = d_key.reshape(-1, heads, HD).astype(jnp.bfloat16)
    d_value = d_value.reshape(-1, heads, HD).astype(jnp.bfloat16)
    d_query_bias = jnp.sum(d_query.astype(jnp.float32), 0).reshape(-1)
    d_value_bias = jnp.sum(d_value.astype(jnp.float32), 0).reshape(-1)
    if kind == AT_CROSS:
        context = setup[AT_CONTEXT]
        d_query_weight = lax.dot_general(
            saved[AT_GATHERED],
            d_query.reshape(-1, width_local),
            CONTRACT_ROWS,
            preferred_element_type=jnp.float32,
        ).reshape(D, heads, 1, HD)
        d_key_weight = jnp.einsum("cd,che->dhe", context, d_key, preferred_element_type=jnp.float32)
        d_value_weight = jnp.einsum(
            "cd,che->dhe", context, d_value, preferred_element_type=jnp.float32
        )
        d_in = jnp.concatenate(
            [d_query_weight, d_key_weight[:, :, None], d_value_weight[:, :, None]], 2
        )
        d_context = jnp.einsum(
            "che,dhe->cd", d_key, weight[:, :, 1, :], preferred_element_type=jnp.float32
        ) + jnp.einsum(
            "che,dhe->cd", d_value, weight[:, :, 2, :], preferred_element_type=jnp.float32
        )
        grad_x = grad_x + back_in(
            d_query.reshape(-1, width_local), weight[:, :, 0, :].reshape(D, width_local)
        )
        mod_grads = None
    else:
        d_proj = jnp.stack([d_query, d_key, d_value], 2).reshape(-1, 3 * width_local)
        d_in = lax.dot_general(
            saved[AT_GATHERED], d_proj, CONTRACT_ROWS, preferred_element_type=jnp.float32
        ).reshape(D, heads, 3, HD)
        d_source = back_in(d_proj, weight[:, :, :3, :].reshape(D, 3 * width_local))
        unused, norm_pull = jax.vjp(modulate, saved[AT_INPUT], mods[0], mods[1])
        d_input, d_shift, d_scale = norm_pull(d_source)
        grad_x = grad_x + d_input
        mod_grads = (d_shift, d_scale, d_gate)
        d_context = None
    d_weight = jnp.concatenate([d_in, d_out_weight.reshape(D, heads, 1, HD)], 2)
    d_bias = jnp.stack([placed(d_query_bias, part, D), placed(d_value_bias, part, D), d_out_bias])
    return (grad_x, d_weight, d_bias, mod_grads, d_context)


def ffn_forward(x, index, mods, setup):
    weight_in = setup[AT_FFN][index, 0]
    weight_out = setup[AT_FFN][index, 1]
    source = modulate(x, mods[3], mods[4])
    pre, gathered = project_in(source.astype(jnp.bfloat16), weight_in)
    pre = pre + own_slice(setup[AT_PARTS][FFN_BIAS_ONE][index], setup[AT_PART], weight_in.shape[1])
    hidden = gelu_tanh(pre).astype(jnp.bfloat16)
    branch = project_out(hidden, weight_out) + setup[AT_PARTS][FFN_BIAS_TWO][index]
    saved = {AT_INPUT: x, AT_GATHERED: gathered, AT_PRE: pre, AT_HIDDEN: hidden, AT_BRANCH: branch}
    return (x + mods[5] * branch, saved)


def ffn_backward(grad_x, index, mods, saved, setup):
    weight_in = setup[AT_FFN][index, 0]
    weight_out = setup[AT_FFN][index, 1]
    d_gate = jnp.sum(grad_x * saved[AT_BRANCH], 0)
    d_branch = (mods[5] * grad_x).astype(jnp.bfloat16)
    d_bias_two = jnp.sum(d_branch.astype(jnp.float32), 0)
    d_hidden, d_weight_out = back_out(d_branch, saved[AT_HIDDEN], weight_out)
    unused, gelu_pull = jax.vjp(gelu_tanh, saved[AT_PRE])
    d_pre = gelu_pull(d_hidden)[0].astype(jnp.bfloat16)
    d_bias_one = jnp.sum(d_pre.astype(jnp.float32), 0)
    d_weight_in = lax.dot_general(
        saved[AT_GATHERED], d_pre, CONTRACT_ROWS, preferred_element_type=jnp.float32
    )
    d_source = back_in(d_pre, weight_in)
    unused, norm_pull = jax.vjp(modulate, saved[AT_INPUT], mods[3], mods[4])
    d_input, d_shift, d_scale = norm_pull(d_source)
    biases = (placed(d_bias_one, setup[AT_PART], FF), d_bias_two)
    return (
        grad_x + d_input,
        jnp.stack([d_weight_in, d_weight_out]),
        biases,
        (d_shift, d_scale, d_gate),
    )


def block_forward(x, kind, mods, setup):
    index = 0 if kind == AT_SPACE else 1
    x, first = attention_forward(x, index, mods, kind, setup)
    second = None
    if kind == AT_SPACE:
        x, second = attention_forward(x, 2, mods, AT_CROSS, setup)
    x, third = ffn_forward(x, index, mods, setup)
    return (x, (first, second, third))


def block_backward(grad_x, kind, mods, saved, setup):
    index = 0 if kind == AT_SPACE else 1
    first, second, third = saved
    grad_x, d_ffn, d_ffn_bias, ffn_mods = ffn_backward(grad_x, index, mods, third, setup)
    cross_part = None
    if kind == AT_SPACE:
        grad_x, d_cross, d_cross_bias, unused, d_context = attention_backward(
            grad_x, 2, mods, AT_CROSS, second, setup
        )
        cross_part = (d_cross, d_cross_bias, d_context)
    grad_x, d_attn, d_attn_bias, attn_mods, unused = attention_backward(
        grad_x, index, mods, kind, first, setup
    )
    d_mods = jnp.stack(list(attn_mods) + list(ffn_mods))
    return (grad_x, (d_attn, d_attn_bias, d_ffn, d_ffn_bias, d_mods), cross_part)


def adam_update(weight, first, second, ema, grad, rate):
    first_new = BETA_FIRST * first + (1.0 - BETA_FIRST) * grad
    second_new = BETA_SECOND * second + (1.0 - BETA_SECOND) * grad * grad
    corr_one = 1.0 - BETA_FIRST**STEP
    corr_two = 1.0 - BETA_SECOND**STEP
    weight_new = weight - rate * (
        first_new / corr_one / (jnp.sqrt(second_new / corr_two) + ADAM_EPSILON)
        + WEIGHT_DECAY * weight
    )
    return (first_new, second_new, weight_new, EMA_DECAY * ema + (1.0 - EMA_DECAY) * weight_new)


def per_device(
    latents,
    noise,
    caption,
    caption_lens,
    timesteps,
    grid_hw,
    frame_counts,
    attn_mats,
    ffn_mats,
    embed_mats,
    vectors,
    attn_first,
    ffn_first,
    embed_first,
    vector_first,
    attn_second,
    ffn_second,
    embed_second,
    vector_second,
    attn_ema,
    ffn_ema,
    embed_ema,
    vector_ema,
):
    group = lax.axis_index(DP)
    part = lax.axis_index(MP)
    mp_size = lax.axis_size(MP)
    rows = latents.shape[1]
    heads = HEADS // mp_size
    width_local = D // mp_size
    attn_all, ffn_all, embed_all = (
        lax.all_gather(attn_mats.astype(jnp.bfloat16), DP, axis=1, tiled=True),
        lax.all_gather(ffn_mats.astype(jnp.bfloat16), DP, axis=2, tiled=True),
        lax.all_gather(embed_mats.astype(jnp.bfloat16), DP, axis=0, tiled=True),
    )
    parts = unpack(vectors)
    pick = jnp.arange(timesteps.shape[0], dtype=jnp.int32) == group

    def select(values):
        return jnp.sum(jnp.where(pick, values, 0))

    tstep = select(timesteps)
    cap_len = select(caption_lens)
    height = select(grid_hw[:, 0])
    width_grid = select(grid_hw[:, 1])
    frames = select(frame_counts)
    count = jnp.sum(frame_counts * grid_hw[:, 0] * grid_hw[:, 1]).astype(jnp.float32)
    betas, cumul = roster()
    step_ids = jnp.arange(1000, dtype=jnp.int32)
    alpha_bar = jnp.sum(jnp.where(step_ids == tstep, cumul, 0.0))
    alpha_prev = jnp.sum(jnp.where(step_ids == tstep - 1, cumul, 0.0))
    beta_now = jnp.sum(jnp.where(step_ids == tstep, betas, 0.0))
    t_one = embed_all[:TFREQ]
    c_one = embed_all[TFREQ : TFREQ + TXT]
    t_two = embed_all[TFREQ + TXT : TFREQ + TXT + D]
    c_two = embed_all[TFREQ + TXT + D : TFREQ + TXT + 2 * D]
    t_mod = embed_all[TFREQ + TXT + 2 * D :]
    freq = waves(tstep.astype(jnp.float32), TFREQ).astype(jnp.bfloat16)
    t_pre = jnp.dot(freq, t_one, preferred_element_type=jnp.float32) + own_slice(
        parts[T_BIAS_ONE], part, width_local
    )
    t_hidden = jax.nn.silu(t_pre).astype(jnp.bfloat16)
    t_part = jnp.dot(t_two, t_hidden, preferred_element_type=jnp.float32)
    caption_rows = caption[0]
    c_pre = jnp.dot(caption_rows, c_one, preferred_element_type=jnp.float32) + own_slice(
        parts[C_BIAS_ONE], part, width_local
    )
    c_hidden = gelu_tanh(c_pre).astype(jnp.bfloat16)
    c_part = lax.dot_general(c_hidden, c_two, CONTRACT_LAST, preferred_element_type=jnp.float32)
    t_sum, c_sum = (
        lax.psum(t_part.astype(jnp.bfloat16), MP).astype(jnp.float32),
        lax.psum(c_part.astype(jnp.bfloat16), MP).astype(jnp.float32),
    )
    t_emb = t_sum + parts[T_BIAS_TWO]
    context = (c_sum + parts[C_BIAS_TWO]).astype(jnp.bfloat16)
    t_emb_local = own_slice(t_emb, part, width_local)
    silu_local = jax.nn.silu(t_emb_local).astype(jnp.bfloat16)
    t_mod_vec = (
        lax.psum(jnp.dot(t_mod, silu_local, preferred_element_type=jnp.float32), MP)
        + parts[T_BIAS_MOD]
    )
    token_ids = part * rows + jnp.arange(rows, dtype=jnp.int32)
    frame_slot = token_ids // PM
    patch_slot = token_ids % PM
    area = height * width_grid
    shifted = patch_slot - (PM - area)
    valid = (frame_slot >= FR - frames) & (patch_slot >= PM - area)
    setup = {
        AT_ATTN: attn_all.reshape(3, D, heads, 4, HD),
        AT_FFN: ffn_all,
        AT_PARTS: parts,
        AT_PART: part,
        AT_CONTEXT: context,
        AT_KEEP: {
            AT_SPACE: (jnp.arange(PM, dtype=jnp.int32) >= PM - area).reshape(1, 1, 1, PM),
            AT_TIME: (jnp.arange(FR, dtype=jnp.int32) >= FR - frames).reshape(1, 1, 1, FR),
            AT_CROSS: (jnp.arange(CAP, dtype=jnp.int32) < cap_len).reshape(1, 1, CAP),
        },
    }
    noisy = jnp.sqrt(alpha_bar) * latents[0] + jnp.sqrt(1.0 - alpha_bar) * noise[0]
    noisy_low = noisy.astype(jnp.bfloat16)
    position = jnp.concatenate(
        [
            waves((shifted // width_grid).astype(jnp.float32), D // 2),
            waves((shifted % width_grid).astype(jnp.float32), D // 2),
        ],
        -1,
    )
    x = jnp.dot(
        noisy_low, parts[PATCH_W].astype(jnp.bfloat16), preferred_element_type=jnp.float32
    )
    x = x + parts[PATCH_B] + position
    tables = parts[TABLES] + t_mod_vec.reshape(1, 6, D)
    x, saved_space = block_forward(x, AT_SPACE, tables[0], setup)
    x = x + waves((frame_slot - (FR - frames)).astype(jnp.float32), D)
    x, saved_time = block_forward(x, AT_TIME, tables[1], setup)
    final_mods = parts[FINAL_TABLE] + t_emb
    final_source = modulate(x, final_mods[0], final_mods[1]).astype(jnp.bfloat16)
    final_low = parts[FINAL_W].astype(jnp.bfloat16)
    output = (
        lax.dot_general(final_source, final_low, CONTRACT_LAST, preferred_element_type=jnp.float32)
        + parts[FINAL_B]
    )
    frozen = output[:, :CIN]

    def shard_loss(values):
        losses = token_losses(
            values, frozen, latents[0], noise[0], (noisy, alpha_bar, alpha_prev, beta_now)
        )
        return jnp.sum(jnp.where(valid, losses, 0.0))

    loss_part, loss_pull = jax.vjp(shard_loss, output)
    loss_total = lax.psum(loss_part, (DP, MP))
    d_output = loss_pull(1.0 / count)[0].astype(jnp.bfloat16)
    d_final_w = lax.dot_general(
        d_output, final_source, CONTRACT_ROWS, preferred_element_type=jnp.float32
    )
    d_final_b = jnp.sum(d_output.astype(jnp.float32), 0)
    d_final_source = jnp.dot(d_output, final_low, preferred_element_type=jnp.float32)
    unused, final_pull = jax.vjp(modulate, x, final_mods[0], final_mods[1])
    grad_x, d_final_shift, d_final_scale = final_pull(d_final_source)
    grad_x, time_grads, unused = block_backward(grad_x, AT_TIME, tables[1], saved_time, setup)
    grad_x, space_grads, cross_grads = block_backward(
        grad_x, AT_SPACE, tables[0], saved_space, setup
    )
    d_patch = grad_x.astype(jnp.bfloat16)
    d_patch_b = jnp.sum(d_patch.astype(jnp.float32), 0)
    d_patch_w = lax.dot_general(
        noisy_low, d_patch, CONTRACT_ROWS, preferred_element_type=jnp.float32
    )
    d_mod_part = space_grads[4].reshape(-1) + time_grads[4].reshape(-1)
    d_temb_part = d_final_shift + d_final_scale
    d_mod_vec, d_temb_sum, d_context = (
        lax.psum(d_mod_part.astype(jnp.bfloat16), MP).astype(jnp.float32),
        lax.psum(d_temb_part.astype(jnp.bfloat16), MP).astype(jnp.float32),
        lax.psum(cross_grads[2].astype(jnp.bfloat16), MP).astype(jnp.float32),
    )
    d_t_mod = jnp.outer(d_mod_vec, silu_local.astype(jnp.float32))
    d_silu_local = jnp.dot(d_mod_vec, t_mod, preferred_element_type=jnp.float32)
    unused, silu_pull = jax.vjp(jax.nn.silu, t_emb_local)
    d_temb_local = silu_pull(d_silu_local)[0]
    d_temb = d_temb_sum + lax.all_gather(d_temb_local, MP, axis=0, tiled=True)
    d_t_two = jnp.outer(d_temb, t_hidden.astype(jnp.float32))
    d_t_hidden = jnp.dot(d_temb, t_two, preferred_element_type=jnp.float32)
    unused, pre_pull = jax.vjp(jax.nn.silu, t_pre)
    d_t_pre = pre_pull(d_t_hidden)[0]
    d_t_one = jnp.outer(freq.astype(jnp.float32), d_t_pre)
    d_context = d_context.astype(jnp.bfloat16)
    d_c_bias_two = jnp.sum(d_context.astype(jnp.float32), 0) * (part == 0).astype(jnp.float32)
    d_c_two = lax.dot_general(
        d_context, c_hidden, CONTRACT_ROWS, preferred_element_type=jnp.float32
    )
    d_c_hidden = jnp.dot(d_context, c_two, preferred_element_type=jnp.float32)
    unused, cap_pull = jax.vjp(gelu_tanh, c_pre)
    d_c_pre = cap_pull(d_c_hidden)[0].astype(jnp.bfloat16)
    d_c_one = lax.dot_general(
        caption_rows, d_c_pre, CONTRACT_ROWS, preferred_element_type=jnp.float32
    )
    d_c_bias_one = jnp.sum(d_c_pre.astype(jnp.float32), 0)
    d_attn = jnp.stack([space_grads[0], time_grads[0], cross_grads[0]]).reshape(
        3, D, heads * 4 * HD
    )
    d_ffn = jnp.stack([space_grads[2], time_grads[2]])
    d_embed = jnp.concatenate([d_t_one, d_c_one, d_t_two, d_c_two, d_t_mod], 0)
    vector_grads = {
        PATCH_W: d_patch_w,
        PATCH_B: d_patch_b,
        FINAL_W: d_final_w,
        FINAL_B: d_final_b,
        T_BIAS_ONE: placed(d_t_pre, part, D),
        T_BIAS_TWO: d_temb_part + placed(d_temb_local, part, D),
        T_BIAS_MOD: d_mod_part,
        C_BIAS_ONE: placed(d_c_bias_one, part, D),
        C_BIAS_TWO: d_c_bias_two,
        ATTN_BIAS: jnp.stack([space_grads[1], time_grads[1], cross_grads[1]]),
        FFN_BIAS_ONE: jnp.stack([space_grads[3][0], time_grads[3][0]]),
        FFN_BIAS_TWO: jnp.stack([space_grads[3][1], time_grads[3][1]]),
        TABLES: jnp.stack([space_grads[4], time_grads[4]]),
        FINAL_TABLE: jnp.stack([d_final_shift, d_final_scale]),
    }
    vector_grad = jnp.concatenate(
        [vector_grads[label].reshape(-1) for label, extent in vector_parts()]
    )
    g_attn, g_ffn, g_embed = (
        lax.psum_scatter(d_attn.astype(jnp.bfloat16), DP, scatter_dimension=1, tiled=True).astype(
            jnp.float32
        ),
        lax.psum_scatter(d_ffn.astype(jnp.bfloat16), DP, scatter_dimension=2, tiled=True).astype(
            jnp.float32
        ),
        lax.psum_scatter(
            d_embed.astype(jnp.bfloat16), DP, scatter_dimension=0, tiled=True
        ).astype(jnp.float32),
    )
    g_vector = lax.psum(vector_grad, (DP, MP))
    matrix_squares = jnp.sum(g_attn * g_attn) + jnp.sum(g_ffn * g_ffn) + jnp.sum(g_embed * g_embed)
    squares = lax.psum(matrix_squares, (DP, MP)) + jnp.sum(g_vector * g_vector)
    grad_norm = jnp.sqrt(squares)
    factor = CLIP_NORM / (grad_norm + 1e-06)
    new_attn = adam_update(
        attn_mats, attn_first, attn_second, attn_ema, g_attn * factor, LEARN_RATE
    )
    new_ffn = adam_update(ffn_mats, ffn_first, ffn_second, ffn_ema, g_ffn * factor, LEARN_RATE)
    new_embed = adam_update(
        embed_mats, embed_first, embed_second, embed_ema, g_embed * factor, LEARN_RATE
    )
    new_vector = adam_update(
        vectors, vector_first, vector_second, vector_ema, g_vector * factor, VECTOR_RATE
    )
    return (
        loss_total,
        count,
        grad_norm,
        new_attn[0],
        new_ffn[0],
        new_embed[0],
        new_vector[0],
        new_attn[1],
        new_ffn[1],
        new_embed[1],
        new_vector[1],
        new_attn[2],
        new_ffn[2],
        new_embed[2],
        new_vector[2],
        new_attn[3],
        new_ffn[3],
        new_embed[3],
        new_vector[3],
    )


SPAN = 4 * HD
EMB_ALL = TFREQ + TXT + 8 * D
EMB_LOCAL = EMB_ALL // 8
MESH = pl.DeviceIdType.MESH
BLOCK = 144
BIG = 58 * 2**20
PIECES = {1: 2, 2: 2}


class Chips:
    def __init__(self):
        dp = lax.axis_index(DP)
        mp = lax.axis_index(MP)
        self.z, self.x = dp // 2, dp % 2
        self.y, self.c = mp // 2, mp % 2

    def z_at(self, j):
        z = self.z
        return (z, z + 1 - 2 * (z % 2), z + 2 - 4 * (z // 2), 3 - z)[j]

    def dp_at(self, jz, jx):
        return self.z_at(jz) * 2 + (1 - self.x if jx else self.x)

    def mp_at(self, jy, jc):
        return (1 - self.y if jy else self.y) * 2 + (1 - self.c if jc else self.c)

    def peer_x(self):
        return {DP: self.dp_at(0, 1)}

    def peer_y(self):
        return {MP: self.mp_at(1, 0)}

    def peer_core(self):
        return {MP: self.mp_at(0, 1)}

    def peer_z(self, j):
        return {DP: self.dp_at(j, 0)}

    def greet(self):
        barrier = pltpu.get_barrier_semaphore()
        peers = [self.peer_x(), self.peer_y(), self.peer_core()]
        peers += [self.peer_z(j) for j in (1, 2, 3)]
        for peer in peers:
            pl.semaphore_signal(barrier, inc=1, device_id=peer, device_id_type=MESH)
        pl.semaphore_wait(barrier, len(peers))


class Work:
    def __init__(self, chips, send, recv):
        self.chips, self.send, self.recv = chips, send, recv
        self.started = []

    def start(self, src, dst, slot, peer):
        def copy():
            return pltpu.make_async_remote_copy(
                src_ref=src(),
                dst_ref=dst(),
                send_sem=self.send.at[slot],
                recv_sem=self.recv.at[slot],
                device_id=peer(),
                device_id_type=MESH,
            )

        copy().start()
        self.started.append(copy)

    def arrived(self, dst, slot):
        pltpu.make_async_remote_copy(
            src_ref=dst,
            dst_ref=dst,
            send_sem=self.send.at[slot],
            recv_sem=self.recv.at[slot],
            device_id=self.chips.peer_core(),
            device_id_type=MESH,
        ).wait_recv()

    def finish(self):
        for copy in self.started:
            copy().wait_send()


class Gather(Work):
    def __init__(self, chips, shard, full, row, size, send, recv, local):
        super().__init__(chips, send, recv)
        self.source, self.full, self.local = shard, full, local
        self.rows = pl.ds(row, size)

    def shard(self):
        return self.source.at[:, self.rows]

    def block(self, jy, jz, jx, jc=0):
        chips = self.chips
        return self.full.at[:, chips.mp_at(jy, jc), chips.dp_at(jz, jx), self.rows]

    def arrive(self, jy, jz, jx, jc=0):
        self.arrived(self.block(jy, jz, jx, jc), jc * 16 + jy * 8 + jz * 2 + jx)

    def pass_on(self, place, slot, peer):
        self.start(lambda: self.block(*place), lambda: self.block(*place), slot, peer)

    def core(self, jy, jz, jx):
        self.pass_on((jy, jz, jx), 16 + jy * 8 + jz * 2 + jx, self.chips.peer_core)

    def own(self):
        return pltpu.make_async_copy(self.shard(), self.block(0, 0, 0), self.local)

    def begin(self):
        chips = self.chips
        shard, block = self.shard, (lambda: self.block(0, 0, 0))
        self.start(shard, block, 1, chips.peer_x)
        self.start(shard, block, 8, chips.peer_y)
        for j in (1, 2, 3):
            self.start(shard, block, 2 * j, functools.partial(chips.peer_z, j))
        self.start(shard, block, 16, chips.peer_core)
        self.own().start()

    def second(self, jz):
        self.arrive(0, jz, 0)
        self.pass_on((0, jz, 0), jz * 2 + 1, self.chips.peer_x)
        self.pass_on((0, jz, 0), jz * 2 + 8, self.chips.peer_y)
        self.core(0, jz, 0)

    def third(self, jz):
        place = (0, jz, 1) if jz < 2 else (1, jz, 0)
        self.arrive(*place)
        self.pass_on(place, 9 + jz * 2, self.chips.peer_y if jz < 2 else self.chips.peer_x)
        self.core(*place)

    def fourth(self, jz):
        place = (1, jz, 0) if jz < 2 else (0, jz, 1)
        self.arrive(*place)
        self.core(*place)

    def fifth(self, jz):
        self.arrive(1, jz, 1)
        self.core(1, jz, 1)

    def last(self):
        self.own().wait()
        for jy in range(2):
            for jz in range(4):
                for jx in range(2):
                    self.arrive(jy, jz, jx, 1)

    def steps(self):
        order = (0, 2, 1, 3)
        parts = [[self.begin]]
        parts.append([functools.partial(self.second, j) for j in (1, 2, 3)])
        parts.append([functools.partial(self.third, j) for j in order])
        parts.append([functools.partial(self.fourth, j) for j in order])
        parts.append([functools.partial(self.fifth, j) for j in order])
        parts.append([self.last])
        return parts


GATHER_SEMS = [
    pltpu.SemaphoreType.DMA((32,)),
    pltpu.SemaphoreType.DMA((32,)),
    pltpu.SemaphoreType.DMA,
]


class Ticks:
    def __init__(self, steps, spots):
        self.step = pl.program_id(0)
        total = 4 * spots
        self.table = [[] for unused in range(total)]
        count = len(steps)
        for i, step in enumerate(steps):
            at = 0 if i == 0 else total - 1 if i == count - 1 else 1 + (i - 1) * (total - 2) // (count - 2)
            self.table[at].append(step)
        self.spots = spots

    def __call__(self, spot):
        for turn in range(4):
            todo = self.table[turn * self.spots + spot]
            if todo:

                @pl.when(self.step == turn)
                def run(todo=todo):
                    for step in todo:
                        step()


def no_ticks(spot):
    return None


def woven(plans):
    order = [step for plan in plans for step in plan[0]]
    plans = [plan[1:] for plan in plans]
    deep = max(len(plan) for plan in plans)
    for turn in range(len(plans) + deep - 1):
        for i, plan in enumerate(plans):
            if 0 <= turn - i < len(plan):
                order += plan[turn - i]
    return order


ROWS = {1: [144], 2: [80, 64], 3: [48, 48, 48]}
GATHER_PIECES = {1: 3, 2: 3}


def gather_steps(chips, shard, full, sems):
    pieces = len(sems) // 3
    sizes = ROWS[pieces]
    works = [
        Gather(chips, shard, full, sum(sizes[:i]), sizes[i], *sems[3 * i : 3 * i + 3])
        for i in range(pieces)
    ]

    def finish():
        for work in works:
            work.finish()

    return woven([work.steps() for work in works]) + [finish]


def entered(chips, steps, begins, spots):
    def enter():
        chips.greet()
        for begin in steps[:begins]:
            begin()

    return Ticks([enter] + steps[begins:], spots)


def gather_ticks(refs, spots, unused):
    chips = Chips()
    return entered(chips, gather_steps(chips, refs[0], refs[1], refs[2:]), len(refs) // 3, spots)


def gather_kernel(shard, full, *sems):
    chips = Chips()
    chips.greet()
    for step in gather_steps(chips, shard, full, sems):
        step()


def gather_all(shard, ident):
    return pl.pallas_call(
        gather_kernel,
        out_shape=jax.ShapeDtypeStruct((shard.shape[0], 4, 8) + shard.shape[1:], shard.dtype),
        in_specs=[pl.BlockSpec(memory_space=pl.ANY)],
        out_specs=pl.BlockSpec(memory_space=pl.ANY),
        scratch_shapes=GATHER_SEMS * GATHER_PIECES[shard.shape[0]],
        compiler_params=pltpu.CompilerParams(collective_id=ident, has_side_effects=True),
    )(shard)


def sorted_columns(value):
    return jnp.concatenate(
        [value[:, (h * 4 + k) * HD : (h * 4 + k + 1) * HD] for k in range(4) for h in range(4)], 1
    )


def unsorted_columns(value):
    return jnp.concatenate(
        [value[:, (k * 4 + h) * HD : (k * 4 + h + 1) * HD] for h in range(4) for k in range(4)], 1
    )


def sort_kernel(mats, out):
    out[0] = sorted_columns(mats[0]).astype(jnp.bfloat16)


def sort_panels(mats):
    spec = pl.BlockSpec((1,) + mats.shape[1:], lambda i: (i, 0, 0))
    return pl.pallas_call(
        sort_kernel,
        grid=(3,),
        in_specs=[spec],
        out_specs=spec,
        out_shape=jax.ShapeDtypeStruct(mats.shape, jnp.bfloat16),
    )(mats)


class Scatter(Work):
    def __init__(self, chips, full, total, m, row, near, far, own, send, recv, load):
        super().__init__(chips, send, recv)
        self.sorted = full.shape[0] == 1
        self.full, self.total = full, total
        self.m, self.row, self.size = m, row, near.shape[1]
        self.near, self.far, self.own, self.load = near, far, own, load
        diagonal = [(1, jz, 1) for jz in (0, 2, 1, 3)]
        straight = [(1, jz, 0) if jz < 2 else (0, jz, 1) for jz in (0, 2, 1, 3)]
        bent = [(0, jz, 1) if jz < 2 else (1, jz, 0) for jz in (0, 2, 1, 3)]
        column = [(0, jz, 0) for jz in (2, 3, 1, 0)]
        self.order = diagonal + straight + bent + column
        self.turns = {jy * 8 + jz * 2 + jx: i for i, (jy, jz, jx) in enumerate(self.order)}

    def block(self, jy, jz, jx, jc):
        chips = self.chips
        return self.full.at[
            self.m, chips.mp_at(jy, jc), chips.dp_at(jz, jx), pl.ds(self.row, self.size)
        ]

    def fetch(self, turn):
        buffer = turn % self.own.shape[0]
        return pltpu.make_async_copy(
            self.block(*self.order[turn], 0), self.own.at[buffer], self.load.at[buffer]
        )

    def begin(self):
        for place in self.order:
            slot = place[0] * 8 + place[1] * 2 + place[2]
            self.start(
                functools.partial(self.block, *place, 1),
                functools.partial(lambda at: self.near.at[at], slot),
                slot,
                self.chips.peer_core,
            )
        for turn in range(self.own.shape[0]):
            self.fetch(turn).start()

    def add(self, slot, others):
        turn, near, own = self.turns[slot], self.near, self.own
        buffer = turn % own.shape[0]
        self.fetch(turn).wait()
        self.arrived(near.at[slot], slot)

        def rows(i, carry):
            at = pl.ds(pl.multiple_of(i * 16, 16), 16)
            value = near[slot, at].astype(jnp.float32) + own[buffer, at].astype(jnp.float32)
            for index in others:
                value += self.far[index, at].astype(jnp.float32)
            near[slot, at] = value.astype(jnp.bfloat16)
            return carry

        lax.fori_loop(0, self.size // 16, rows, 0)
        if turn + own.shape[0] < 16:
            self.fetch(turn + own.shape[0]).start()

    def move(self, slot, index, where, peer):
        self.start(lambda: self.near.at[slot], lambda: self.far.at[index], where, peer)

    def along_x(self, slot, jz):
        self.move(slot, 4 + jz, 20 + jz, self.chips.peer_x)

    def along_y(self, slot, jz):
        self.move(slot, 8 + jz, 24 + jz, self.chips.peer_y)

    def diagonal(self, jz):
        slot = 9 + jz * 2
        self.add(slot, [])
        self.move(slot, jz, 16 + jz, self.chips.peer_y if jz < 2 else self.chips.peer_x)

    def straight(self, jz):
        slot = jz * 2 + (8 if jz < 2 else 1)
        self.add(slot, [])
        (self.along_y if jz < 2 else self.along_x)(slot, jz)

    def bent(self, jz):
        slot = jz * 2 + (1 if jz < 2 else 8)
        self.arrived(self.far.at[jz], 16 + jz)
        self.add(slot, [jz])
        (self.along_x if jz < 2 else self.along_y)(slot, jz)

    def column(self, jz):
        self.arrived(self.far.at[4 + jz], 20 + jz)
        self.arrived(self.far.at[8 + jz], 24 + jz)
        if jz:
            self.add(jz * 2, [4 + jz, 8 + jz])
            self.move(jz * 2, 11 + jz, 27 + jz, functools.partial(self.chips.peer_z, jz))

    def last(self):
        turn, near, own, far = 15, self.near, self.own, self.far
        buffer = turn % own.shape[0]
        self.fetch(turn).wait()
        self.arrived(near.at[0], 0)
        for jz in (2, 3, 1):
            self.arrived(far.at[11 + jz], 27 + jz)

        def rows(i, carry):
            at = pl.ds(pl.multiple_of(i * 16, 16), 16)
            value = near[0, at].astype(jnp.float32) + own[buffer, at].astype(jnp.float32)
            for index in (4, 8, 12, 13, 14):
                value += far[index, at].astype(jnp.float32)
            if self.sorted:
                value = unsorted_columns(value)
            self.total[self.m, pl.ds(pl.multiple_of(self.row + i * 16, 16), 16)] = value
            return carry

        lax.fori_loop(0, self.size // 16, rows, 0)

    def steps(self):
        order = (0, 2, 1, 3)
        parts = [[self.begin]]
        parts.append([functools.partial(self.diagonal, j) for j in order])
        parts[-1] += [functools.partial(self.straight, j) for j in order]
        parts.append([functools.partial(self.bent, j) for j in order])
        parts.append([functools.partial(self.column, j) for j in (2, 3, 1, 0)])
        parts.append([self.last])
        return parts


def chunks_of(k, pieces):
    sizes = ROWS[pieces]
    return [(m, sum(sizes[:i]), sizes[i]) for m in range(k) for i in range(pieces)]


def scatter_scratch(chunks):
    out = []
    for unused, unused_row, size in chunks:
        out += [
            pltpu.VMEM((16, size, 1152), jnp.bfloat16),
            pltpu.VMEM((15, size, 1152), jnp.bfloat16),
            pltpu.VMEM((4, size, 1152), jnp.bfloat16),
            pltpu.SemaphoreType.DMA((31,)),
            pltpu.SemaphoreType.DMA((31,)),
            pltpu.SemaphoreType.DMA((4,)),
        ]
    return out


def scatter_steps(chips, full, total, scratch, chunks):
    works = [
        Scatter(chips, full, total, m, row, *scratch[6 * i : 6 * i + 6])
        for i, (m, row, unused) in enumerate(chunks)
    ]

    def finish():
        for work in works:
            work.finish()

    return woven([work.steps() for work in works]) + [finish]


def scatter_ticks(refs, spots, chunks):
    chips = Chips()
    return entered(chips, scatter_steps(chips, refs[0], refs[1], refs[2:], chunks), len(chunks), spots)


def scatter_kernel(chunks, full, total, *scratch):
    chips = Chips()
    chips.greet()
    for step in scatter_steps(chips, full, total, scratch, chunks):
        step()


def scatter_one(full, ident, pieces=PIECES):
    k = full.shape[0]
    chunks = chunks_of(k, pieces[k])
    return pl.pallas_call(
        functools.partial(scatter_kernel, chunks),
        out_shape=jax.ShapeDtypeStruct((k,) + full.shape[3:], jnp.float32),
        in_specs=[pl.BlockSpec(memory_space=pl.ANY)],
        out_specs=pl.BlockSpec(memory_space=pltpu.VMEM),
        scratch_shapes=scatter_scratch(chunks),
        compiler_params=pltpu.CompilerParams(
            collective_id=ident, has_side_effects=True, vmem_limit_bytes=BIG
        ),
    )(full)


CLIPS, PARTS = 8, 4


def all_peers(names):
    peers = []
    for name, size in ((DP, CLIPS), (MP, PARTS)):
        if name in names:
            me = lax.axis_index(name)
            peers += [{name: (me + o) % size} for o in range(1, size)]
    return peers


def greet_all(peers):
    barrier = pltpu.get_barrier_semaphore()
    for peer in peers:
        pl.semaphore_signal(barrier, inc=1, device_id=peer, device_id_type=MESH)
    pl.semaphore_wait(barrier, len(peers))


def trade(name, size, source, target, landing, send, recv, first=0):
    me = lax.axis_index(name)

    def copy(o, src, dst):
        return pltpu.make_async_remote_copy(
            src_ref=src,
            dst_ref=dst,
            send_sem=send.at[first + o],
            recv_sem=recv.at[first + o],
            device_id={name: (me + o) % size},
            device_id_type=MESH,
        )

    out = [copy(o, source((me + o) % size), target()) for o in range(1, size)]
    for one in out:
        one.start()
    for o in range(1, size):
        land = landing((me + size - o) % size)
        copy(o, land, land).wait_recv()
    for one in out:
        one.wait_send()


def exchange_call(kernel, ident, out_shape, scratch, operand, anywhere=False):
    spec = pl.BlockSpec(memory_space=pl.ANY if anywhere else pltpu.VMEM)
    return pl.pallas_call(
        kernel,
        out_shape=out_shape,
        in_specs=[spec],
        out_specs=spec,
        scratch_shapes=scratch + [pltpu.SemaphoreType.DMA((18,)), pltpu.SemaphoreType.DMA((18,))],
        compiler_params=pltpu.CompilerParams(
            collective_id=ident, has_side_effects=True, vmem_limit_bytes=BIG
        ),
    )(operand)


def share_kernel(name, size, x, out, send, recv):
    me = lax.axis_index(name)
    greet_all(all_peers((name,)))
    out[me] = x[...]
    trade(name, size, lambda to: x, lambda: out.at[me], lambda at: out.at[at], send, recv)


def share(x, name, ident):
    size = CLIPS if name == DP else PARTS
    shape = jax.ShapeDtypeStruct((size,) + x.shape, x.dtype)
    return exchange_call(functools.partial(share_kernel, name, size), ident, shape, [], x)


def gathered_sum(refs, count):
    value = refs[0]
    for i in range(1, count):
        value = value + refs[i]
    return value


def part_sum_kernel(x, out, near, one, send, recv):
    part, clip = lax.axis_index(MP), lax.axis_index(DP)
    greet_all(all_peers((DP, MP)))
    near[part] = x[...]
    trade(MP, PARTS, lambda to: x, lambda: near.at[part], lambda at: near.at[at], send, recv, 8)
    one[...] = gathered_sum(near, PARTS)
    out[clip] = one[...]
    trade(DP, CLIPS, lambda to: one, lambda: out.at[clip], lambda at: out.at[at], send, recv)


def part_sum(x, ident):
    scratch = [pltpu.VMEM((PARTS,) + x.shape, x.dtype), pltpu.VMEM(x.shape, x.dtype)]
    shape = jax.ShapeDtypeStruct((CLIPS,) + x.shape, x.dtype)
    return exchange_call(part_sum_kernel, ident, shape, scratch, x)


def whole_sum_kernel(x, out, far, near, one, two, send, recv):
    part, clip = lax.axis_index(MP), lax.axis_index(DP)
    greet_all(all_peers((DP, MP)))
    far[clip] = x[clip]
    trade(DP, CLIPS, lambda to: x.at[to], lambda: far.at[clip], lambda at: far.at[at], send, recv)
    one[...] = gathered_sum(far, CLIPS)
    near[part] = one[...]
    trade(MP, PARTS, lambda to: one, lambda: near.at[part], lambda at: near.at[at], send, recv, 7)
    two[...] = gathered_sum(near, PARTS)
    out[clip] = two[...]
    trade(DP, CLIPS, lambda to: two, lambda: out.at[clip], lambda at: out.at[at], send, recv, 10)


def whole_sum(x, ident):
    row = x.shape[1:]
    scratch = [pltpu.VMEM((n,) + row, x.dtype) for n in (CLIPS, PARTS)]
    scratch += [pltpu.VMEM(row, x.dtype)] * 2
    return exchange_call(whole_sum_kernel, ident, jax.ShapeDtypeStruct(x.shape, x.dtype), scratch, x)


def deal_kernel(x, out, send, recv):
    clip = lax.axis_index(DP)
    greet_all(all_peers((DP,)))
    out[clip] = x[clip]
    trade(DP, CLIPS, lambda to: x.at[to], lambda: out.at[clip], lambda at: out.at[at], send, recv)


def deal(x, ident):
    return exchange_call(deal_kernel, ident, jax.ShapeDtypeStruct(x.shape, x.dtype), [], x)


def to_time_kernel(x, out, local, send, recv):
    part = lax.axis_index(MP)
    greet_all(all_peers((MP,)))
    own = pltpu.make_async_copy(x.at[part], out.at[:, part], local)
    own.start()
    trade(MP, PARTS, lambda to: x.at[to], lambda: out.at[:, part], lambda at: out.at[:, at], send, recv)
    own.wait()


def to_space_kernel(x, out, local, send, recv):
    part = lax.axis_index(MP)
    greet_all(all_peers((MP,)))
    own = pltpu.make_async_copy(x.at[:, part], out.at[part], local)
    own.start()
    trade(MP, PARTS, lambda to: x.at[:, to], lambda: out.at[part], lambda at: out.at[at], send, recv)
    own.wait()


def to_time(x, ident):
    shape = jax.ShapeDtypeStruct((2, FR, PM // 8, D), x.dtype)
    operand = x.reshape(FR, 2, PM // 8, D)
    return exchange_call(
        to_time_kernel, ident, shape, [pltpu.SemaphoreType.DMA], operand, True
    ).reshape(PM, D)


def to_space(x, ident):
    shape = jax.ShapeDtypeStruct((FR, 2, PM // 8, D), x.dtype)
    operand = x.reshape(2, FR, PM // 8, D)
    return exchange_call(
        to_space_kernel, ident, shape, [pltpu.SemaphoreType.DMA], operand, True
    ).reshape(PM, D)


def normal_parts(x):
    centered = x - jnp.mean(x, -1, keepdims=True)
    inverse = lax.rsqrt(jnp.mean(centered * centered, -1, keepdims=True) + EPS_NORM)
    return centered * inverse, inverse


def normal_back(x, scale_vec, grad):
    normed, inverse = normal_parts(x)
    inner = grad * (1.0 + scale_vec)
    d_x = inverse * (
        inner
        - jnp.mean(inner, -1, keepdims=True)
        - normed * jnp.mean(inner * normed, -1, keepdims=True)
    )
    return d_x, jnp.sum(grad, 0, keepdims=True), jnp.sum(grad * normed, 0, keepdims=True)


def mxu(left, right, dims=(((1,), (0,)), ((), ()))):
    return lax.dot_general(left, right, dims, preferred_element_type=jnp.float32)


def padded_heads(pieces, before, after):
    rows = pieces[0].shape[0]
    parts = list(pieces)
    if before:
        parts.insert(0, jnp.zeros((rows, before), pieces[0].dtype))
    if after:
        parts.append(jnp.zeros((rows, after), pieces[0].dtype))
    return jnp.concatenate(parts, 1)


def head_forward(query, key_rows, value_rows, bias):
    scores = mxu(key_rows, query, CONTRACT_LAST) * HD ** (-0.5) + bias
    expd = jnp.exp(scores - jnp.max(scores, 0, keepdims=True))
    probs = (expd / jnp.sum(expd, 0, keepdims=True)).astype(jnp.bfloat16)
    return mxu(probs, value_rows, CONTRACT_ROWS)


def head_backward(query, key_rows, value_rows, bias, d_mixed):
    scores = mxu(key_rows, query, CONTRACT_LAST) * HD ** (-0.5) + bias
    expd = jnp.exp(scores - jnp.max(scores, 0, keepdims=True))
    probs = expd / jnp.sum(expd, 0, keepdims=True)
    d_value = mxu(probs.astype(jnp.bfloat16), d_mixed)
    d_probs = mxu(value_rows, d_mixed, CONTRACT_LAST)
    offset = jnp.sum(d_probs * probs, 0, keepdims=True)
    d_scores = (probs * (d_probs - offset) * HD ** (-0.5)).astype(jnp.bfloat16)
    d_query = mxu(d_scores, key_rows, CONTRACT_ROWS)
    d_key = mxu(d_scores, query)
    return d_query, d_key, d_value


def self_forward_kernel(tiles, tick, x, mods, bias, panel, mask, out, branch, source, proj, mixed, total):
    step = pl.program_id(0)
    rows = PM // tiles
    tick(0)

    @pl.when(step == 0)
    def first():
        normed, unused = normal_parts(x[...])
        source[...] = (normed * (1.0 + mods[1:2]) + mods[0:1]).astype(jnp.bfloat16)
        total[...] = jnp.zeros_like(total)

    values = mxu(source[...], panel[0, :, :896]) + bias[0]
    values = values.astype(jnp.bfloat16)
    proj[0] = values
    heads = []
    for h in range(4):
        tops = []
        for t in range(tiles):
            part = values[t * rows : (t + 1) * rows]
            at = h * HD
            tops.append(
                head_forward(
                    part[:, at : at + HD],
                    part[:, SPAN + at : SPAN + at + HD],
                    part[:, 2 * SPAN + at : 2 * SPAN + at + HD],
                    mask[...],
                )
            )
        heads.append(jnp.concatenate(tops, 0) if tiles > 1 else tops[0])
        tick(h + 1)
    packed = padded_heads(heads, 96, 0).astype(jnp.bfloat16)
    mixed[0] = packed
    total[...] += mxu(packed, panel[0, :, 768:], CONTRACT_LAST)

    @pl.when(step == 3)
    def last():
        value = total[...] + mods[6:7]
        branch[...] = value
        out[...] = x[...] + mods[2:3] * value

    tick(5)


def whole(shape):
    return pl.BlockSpec(shape, lambda i: (0,) * len(shape), pipeline_mode=pl.Buffered(1))


def slab(shape):
    return pl.BlockSpec((1,) + shape, lambda i: (i,) + (0,) * len(shape))


def grid_params(ident=None):
    if ident is None:
        return pltpu.CompilerParams(vmem_limit_bytes=BIG)
    return pltpu.CompilerParams(vmem_limit_bytes=BIG, collective_id=ident, has_side_effects=True)


def beside(kernel, ticks, spots, inputs, outputs, scratch, chunks):
    def run(*refs):
        ins, given = refs[:inputs], refs[inputs]
        outs, made = refs[inputs + 1 : inputs + 1 + outputs], refs[inputs + 1 + outputs]
        rest = refs[inputs + outputs + 2 :]
        kernel(ticks((given, made) + rest[scratch:], spots, chunks), *ins, *outs, *rest[:scratch])

    return run


def call_with(kernel, spots, operands, in_specs, out_specs, out_shape, scratch, given, ident):
    if given is None:
        return pl.pallas_call(
            functools.partial(kernel, no_ticks),
            grid=(4,),
            in_specs=in_specs,
            out_specs=out_specs,
            out_shape=out_shape,
            scratch_shapes=scratch,
            compiler_params=grid_params(),
        )(*operands)
    remote = pl.BlockSpec(memory_space=pl.ANY)
    k = given.shape[0]
    if given.ndim == 3:
        ticks, chunks, extra = gather_ticks, None, GATHER_SEMS * GATHER_PIECES[k]
        made = jax.ShapeDtypeStruct((k, 4, 8) + given.shape[1:], given.dtype)
        made_spec = remote
    else:
        ticks, chunks = scatter_ticks, chunks_of(k, PIECES[k])
        extra = scatter_scratch(chunks)
        made = jax.ShapeDtypeStruct((k,) + given.shape[3:], jnp.float32)
        made_spec = whole(made.shape)
    return pl.pallas_call(
        beside(kernel, ticks, spots, len(in_specs), len(out_specs), len(scratch), chunks),
        grid=(4,),
        in_specs=in_specs + [remote],
        out_specs=out_specs + [made_spec],
        out_shape=out_shape + [made],
        scratch_shapes=scratch + extra,
        compiler_params=grid_params(ident),
    )(*operands, given)


def self_forward(x, mods, bias, panels, mask, tiles, given=None, ident=None):
    f32, bf16 = jnp.float32, jnp.bfloat16
    rows = PM // tiles
    return call_with(
        functools.partial(self_forward_kernel, tiles),
        6,
        (x, mods, bias, panels, mask),
        [whole((PM, D)), whole((8, D)), slab((1, 896)), slab((D, D)), whole((rows, rows))],
        [whole((PM, D)), whole((PM, D)), whole((PM, D)), slab((PM, 896)), slab((PM, 384))],
        [
            jax.ShapeDtypeStruct((PM, D), f32),
            jax.ShapeDtypeStruct((PM, D), f32),
            jax.ShapeDtypeStruct((PM, D), bf16),
            jax.ShapeDtypeStruct((4, PM, 896), bf16),
            jax.ShapeDtypeStruct((4, PM, 384), bf16),
        ],
        [pltpu.VMEM((PM, D), f32)],
        given,
        ident,
    )


def self_backward_kernel(
    tiles, tick, x, grad, mods, branch, source, proj, mixed, panel, mask, out, sums, d_bias, d_panel, d_branch, total, pieces, held
):
    step = pl.program_id(0)
    rows = PM // tiles
    tick(0)

    @pl.when(step == 0)
    def first():
        value = grad[...]
        low = (mods[2:3] * value).astype(jnp.bfloat16)
        d_branch[...] = low
        sums[2:3] = jnp.sum(value * branch[...], 0, keepdims=True)
        sums[3:4] = jnp.sum(low.astype(jnp.float32), 0, keepdims=True)
        total[...] = jnp.zeros_like(total)

    low = d_branch[...]
    d_mixed = mxu(low, panel[0, :, 768:]).astype(jnp.bfloat16)
    held[...] = d_mixed
    pieces[:, 3 * SPAN :] = jnp.zeros((PM, 32), jnp.bfloat16)
    for h in range(4):
        at = h * HD
        for t in range(tiles):
            here = slice(t * rows, (t + 1) * rows)
            part = proj[0, here]
            three = head_backward(
                part[:, at : at + HD],
                part[:, SPAN + at : SPAN + at + HD],
                part[:, 2 * SPAN + at : 2 * SPAN + at + HD],
                mask[...],
                held[here, 96 + at : 96 + at + HD],
            )
            for index in range(3):
                base = index * SPAN + at
                pieces[here, base : base + HD] = three[index].astype(jnp.bfloat16)
        tick(h + 1)
    low = d_branch[...]
    d_proj = pieces[...]
    d_bias[0] = jnp.sum(d_proj.astype(jnp.float32), 0, keepdims=True)
    columns = lax.broadcasted_iota(jnp.int32, (1, 896), 1)
    kept = jnp.where(columns < 3 * SPAN, panel[0, :, :896], jnp.zeros((), jnp.bfloat16))
    total[...] += mxu(d_proj, kept, CONTRACT_LAST)
    src = source[...]
    d_panel[0, :, :768] = mxu(src, d_proj[:, :768], CONTRACT_ROWS).astype(jnp.bfloat16)
    tick(5)
    packed = mixed[0]
    d_panel[0, :, 768:896] = (
        mxu(src, d_proj[:, 768:], CONTRACT_ROWS) + mxu(low, packed[:, :128], CONTRACT_ROWS)
    ).astype(jnp.bfloat16)
    d_panel[0, :, 896:] = mxu(low, packed[:, 128:], CONTRACT_ROWS).astype(jnp.bfloat16)

    @pl.when(step == 3)
    def last():
        d_x, d_shift, d_scale = normal_back(x[...], mods[1:2], total[...])
        sums[0:1] = d_shift
        sums[1:2] = d_scale
        out[...] = grad[...] + d_x

    tick(6)


def self_backward(x, grad, mods, branch, source, proj, mixed, panels, mask, tiles, given=None, ident=None):
    f32, bf16 = jnp.float32, jnp.bfloat16
    rows = PM // tiles
    return call_with(
        functools.partial(self_backward_kernel, tiles),
        7,
        (x, grad, mods, branch, source, proj, mixed, panels, mask),
        [
            whole((PM, D)),
            whole((PM, D)),
            whole((8, D)),
            whole((PM, D)),
            whole((PM, D)),
            slab((PM, 896)),
            slab((PM, 384)),
            slab((D, D)),
            whole((rows, rows)),
        ],
        [whole((PM, D)), whole((8, D)), slab((1, 896)), slab((D, D))],
        [
            jax.ShapeDtypeStruct((PM, D), f32),
            jax.ShapeDtypeStruct((8, D), f32),
            jax.ShapeDtypeStruct((4, 1, 896), f32),
            jax.ShapeDtypeStruct((4, D, D), bf16),
        ],
        [
            pltpu.VMEM((PM, D), bf16),
            pltpu.VMEM((PM, D), f32),
            pltpu.VMEM((PM, 896), bf16),
            pltpu.VMEM((PM, 384), bf16),
        ],
        given,
        ident,
    )


def cross_forward_kernel(tick, x, mods, bias, context, panel, mask, out, proj, pair, mixed, total):
    step = pl.program_id(0)
    tick(0)

    @pl.when(step == 0)
    def first():
        total[...] = jnp.zeros_like(total)

    query = (mxu(x[...].astype(jnp.bfloat16), panel[0, :, :384]) + bias[0, :, :384]).astype(jnp.bfloat16)
    both = (mxu(context[...], panel[0, :, 256:896]) + bias[0, :, 256:896]).astype(jnp.bfloat16)
    proj[0] = query
    pair[0] = both
    heads = []
    for h in range(4):
        at = h * HD
        heads.append(
            head_forward(
                query[:, at : at + HD],
                both[:, 32 + at : 32 + at + HD],
                both[:, 32 + SPAN + at : 32 + SPAN + at + HD],
                mask[...],
            )
        )
        tick(h + 1)
    packed = padded_heads(heads, 96, 0).astype(jnp.bfloat16)
    mixed[0] = packed
    total[...] += mxu(packed, panel[0, :, 768:], CONTRACT_LAST)

    @pl.when(step == 3)
    def last():
        out[...] = x[...] + total[...] + mods[6:7]

    tick(5)


def cross_forward(x, mods, bias, context, panels, mask, given=None, ident=None):
    f32, bf16 = jnp.float32, jnp.bfloat16
    return call_with(
        cross_forward_kernel,
        6,
        (x, mods, bias, context, panels, mask),
        [
            whole((PM, D)),
            whole((8, D)),
            slab((1, 896)),
            whole((128, D)),
            slab((D, D)),
            whole((128, 1)),
        ],
        [whole((PM, D)), slab((PM, 384)), slab((128, 640)), slab((PM, 384))],
        [
            jax.ShapeDtypeStruct((PM, D), f32),
            jax.ShapeDtypeStruct((4, PM, 384), bf16),
            jax.ShapeDtypeStruct((4, 128, 640), bf16),
            jax.ShapeDtypeStruct((4, PM, 384), bf16),
        ],
        [pltpu.VMEM((PM, D), f32)],
        given,
        ident,
    )


def cross_backward_kernel(
    tick, x, grad, context, proj, pair, mixed, panel, mask, out, d_context, sums, d_bias, d_panel, total, ask, keys, held
):
    step = pl.program_id(0)
    tick(0)

    @pl.when(step == 0)
    def first():
        low = grad[...].astype(jnp.bfloat16)
        sums[0:1] = jnp.sum(low.astype(jnp.float32), 0, keepdims=True)
        total[...] = jnp.zeros_like(total)
        d_context[...] = jnp.zeros_like(d_context)

    low = grad[...].astype(jnp.bfloat16)
    d_mixed = mxu(low, panel[0, :, 768:]).astype(jnp.bfloat16)
    held[...] = d_mixed
    ask[:, SPAN:] = jnp.zeros((PM, 96), jnp.bfloat16)
    keys[...] = jnp.zeros_like(keys)
    for h in range(4):
        at = h * HD
        query, both = proj[0], pair[0]
        three = head_backward(
            query[:, at : at + HD],
            both[:, 32 + at : 32 + at + HD],
            both[:, 32 + SPAN + at : 32 + SPAN + at + HD],
            mask[...],
            held[:, 96 + at : 96 + at + HD],
        )
        ask[:, at : at + HD] = three[0].astype(jnp.bfloat16)
        keys[:, 32 + at : 32 + at + HD] = three[1].astype(jnp.bfloat16)
        keys[:, 32 + SPAN + at : 32 + SPAN + at + HD] = three[2].astype(jnp.bfloat16)
        tick(h + 1)
    d_ask, d_both = ask[...], keys[...]
    low = grad[...].astype(jnp.bfloat16)
    sum_both = jnp.sum(d_both.astype(jnp.float32), 0, keepdims=True)
    d_bias[0, :, :384] = jnp.sum(d_ask.astype(jnp.float32), 0, keepdims=True)
    d_bias[0, :, 384:] = sum_both
    total[...] += mxu(d_ask, panel[0, :, :384], CONTRACT_LAST)
    d_context[...] += mxu(d_both, panel[0, :, 256:896], CONTRACT_LAST)
    src, ctx, packed = x[...].astype(jnp.bfloat16), context[...], mixed[0]
    d_panel[0, :, :256] = mxu(src, d_ask[:, :256], CONTRACT_ROWS).astype(jnp.bfloat16)
    d_panel[0, :, 256:384] = (
        mxu(src, d_ask[:, 256:], CONTRACT_ROWS) + mxu(ctx, d_both[:, :128], CONTRACT_ROWS)
    ).astype(jnp.bfloat16)
    tick(5)
    d_panel[0, :, 384:768] = mxu(ctx, d_both[:, 128:512], CONTRACT_ROWS).astype(jnp.bfloat16)
    d_panel[0, :, 768:896] = (
        mxu(ctx, d_both[:, 512:], CONTRACT_ROWS) + mxu(low, packed[:, :128], CONTRACT_ROWS)
    ).astype(jnp.bfloat16)
    d_panel[0, :, 896:] = mxu(low, packed[:, 128:], CONTRACT_ROWS).astype(jnp.bfloat16)

    @pl.when(step == 3)
    def last():
        out[...] = grad[...] + total[...]

    tick(6)


def cross_backward(x, grad, context, proj, pair, mixed, panels, mask, given=None, ident=None):
    f32, bf16 = jnp.float32, jnp.bfloat16
    return call_with(
        cross_backward_kernel,
        7,
        (x, grad, context, proj, pair, mixed, panels, mask),
        [
            whole((PM, D)),
            whole((PM, D)),
            whole((128, D)),
            slab((PM, 384)),
            slab((128, 640)),
            slab((PM, 384)),
            slab((D, D)),
            whole((128, 1)),
        ],
        [whole((PM, D)), whole((128, D)), whole((8, D)), slab((1, 1024)), slab((D, D))],
        [
            jax.ShapeDtypeStruct((PM, D), f32),
            jax.ShapeDtypeStruct((128, D), f32),
            jax.ShapeDtypeStruct((8, D), f32),
            jax.ShapeDtypeStruct((4, 1, 1024), f32),
            jax.ShapeDtypeStruct((4, D, D), bf16),
        ],
        [
            pltpu.VMEM((PM, D), f32),
            pltpu.VMEM((PM, 384), bf16),
            pltpu.VMEM((128, 640), bf16),
            pltpu.VMEM((PM, 384), bf16),
        ],
        given,
        ident,
    )


GELU_A = math.sqrt(2.0 / math.pi)
GELU_B = 0.044715


def ffn_forward_kernel(tick, x, mods, bias, w_in, w_out, out, branch, source, pre, total):
    step = pl.program_id(0)
    tick(0)

    @pl.when(step == 0)
    def first():
        normed, unused = normal_parts(x[...])
        source[...] = (normed * (1.0 + mods[4:5]) + mods[3:4]).astype(jnp.bfloat16)
        total[...] = jnp.zeros_like(total)

    value = mxu(source[...], w_in[0, 0]) + bias[0]
    pre[0] = value
    tick(1)
    hidden = 0.5 * value * (1.0 + jnp.tanh(GELU_A * (value + GELU_B * value * value * value)))
    tick(2)
    total[...] += mxu(hidden.astype(jnp.bfloat16), w_out[0, 0], CONTRACT_LAST)

    @pl.when(step == 3)
    def last():
        result = total[...] + mods[6:7]
        branch[...] = result
        out[...] = x[...] + mods[5:6] * result

    tick(3)


def half(index):
    return pl.BlockSpec((1, 1, D, D), lambda i: (index, i, 0, 0))


def ffn_forward_chip(x, mods, bias, panels, given=None, ident=None):
    f32, bf16 = jnp.float32, jnp.bfloat16
    return call_with(
        ffn_forward_kernel,
        4,
        (x, mods, bias, panels, panels),
        [whole((PM, D)), whole((8, D)), slab((1, D)), half(0), half(1)],
        [whole((PM, D)), whole((PM, D)), whole((PM, D)), slab((PM, D))],
        [
            jax.ShapeDtypeStruct((PM, D), f32),
            jax.ShapeDtypeStruct((PM, D), f32),
            jax.ShapeDtypeStruct((PM, D), bf16),
            jax.ShapeDtypeStruct((4, PM, D), f32),
        ],
        [pltpu.VMEM((PM, D), f32)],
        given,
        ident,
    )


def ffn_backward_kernel(
    tick, x, grad, mods, branch, source, pre, w_in, w_out, out, sums, d_bias, d_panel, d_branch, total
):
    step = pl.program_id(0)
    tick(0)

    @pl.when(step == 0)
    def first():
        value = grad[...]
        low = (mods[5:6] * value).astype(jnp.bfloat16)
        d_branch[...] = low
        sums[2:3] = jnp.sum(value * branch[...], 0, keepdims=True)
        sums[3:4] = jnp.sum(low.astype(jnp.float32), 0, keepdims=True)
        total[...] = jnp.zeros_like(total)

    low = d_branch[...]
    value = pre[0]
    square = value * value
    bent = jnp.tanh(GELU_A * (value + GELU_B * value * square))
    slope = 0.5 * (1.0 + bent) + 0.5 * value * (1.0 - bent * bent) * GELU_A * (
        1.0 + 3.0 * GELU_B * square
    )
    hidden = (0.5 * value * (1.0 + bent)).astype(jnp.bfloat16)
    d_pre = (mxu(low, w_out[0, 0]) * slope).astype(jnp.bfloat16)
    tick(1)
    d_bias[0] = jnp.sum(d_pre.astype(jnp.float32), 0, keepdims=True)
    total[...] += mxu(d_pre, w_in[0, 0], CONTRACT_LAST)
    tick(2)
    d_panel[0, 0] = mxu(source[...], d_pre, CONTRACT_ROWS).astype(jnp.bfloat16)
    tick(3)
    d_panel[1, 0] = mxu(low, hidden, CONTRACT_ROWS).astype(jnp.bfloat16)

    @pl.when(step == 3)
    def last():
        d_x, d_shift, d_scale = normal_back(x[...], mods[4:5], total[...])
        sums[0:1] = d_shift
        sums[1:2] = d_scale
        out[...] = grad[...] + d_x

    tick(4)


def ffn_backward_chip(x, grad, mods, branch, source, pre, panels, given=None, ident=None):
    f32, bf16 = jnp.float32, jnp.bfloat16
    return call_with(
        ffn_backward_kernel,
        5,
        (x, grad, mods, branch, source, pre, panels, panels),
        [
            whole((PM, D)),
            whole((PM, D)),
            whole((8, D)),
            whole((PM, D)),
            whole((PM, D)),
            slab((PM, D)),
            half(0),
            half(1),
        ],
        [
            whole((PM, D)),
            whole((8, D)),
            slab((1, D)),
            pl.BlockSpec((2, 1, D, D), lambda i: (0, i, 0, 0), pipeline_mode=pl.Buffered(1)),
        ],
        [
            jax.ShapeDtypeStruct((PM, D), f32),
            jax.ShapeDtypeStruct((8, D), f32),
            jax.ShapeDtypeStruct((4, 1, D), f32),
            jax.ShapeDtypeStruct((2, 4, D, D), bf16),
        ],
        [pltpu.VMEM((PM, D), bf16), pltpu.VMEM((PM, D), f32)],
        given,
        ident,
    )


def modulate_back(x, shift_vec, scale_vec, grad):
    unused, pull = jax.vjp(modulate, x, shift_vec, scale_vec)
    return pull(grad)


def padded_rows(value):
    return jnp.pad(value, ((0, 128 - value.shape[0]), (0, 0)))


def local_rows(full, group):
    return lax.dynamic_slice_in_dim(full, group * EMB_LOCAL, EMB_LOCAL, 1)


def per_device_chips(
    latents,
    noise,
    caption,
    caption_lens,
    timesteps,
    grid_hw,
    frame_counts,
    attn_mats,
    ffn_mats,
    embed_mats,
    vectors,
    attn_first,
    ffn_first,
    embed_first,
    vector_first,
    attn_second,
    ffn_second,
    embed_second,
    vector_second,
    attn_ema,
    ffn_ema,
    embed_ema,
    vector_ema,
):
    group = lax.axis_index(DP)
    part = lax.axis_index(MP)
    clips = timesteps.shape[0]
    parts = unpack(vectors)
    bf16 = jnp.bfloat16
    f32 = jnp.float32

    attn_low = sort_panels(attn_mats)
    ffn_low = ffn_mats.astype(bf16)

    def panels(full):
        full = full.reshape(full.shape[:2] + (D, D))
        return full if full.shape[0] > 1 else full[0]

    w_space = panels(gather_all(attn_low[0:1], 0))

    pick = jnp.arange(clips, dtype=jnp.int32) == group

    def select(values):
        return jnp.sum(jnp.where(pick, values, 0))

    tstep = select(timesteps)
    cap_len = select(caption_lens)
    height = select(grid_hw[:, 0])
    width_grid = select(grid_hw[:, 1])
    frames = select(frame_counts)
    count = jnp.sum(frame_counts * grid_hw[:, 0] * grid_hw[:, 1]).astype(f32)
    betas, cumul = roster()
    step_ids = jnp.arange(1000, dtype=jnp.int32)
    alpha_bar = jnp.sum(jnp.where(step_ids == tstep, cumul, 0.0))
    alpha_prev = jnp.sum(jnp.where(step_ids == tstep - 1, cumul, 0.0))
    beta_now = jnp.sum(jnp.where(step_ids == tstep, betas, 0.0))

    embed_low = embed_mats.astype(bf16)
    width_local = embed_low.shape[1]
    captions = lax.all_gather(caption[0], DP, axis=0, tiled=True)
    lead = TFREQ + TXT
    cap_rows = local_rows(jnp.pad(captions, ((0, 0), (TFREQ, EMB_ALL - lead))), group)
    freq = waves(timesteps.astype(f32), TFREQ).astype(bf16)
    freq_rows = local_rows(jnp.pad(freq, ((0, 0), (0, EMB_ALL - TFREQ))), group)

    def from_rows(local):
        return part_sum(local, 1).swapaxes(0, 1).reshape(clips, EMB_ALL)

    def over_clips(value):
        return jnp.sum(share(value, DP, 2), 0)

    t_pre = over_clips(jnp.dot(freq_rows, embed_low, preferred_element_type=f32))
    t_pre = t_pre + own_slice(parts[T_BIAS_ONE], part, width_local)
    t_hidden = jax.nn.silu(t_pre).astype(bf16)
    t_sum = from_rows(lax.dot_general(t_hidden, embed_low, CONTRACT_LAST, preferred_element_type=f32))
    t_emb_all = t_sum[:, lead : lead + D] + parts[T_BIAS_TWO]
    t_emb_local = lax.dynamic_slice_in_dim(t_emb_all, part * width_local, width_local, 1)
    silu_local = jax.nn.silu(t_emb_local).astype(bf16)
    mod_sum = from_rows(
        lax.dot_general(silu_local, embed_low, CONTRACT_LAST, preferred_element_type=f32)
    )[:, lead + 2 * D :]
    t_mod_vec = jnp.sum(jnp.where(pick[:, None], mod_sum, 0.0), 0) + parts[T_BIAS_MOD]
    t_emb = jnp.sum(jnp.where(pick[:, None], t_emb_all, 0.0), 0)

    c_two_row = lead + D - group * EMB_LOCAL
    c_row_ids = c_two_row + jnp.arange(D, dtype=jnp.int32)
    c_held = (c_two_row >= 0) & (c_two_row + D <= EMB_LOCAL)
    c_two = lax.dynamic_slice_in_dim(embed_low, jnp.clip(c_two_row, 0, EMB_LOCAL - D), D, 0)
    c_two = lax.psum(jnp.where(c_held, c_two, jnp.zeros_like(c_two)), DP)
    c_product = jnp.dot(cap_rows, embed_low, preferred_element_type=f32)
    c_pre = jnp.sum(deal(c_product.reshape(clips, CAP, width_local), 3), 0)
    c_pre = c_pre + own_slice(parts[C_BIAS_ONE], part, width_local)
    c_hidden = gelu_tanh(c_pre).astype(bf16)
    c_part = lax.dot_general(c_hidden, c_two, CONTRACT_LAST, preferred_element_type=f32)

    def over_parts(value):
        return jnp.sum(share(padded_rows(value.astype(bf16)), MP, 4).astype(f32), 0)

    context = padded_rows((over_parts(c_part)[:CAP] + parts[C_BIAS_TWO]).astype(bf16))

    area = height * width_grid
    patch_ids = jnp.arange(PM, dtype=jnp.int32)
    shifted = patch_ids - (PM - area)
    noisy = jnp.sqrt(alpha_bar) * latents[0] + jnp.sqrt(1.0 - alpha_bar) * noise[0]
    noisy_low = noisy.astype(bf16)
    position = jnp.concatenate(
        [
            waves((shifted // width_grid).astype(f32), D // 2),
            waves((shifted % width_grid).astype(f32), D // 2),
        ],
        -1,
    )
    x = jnp.dot(noisy_low, parts[PATCH_W].astype(bf16), preferred_element_type=f32)
    x = x + parts[PATCH_B] + position
    tables = parts[TABLES] + t_mod_vec.reshape(1, 6, D)
    mods0, mods1 = tables[0], tables[1]
    mask_space = jnp.where(patch_ids >= PM - area, 0.0, NEG_LARGE)[:, None]
    mask_space = jnp.broadcast_to(mask_space, (PM, PM))
    mask_cross = jnp.where(jnp.arange(128, dtype=jnp.int32) < cap_len, 0.0, NEG_LARGE)[:, None]
    half_ids = jnp.arange(PM // 2, dtype=jnp.int32)
    frame_ids, place_ids = half_ids // (PM // 8), half_ids % (PM // 8)
    mask_time = jnp.where(
        (place_ids[:, None] == place_ids[None]) & (frame_ids[:, None] >= FR - frames), 0.0, NEG_LARGE
    )
    biases = parts[ATTN_BIAS]

    def side(values):
        blank = jnp.zeros((4, SPAN), f32)
        rows = [values[0].reshape(4, SPAN), blank, values[1].reshape(4, SPAN), blank[:, :32]]
        return jnp.concatenate(rows, 1)[:, None]

    def vectors_of(mods, out_bias):
        return jnp.concatenate([mods, out_bias[None], jnp.zeros((1, D), f32)])

    x0 = x
    m_space, m_ffn0 = vectors_of(mods0, biases[0, 2]), vectors_of(mods0, parts[FFN_BIAS_TWO][0])
    x1, branch0, source0, proj0, mixed0, full = self_forward(
        x0, m_space, side(biases[0]), w_space, mask_space, 1, attn_low[2:3], 5
    )
    w_cross = panels(full)
    m_cross = vectors_of(mods0, biases[2, 2])
    x2, cross_q, cross_kv, mixed1, full = cross_forward(
        x1, m_cross, side(biases[2]), context, w_cross, mask_cross, ffn_low[0], 6
    )
    w_ffn0 = panels(full)
    bias_ffn = parts[FFN_BIAS_ONE].reshape(2, 4, 1, D)
    x3, branch2, source2, pre2, full = ffn_forward_chip(
        x2, m_ffn0, bias_ffn[0], w_ffn0, attn_low[1:2], 7
    )
    w_time = panels(full)
    x3 = x3 + waves((part - (FR - frames)).astype(f32)[None], D)

    share_rows = PM // FR
    pixels = jnp.concatenate([latents[0], noise[0]], 1).reshape(FR, share_rows, -1)
    pixels = lax.all_to_all(pixels, MP, 0, 0, tiled=True).reshape(FR, 2, PM // 8, -1)
    pixels = pixels.swapaxes(0, 1).reshape(PM, -1)
    latent_time, noise_time = pixels[:, :CIN], pixels[:, CIN:]
    x4 = to_time(x3, 8)
    m_time, m_ffn1 = vectors_of(mods1, biases[1, 2]), vectors_of(mods1, parts[FFN_BIAS_TWO][1])
    x5, branch4, source4, proj4, mixed4, full = self_forward(
        x4, m_time, side(biases[1]), w_time, mask_time, 2, ffn_low[1], 9
    )
    w_ffn1 = panels(full)
    x6, branch5, source5, pre5 = ffn_forward_chip(x5, m_ffn1, bias_ffn[1], w_ffn1)

    final_mods = parts[FINAL_TABLE] + t_emb
    final_source = modulate(x6, final_mods[0], final_mods[1]).astype(bf16)
    final_low = parts[FINAL_W].astype(bf16)
    output = (
        lax.dot_general(final_source, final_low, CONTRACT_LAST, preferred_element_type=f32)
        + parts[FINAL_B]
    )
    frozen = output[:, :CIN]
    noisy_time = jnp.sqrt(alpha_bar) * latent_time + jnp.sqrt(1.0 - alpha_bar) * noise_time
    row_ids = jnp.arange(PM, dtype=jnp.int32)
    row_frames = (row_ids % (PM // 2)) // (PM // 8)
    row_patches = part * share_rows + (row_ids // (PM // 2)) * (PM // 8) + row_ids % (PM // 8)
    valid = (row_frames >= FR - frames) & (row_patches >= PM - area)

    def shard_loss(values):
        losses = token_losses(
            values, frozen, latent_time, noise_time, (noisy_time, alpha_bar, alpha_prev, beta_now)
        )
        return jnp.sum(jnp.where(valid, losses, 0.0))

    loss_part, loss_pull = jax.vjp(shard_loss, output)
    d_output = loss_pull(1.0 / count)[0].astype(bf16)
    d_final_w = lax.dot_general(d_output, final_source, CONTRACT_ROWS, preferred_element_type=f32)
    d_final_b = jnp.sum(d_output.astype(f32), 0)
    d_final_source = jnp.dot(d_output, final_low, preferred_element_type=f32)
    grad_x, d_final_shift, d_final_scale = modulate_back(
        x6, final_mods[0], final_mods[1], d_final_source
    )

    def blocks(grads):
        return grads.reshape((-1, 4, 8, BLOCK, D))

    grad_x, sums5, bias5, d_ffn1 = ffn_backward_chip(
        x5, grad_x, m_ffn1, branch5, source5, pre5, w_ffn1
    )
    grad_x, sums4, bias4, d_time, g_ffn1 = self_backward(
        x4, grad_x, m_time, branch4, source4, proj4, mixed4, w_time, mask_time, 2, blocks(d_ffn1), 10
    )
    d_mods1 = jnp.concatenate([sums4[:3], sums5[:3]])
    grad_x = to_space(grad_x, 12)

    grad_x, sums2, bias2, d_ffn0, g_time = ffn_backward_chip(
        x2, grad_x, m_ffn0, branch2, source2, pre2, w_ffn0, blocks(d_time), 11
    )
    grad_x, d_context, sums1, bias1, d_cross, g_ffn0 = cross_backward(
        x1, grad_x, context, cross_q, cross_kv, mixed1, w_cross, mask_cross, blocks(d_ffn0), 16
    )

    first_part = (part == 0).astype(f32)
    d_context = over_parts(d_context)[:CAP].astype(bf16)
    d_c_bias_two = jnp.sum(d_context.astype(f32), 0) * first_part
    d_c_hidden = jnp.dot(d_context, c_two, preferred_element_type=f32)
    unused, cap_pull = jax.vjp(gelu_tanh, c_pre)
    d_c_pre = cap_pull(d_c_hidden)[0].astype(bf16)
    d_c_bias_one = jnp.sum(d_c_pre.astype(f32), 0)
    caption_all = lax.all_gather(
        jnp.concatenate([d_context, c_hidden, d_c_pre], 1), DP, axis=0, tiled=True
    )
    d_context_all = caption_all[:, :D]
    c_hidden_all = caption_all[:, D : D + width_local]
    d_c_pre_all = caption_all[:, D + width_local :]
    d_c_one = lax.dot_general(cap_rows, d_c_pre_all, CONTRACT_ROWS, preferred_element_type=f32)
    d_c_two = lax.dot_general(d_context_all, c_hidden_all, CONTRACT_ROWS, preferred_element_type=f32)

    grad_x, sums0, bias0, d_space, g_cross = self_backward(
        x0, grad_x, m_space, branch0, source0, proj0, mixed0, w_space, mask_space, 1, blocks(d_cross), 17
    )
    g_space = scatter_one(blocks(d_space), 18)
    d_mods0 = jnp.concatenate([sums0[:3], sums2[:3]])

    def side_sums(values, at_query, at_value, out_bias):
        rows = [values[:, 0, at : at + SPAN].reshape(-1) for at in (at_query, at_value)]
        return jnp.stack(rows + [out_bias])

    d_patch = grad_x.astype(bf16)
    d_patch_b = jnp.sum(d_patch.astype(f32), 0)
    d_patch_w = lax.dot_general(noisy_low, d_patch, CONTRACT_ROWS, preferred_element_type=f32)

    d_mod_part = (d_mods0 + d_mods1).reshape(-1)
    d_temb_part = d_final_shift + d_final_scale
    d_mod_all = part_sum(jnp.concatenate([d_mod_part, d_temb_part]).reshape(8, 7 * D // 8), 13)
    d_mod_all = d_mod_all.reshape(clips, 7 * D)
    d_temb_sum = d_mod_all[:, 6 * D :]
    d_mod_low = d_mod_all[:, : 6 * D].astype(bf16)
    d_mod_rows = local_rows(jnp.pad(d_mod_low, ((0, 0), (lead + 2 * D, 0))), group)
    d_silu = over_clips(jnp.dot(d_mod_rows, embed_low, preferred_element_type=f32))
    unused, silu_pull = jax.vjp(jax.nn.silu, t_emb_local)
    d_temb_local = silu_pull(d_silu)[0]
    d_temb = share(d_temb_local, MP, 14).swapaxes(0, 1).reshape(clips, D) + d_temb_sum
    d_temb_rows = local_rows(jnp.pad(d_temb, ((0, 0), (lead, EMB_ALL - lead - D))), group)
    d_t_hidden = over_clips(
        jnp.dot(d_temb_rows, embed_low.astype(f32), precision=lax.Precision.HIGHEST)
    )
    unused, pre_pull = jax.vjp(jax.nn.silu, t_pre)
    d_t_pre = pre_pull(d_t_hidden)[0]

    def outer(left, right):
        return lax.dot_general(
            left.astype(f32), right.astype(f32), CONTRACT_ROWS, precision=lax.Precision.HIGHEST
        )

    g_embed = (
        lax.dot_general(d_mod_rows, silu_local, CONTRACT_ROWS, preferred_element_type=f32)
        + outer(jnp.concatenate([d_temb_rows, freq_rows.astype(f32)]), jnp.concatenate([t_hidden.astype(f32), d_t_pre]))
        + d_c_one
    )
    here = lax.dynamic_slice_in_dim(g_embed, jnp.clip(c_two_row, 0, EMB_LOCAL - D), D, 0)
    g_embed = lax.dynamic_update_slice_in_dim(
        g_embed, jnp.where(c_held, d_c_two, here), jnp.clip(c_two_row, 0, EMB_LOCAL - D), 0
    )

    first_clip = pick.astype(f32) * first_part
    vector_grads = {
        PATCH_W: d_patch_w,
        PATCH_B: d_patch_b,
        FINAL_W: d_final_w,
        FINAL_B: d_final_b,
        T_BIAS_ONE: placed(jnp.sum(d_t_pre * pick.astype(f32)[:, None], 0), part, D),
        T_BIAS_TWO: d_temb_part
        + placed(jnp.sum(d_temb_local * pick.astype(f32)[:, None], 0), part, D),
        T_BIAS_MOD: d_mod_part,
        C_BIAS_ONE: placed(d_c_bias_one, part, D),
        C_BIAS_TWO: d_c_bias_two,
        ATTN_BIAS: jnp.stack(
            [
                side_sums(bias0, 0, 2 * SPAN, sums0[3]),
                side_sums(bias4, 0, 2 * SPAN, sums4[3]),
                side_sums(bias1, 0, 416 + SPAN, sums1[0]),
            ]
        ),
        FFN_BIAS_ONE: jnp.stack([bias2, bias5]),
        FFN_BIAS_TWO: jnp.stack([sums2[3], sums5[3]]),
        TABLES: jnp.stack([d_mods0, d_mods1]),
        FINAL_TABLE: jnp.stack([d_final_shift, d_final_scale]),
    }
    vector_grad = jnp.concatenate(
        [vector_grads[label].reshape(-1) for label, extent in vector_parts()]
    )
    g_attn = jnp.stack([g_space[0], g_time[0], g_cross[0]])
    g_ffn = jnp.stack([g_ffn0, g_ffn1])
    matrix_squares = jnp.sum(g_attn * g_attn) + jnp.sum(g_ffn * g_ffn) + jnp.sum(g_embed * g_embed)
    length = vector_grad.shape[0]
    spare = -(length + 2) % (8 * 8 * 128)
    totals = jnp.concatenate([vector_grad, matrix_squares[None], loss_part[None], jnp.zeros((spare,), f32)])
    totals = whole_sum(totals.reshape(8, -1, 128), 15).reshape(-1)
    g_vector = totals[:length]
    loss_total = totals[length + 1]
    squares = totals[length] + jnp.sum(g_vector * g_vector)
    grad_norm = jnp.sqrt(squares)
    factor = CLIP_NORM / (grad_norm + 1e-06)
    new_attn = adam_update(
        attn_mats, attn_first, attn_second, attn_ema, g_attn * factor, LEARN_RATE
    )
    new_ffn = adam_update(ffn_mats, ffn_first, ffn_second, ffn_ema, g_ffn * factor, LEARN_RATE)
    new_embed = adam_update(
        embed_mats, embed_first, embed_second, embed_ema, g_embed * factor, LEARN_RATE
    )
    new_vector = adam_update(
        vectors, vector_first, vector_second, vector_ema, g_vector * factor, VECTOR_RATE
    )
    return (loss_total, count, grad_norm) + tuple(
        group_new[kind]
        for kind in range(4)
        for group_new in (new_attn, new_ffn, new_embed, new_vector)
    )


def solution(mesh):
    fits = dict(mesh.shape) == {DP: CLIPS, MP: FR}
    program = per_device_chips if fits else per_device
    return jax.shard_map(
        program,
        mesh=mesh,
        in_specs=(
            P(DP, MP, None),
            P(DP, MP, None),
            P(DP, None, None),
            P(),
            P(),
            P(),
            P(),
            P(None, DP, MP),
            P(None, None, DP, MP),
            P(DP, MP),
            P(),
            P(None, DP, MP),
            P(None, None, DP, MP),
            P(DP, MP),
            P(),
            P(None, DP, MP),
            P(None, None, DP, MP),
            P(DP, MP),
            P(),
            P(None, DP, MP),
            P(None, None, DP, MP),
            P(DP, MP),
            P(),
        ),
        out_specs=(
            P(),
            P(),
            P(),
            P(None, DP, MP),
            P(None, None, DP, MP),
            P(DP, MP),
            P(),
            P(None, DP, MP),
            P(None, None, DP, MP),
            P(DP, MP),
            P(),
            P(None, DP, MP),
            P(None, None, DP, MP),
            P(DP, MP),
            P(),
            P(None, DP, MP),
            P(None, None, DP, MP),
            P(DP, MP),
            P(),
        ),
        check_vma=False,
    )
```

```python
import functools
import math

import jax
import jax.numpy as jnp
from jax import lax
from jax.experimental import pallas as pl
from jax.experimental.pallas import tpu as pltpu
from jax.sharding import PartitionSpec as P

D = 1152
HEADS = 16
HD = 72
FF = 4608
TFREQ = 256
TXT = 4096
CIN = 16
COUT = 32
CAP = 120
FR = 4
PM = 448
STEP = 5
DP, MP = "dp", "mp"
AT_SPACE = 0
AT_TIME = 1
AT_CROSS = 2
AT_ATTN = 3
AT_FFN = 4
AT_PARTS = 5
AT_PART = 6
AT_CONTEXT = 7
AT_KEEP = 8
AT_INPUT = 9
AT_GATHERED = 10
AT_QUERY = 11
AT_KEY_ROWS = 12
AT_VALUE_ROWS = 13
AT_LOGSUM = 14
AT_MIXED = 15
AT_BRANCH = 16
AT_PRE = 17
AT_HIDDEN = 18
PATCH_W = 0
PATCH_B = 1
FINAL_W = 2
FINAL_B = 3
T_BIAS_ONE = 4
T_BIAS_TWO = 5
T_BIAS_MOD = 6
C_BIAS_ONE = 7
C_BIAS_TWO = 8
ATTN_BIAS = 9
FFN_BIAS_ONE = 10
FFN_BIAS_TWO = 11
TABLES = 12
FINAL_TABLE = 13


EPS_NORM = 1e-06
LEARN_RATE = 0.03
VECTOR_RATE = 0.15
BETA_FIRST = 0.5
BETA_SECOND = 0.5
ADAM_EPSILON = 1e-08
WEIGHT_DECAY = 0.01
EMA_DECAY = 0.9
CLIP_NORM = 0.02
NEG_LARGE = -1e30
CONTRACT_ROWS = (((0,), (0,)), ((), ()))
CONTRACT_LAST = (((1,), (1,)), ((), ()))


def vector_parts():
    return [
        (PATCH_W, (CIN, D)),
        (PATCH_B, (D,)),
        (FINAL_W, (COUT, D)),
        (FINAL_B, (COUT,)),
        (T_BIAS_ONE, (D,)),
        (T_BIAS_TWO, (D,)),
        (T_BIAS_MOD, (6 * D,)),
        (C_BIAS_ONE, (D,)),
        (C_BIAS_TWO, (D,)),
        (ATTN_BIAS, (3, 3, D)),
        (FFN_BIAS_ONE, (2, FF)),
        (FFN_BIAS_TWO, (2, D)),
        (TABLES, (2, 6, D)),
        (FINAL_TABLE, (2, D)),
    ]


def unpack(flat):
    result = {}
    offset = 0
    for label, extent in vector_parts():
        length = math.prod(extent)
        result[label] = flat[offset : offset + length].reshape(extent)
        offset += length
    return result


def waves(position, width):
    half = width // 2
    freqs = jnp.exp(-math.log(10000.0) * jnp.arange(half, dtype=jnp.float32) / half)
    angles = position[..., None] * freqs
    return jnp.concatenate([jnp.sin(angles), jnp.cos(angles)], -1)


def roster():
    betas = 0.0001 + (0.02 - 0.0001) * jnp.arange(1000, dtype=jnp.float32) / 999.0
    return (betas, jnp.exp(jnp.cumsum(jnp.log1p(-betas))))


def modulate(x, shift_vec, scale_vec):
    centered = x - jnp.mean(x, -1, keepdims=True)
    normed = centered * lax.rsqrt(jnp.mean(centered * centered, -1, keepdims=True) + EPS_NORM)
    return normed * (1.0 + scale_vec) + shift_vec


def gelu_tanh(values):
    return jax.nn.gelu(values, approximate=True)


def token_losses(output, frozen, latent, noise_part, extra):
    noisy, alpha_bar, alpha_prev, beta_now = extra
    eps = output[:, :CIN]
    var_raw = output[:, CIN:]
    mse = jnp.mean((eps - noise_part) ** 2, -1)
    post_var = beta_now * (1.0 - alpha_prev) / (1.0 - alpha_bar)
    log_post = jnp.log(post_var)
    frac = (var_raw + 1.0) / 2.0
    log_var = frac * jnp.log(beta_now) + (1.0 - frac) * log_post
    coef_start = beta_now * jnp.sqrt(alpha_prev) / (1.0 - alpha_bar)
    coef_now = (1.0 - alpha_prev) * jnp.sqrt(1.0 - beta_now) / (1.0 - alpha_bar)
    true_mean = coef_start * latent + coef_now * noisy
    guess = (noisy - jnp.sqrt(1.0 - alpha_bar) * frozen) / jnp.sqrt(alpha_bar)
    model_mean = coef_start * guess + coef_now * noisy
    kl_term = 0.5 * (
        -1.0
        + log_var
        - log_post
        + jnp.exp(log_post - log_var)
        + (true_mean - model_mean) ** 2 * jnp.exp(-log_var)
    )
    return mse + jnp.mean(kl_term, -1) / math.log(2.0)


def attention_forms(kind):
    if kind == AT_SPACE:
        return ("fqhe,fkhe->fhqk", "fhqk,fkhe->fqhe", "fhqk,fqhe->fkhe")
    if kind == AT_TIME:
        return ("qphe,kphe->phqk", "phqk,kphe->qphe", "phqk,qphe->kphe")
    return ("qhe,khe->hqk", "hqk,khe->qhe", "hqk,qhe->khe")


def own_slice(vector, part, width):
    return lax.dynamic_slice_in_dim(vector, part * width, width, 0)


def placed(piece, part, full):
    return lax.dynamic_update_slice_in_dim(
        jnp.zeros((full,), jnp.float32), piece, part * piece.shape[0], 0
    )


def project_in(shard_rows, weight):
    piece = lax.all_gather(shard_rows, MP, axis=0, tiled=True)
    product = jnp.dot(piece, weight, preferred_element_type=jnp.float32)
    return (product, piece)


def project_out(full_rows, weight_t):
    return lax.psum_scatter(
        lax.dot_general(
            full_rows, weight_t, CONTRACT_LAST, preferred_element_type=jnp.float32
        ).astype(jnp.bfloat16),
        MP,
        scatter_dimension=0,
        tiled=True,
    ).astype(jnp.float32)


def back_out(grad_rows, full_rows, weight_t):
    piece = lax.all_gather(grad_rows, MP, axis=0, tiled=True)
    product = jnp.dot(piece, weight_t, preferred_element_type=jnp.float32)
    d_weight = lax.dot_general(piece, full_rows, CONTRACT_ROWS, preferred_element_type=jnp.float32)
    return (product, d_weight)


def back_in(d_full, weight):
    return lax.psum_scatter(
        lax.dot_general(d_full, weight, CONTRACT_LAST, preferred_element_type=jnp.float32).astype(
            jnp.bfloat16
        ),
        MP,
        scatter_dimension=0,
        tiled=True,
    ).astype(jnp.float32)


def attend_forward(query, key_rows, value_rows, keep, forms):
    scores = jnp.einsum(forms[0], query, key_rows, preferred_element_type=jnp.float32) * HD ** (
        -0.5
    )
    scores = jnp.where(keep, scores, NEG_LARGE)
    peak = jnp.max(scores, -1, keepdims=True)
    expd = jnp.exp(scores - peak)
    total = jnp.sum(expd, -1, keepdims=True)
    probs = (expd / total).astype(jnp.bfloat16)
    mixed = jnp.einsum(forms[1], probs, value_rows, preferred_element_type=jnp.float32)
    return (mixed, peak + jnp.log(total))


def attend_backward(query, key_rows, value_rows, keep, forms, logsum, d_mixed):
    scores = jnp.einsum(forms[0], query, key_rows, preferred_element_type=jnp.float32) * HD ** (
        -0.5
    )
    scores = jnp.where(keep, scores, NEG_LARGE)
    probs_full = jnp.exp(scores - logsum)
    probs = probs_full.astype(jnp.bfloat16)
    d_value = jnp.einsum(forms[2], probs, d_mixed, preferred_element_type=jnp.float32)
    d_probs = jnp.einsum(forms[0], d_mixed, value_rows, preferred_element_type=jnp.float32)
    offset = jnp.sum(d_probs * probs_full, -1, keepdims=True)
    d_scores = (probs_full * (d_probs - offset) * HD ** (-0.5)).astype(jnp.bfloat16)
    d_query = jnp.einsum(forms[1], d_scores, key_rows, preferred_element_type=jnp.float32)
    d_key = jnp.einsum(forms[2], d_scores, query, preferred_element_type=jnp.float32)
    return (d_query, d_key, d_value)


def attention_forward(x, index, mods, kind, setup):
    weight = setup[AT_ATTN][index]
    heads = weight.shape[1]
    width_local = heads * HD
    biases = setup[AT_PARTS][ATTN_BIAS][index]
    part = setup[AT_PART]
    forms = attention_forms(kind)
    query_bias = own_slice(biases[0], part, width_local).reshape(heads, HD)
    value_bias = own_slice(biases[1], part, width_local).reshape(heads, HD)
    if kind == AT_CROSS:
        projected, gathered = project_in(
            x.astype(jnp.bfloat16), weight[:, :, 0, :].reshape(D, width_local)
        )
        query = projected.reshape(-1, heads, HD) + query_bias
        context = setup[AT_CONTEXT]
        key_rows = jnp.einsum(
            "cd,dhe->che", context, weight[:, :, 1, :], preferred_element_type=jnp.float32
        )
        value_rows = (
            jnp.einsum(
                "cd,dhe->che", context, weight[:, :, 2, :], preferred_element_type=jnp.float32
            )
            + value_bias
        )
    else:
        source = modulate(x, mods[0], mods[1])
        projected, gathered = project_in(
            source.astype(jnp.bfloat16), weight[:, :, :3, :].reshape(D, 3 * width_local)
        )
        projected = projected.reshape(FR, PM, heads, 3, HD)
        query = projected[:, :, :, 0] + query_bias
        key_rows = projected[:, :, :, 1]
        value_rows = projected[:, :, :, 2] + value_bias
    query = query.astype(jnp.bfloat16)
    key_rows = key_rows.astype(jnp.bfloat16)
    value_rows = value_rows.astype(jnp.bfloat16)
    mixed, logsum = attend_forward(query, key_rows, value_rows, setup[AT_KEEP][kind], forms)
    mixed = mixed.reshape(-1, width_local).astype(jnp.bfloat16)
    branch = project_out(mixed, weight[:, :, 3, :].reshape(D, width_local)) + biases[2]
    saved = {
        AT_INPUT: x,
        AT_GATHERED: gathered,
        AT_QUERY: query,
        AT_KEY_ROWS: key_rows,
        AT_VALUE_ROWS: value_rows,
        AT_LOGSUM: logsum,
        AT_MIXED: mixed,
        AT_BRANCH: branch,
    }
    if kind == AT_CROSS:
        return (x + branch, saved)
    return (x + mods[2] * branch, saved)


def attention_backward(grad_x, index, mods, kind, saved, setup):
    weight = setup[AT_ATTN][index]
    heads = weight.shape[1]
    width_local = heads * HD
    part = setup[AT_PART]
    forms = attention_forms(kind)
    query = saved[AT_QUERY]
    if kind == AT_CROSS:
        gate_vec = 1.0
        d_gate = None
    else:
        gate_vec = mods[2]
        d_gate = jnp.sum(grad_x * saved[AT_BRANCH], 0)
    d_branch = (gate_vec * grad_x).astype(jnp.bfloat16)
    d_out_bias = jnp.sum(d_branch.astype(jnp.float32), 0)
    d_mixed, d_out_weight = back_out(
        d_branch, saved[AT_MIXED], weight[:, :, 3, :].reshape(D, width_local)
    )
    d_mixed = d_mixed.astype(jnp.bfloat16).reshape(query.shape)
    d_query, d_key, d_value = attend_backward(
        query,
        saved[AT_KEY_ROWS],
        saved[AT_VALUE_ROWS],
        setup[AT_KEEP][kind],
        forms,
        saved[AT_LOGSUM],
        d_mixed,
    )
    d_query = d_query.reshape(-1, heads, HD).astype(jnp.bfloat16)
    d_key = d_key.reshape(-1, heads, HD).astype(jnp.bfloat16)
    d_value = d_value.reshape(-1, heads, HD).astype(jnp.bfloat16)
    d_query_bias = jnp.sum(d_query.astype(jnp.float32), 0).reshape(-1)
    d_value_bias = jnp.sum(d_value.astype(jnp.float32), 0).reshape(-1)
    if kind == AT_CROSS:
        context = setup[AT_CONTEXT]
        d_query_weight = lax.dot_general(
            saved[AT_GATHERED],
            d_query.reshape(-1, width_local),
            CONTRACT_ROWS,
            preferred_element_type=jnp.float32,
        ).reshape(D, heads, 1, HD)
        d_key_weight = jnp.einsum("cd,che->dhe", context, d_key, preferred_element_type=jnp.float32)
        d_value_weight = jnp.einsum(
            "cd,che->dhe", context, d_value, preferred_element_type=jnp.float32
        )
        d_in = jnp.concatenate(
            [d_query_weight, d_key_weight[:, :, None], d_value_weight[:, :, None]], 2
        )
        d_context = jnp.einsum(
            "che,dhe->cd", d_key, weight[:, :, 1, :], preferred_element_type=jnp.float32
        ) + jnp.einsum(
            "che,dhe->cd", d_value, weight[:, :, 2, :], preferred_element_type=jnp.float32
        )
        grad_x = grad_x + back_in(
            d_query.reshape(-1, width_local), weight[:, :, 0, :].reshape(D, width_local)
        )
        mod_grads = None
    else:
        d_proj = jnp.stack([d_query, d_key, d_value], 2).reshape(-1, 3 * width_local)
        d_in = lax.dot_general(
            saved[AT_GATHERED], d_proj, CONTRACT_ROWS, preferred_element_type=jnp.float32
        ).reshape(D, heads, 3, HD)
        d_source = back_in(d_proj, weight[:, :, :3, :].reshape(D, 3 * width_local))
        unused, norm_pull = jax.vjp(modulate, saved[AT_INPUT], mods[0], mods[1])
        d_input, d_shift, d_scale = norm_pull(d_source)
        grad_x = grad_x + d_input
        mod_grads = (d_shift, d_scale, d_gate)
        d_context = None
    d_weight = jnp.concatenate([d_in, d_out_weight.reshape(D, heads, 1, HD)], 2)
    d_bias = jnp.stack([placed(d_query_bias, part, D), placed(d_value_bias, part, D), d_out_bias])
    return (grad_x, d_weight, d_bias, mod_grads, d_context)


def ffn_forward(x, index, mods, setup):
    weight_in = setup[AT_FFN][index, 0]
    weight_out = setup[AT_FFN][index, 1]
    source = modulate(x, mods[3], mods[4])
    pre, gathered = project_in(source.astype(jnp.bfloat16), weight_in)
    pre = pre + own_slice(setup[AT_PARTS][FFN_BIAS_ONE][index], setup[AT_PART], weight_in.shape[1])
    hidden = gelu_tanh(pre).astype(jnp.bfloat16)
    branch = project_out(hidden, weight_out) + setup[AT_PARTS][FFN_BIAS_TWO][index]
    saved = {AT_INPUT: x, AT_GATHERED: gathered, AT_PRE: pre, AT_HIDDEN: hidden, AT_BRANCH: branch}
    return (x + mods[5] * branch, saved)


def ffn_backward(grad_x, index, mods, saved, setup):
    weight_in = setup[AT_FFN][index, 0]
    weight_out = setup[AT_FFN][index, 1]
    d_gate = jnp.sum(grad_x * saved[AT_BRANCH], 0)
    d_branch = (mods[5] * grad_x).astype(jnp.bfloat16)
    d_bias_two = jnp.sum(d_branch.astype(jnp.float32), 0)
    d_hidden, d_weight_out = back_out(d_branch, saved[AT_HIDDEN], weight_out)
    unused, gelu_pull = jax.vjp(gelu_tanh, saved[AT_PRE])
    d_pre = gelu_pull(d_hidden)[0].astype(jnp.bfloat16)
    d_bias_one = jnp.sum(d_pre.astype(jnp.float32), 0)
    d_weight_in = lax.dot_general(
        saved[AT_GATHERED], d_pre, CONTRACT_ROWS, preferred_element_type=jnp.float32
    )
    d_source = back_in(d_pre, weight_in)
    unused, norm_pull = jax.vjp(modulate, saved[AT_INPUT], mods[3], mods[4])
    d_input, d_shift, d_scale = norm_pull(d_source)
    biases = (placed(d_bias_one, setup[AT_PART], FF), d_bias_two)
    return (
        grad_x + d_input,
        jnp.stack([d_weight_in, d_weight_out]),
        biases,
        (d_shift, d_scale, d_gate),
    )


def block_forward(x, kind, mods, setup):
    index = 0 if kind == AT_SPACE else 1
    x, first = attention_forward(x, index, mods, kind, setup)
    second = None
    if kind == AT_SPACE:
        x, second = attention_forward(x, 2, mods, AT_CROSS, setup)
    x, third = ffn_forward(x, index, mods, setup)
    return (x, (first, second, third))


def block_backward(grad_x, kind, mods, saved, setup):
    index = 0 if kind == AT_SPACE else 1
    first, second, third = saved
    grad_x, d_ffn, d_ffn_bias, ffn_mods = ffn_backward(grad_x, index, mods, third, setup)
    cross_part = None
    if kind == AT_SPACE:
        grad_x, d_cross, d_cross_bias, unused, d_context = attention_backward(
            grad_x, 2, mods, AT_CROSS, second, setup
        )
        cross_part = (d_cross, d_cross_bias, d_context)
    grad_x, d_attn, d_attn_bias, attn_mods, unused = attention_backward(
        grad_x, index, mods, kind, first, setup
    )
    d_mods = jnp.stack(list(attn_mods) + list(ffn_mods))
    return (grad_x, (d_attn, d_attn_bias, d_ffn, d_ffn_bias, d_mods), cross_part)


def adam_update(weight, first, second, ema, grad, rate):
    first_new = BETA_FIRST * first + (1.0 - BETA_FIRST) * grad
    second_new = BETA_SECOND * second + (1.0 - BETA_SECOND) * grad * grad
    corr_one = 1.0 - BETA_FIRST**STEP
    corr_two = 1.0 - BETA_SECOND**STEP
    weight_new = weight - rate * (
        first_new / corr_one / (jnp.sqrt(second_new / corr_two) + ADAM_EPSILON)
        + WEIGHT_DECAY * weight
    )
    return (first_new, second_new, weight_new, EMA_DECAY * ema + (1.0 - EMA_DECAY) * weight_new)


def per_device(
    latents,
    noise,
    caption,
    caption_lens,
    timesteps,
    grid_hw,
    frame_counts,
    attn_mats,
    ffn_mats,
    embed_mats,
    vectors,
    attn_first,
    ffn_first,
    embed_first,
    vector_first,
    attn_second,
    ffn_second,
    embed_second,
    vector_second,
    attn_ema,
    ffn_ema,
    embed_ema,
    vector_ema,
):
    group = lax.axis_index(DP)
    part = lax.axis_index(MP)
    mp_size = lax.axis_size(MP)
    rows = latents.shape[1]
    heads = HEADS // mp_size
    width_local = D // mp_size
    attn_all, ffn_all, embed_all = (
        lax.all_gather(attn_mats.astype(jnp.bfloat16), DP, axis=1, tiled=True),
        lax.all_gather(ffn_mats.astype(jnp.bfloat16), DP, axis=2, tiled=True),
        lax.all_gather(embed_mats.astype(jnp.bfloat16), DP, axis=0, tiled=True),
    )
    parts = unpack(vectors)
    pick = jnp.arange(timesteps.shape[0], dtype=jnp.int32) == group

    def select(values):
        return jnp.sum(jnp.where(pick, values, 0))

    tstep = select(timesteps)
    cap_len = select(caption_lens)
    height = select(grid_hw[:, 0])
    width_grid = select(grid_hw[:, 1])
    frames = select(frame_counts)
    count = jnp.sum(frame_counts * grid_hw[:, 0] * grid_hw[:, 1]).astype(jnp.float32)
    betas, cumul = roster()
    step_ids = jnp.arange(1000, dtype=jnp.int32)
    alpha_bar = jnp.sum(jnp.where(step_ids == tstep, cumul, 0.0))
    alpha_prev = jnp.sum(jnp.where(step_ids == tstep - 1, cumul, 0.0))
    beta_now = jnp.sum(jnp.where(step_ids == tstep, betas, 0.0))
    t_one = embed_all[:TFREQ]
    c_one = embed_all[TFREQ : TFREQ + TXT]
    t_two = embed_all[TFREQ + TXT : TFREQ + TXT + D]
    c_two = embed_all[TFREQ + TXT + D : TFREQ + TXT + 2 * D]
    t_mod = embed_all[TFREQ + TXT + 2 * D :]
    freq = waves(tstep.astype(jnp.float32), TFREQ).astype(jnp.bfloat16)
    t_pre = jnp.dot(freq, t_one, preferred_element_type=jnp.float32) + own_slice(
        parts[T_BIAS_ONE], part, width_local
    )
    t_hidden = jax.nn.silu(t_pre).astype(jnp.bfloat16)
    t_part = jnp.dot(t_two, t_hidden, preferred_element_type=jnp.float32)
    caption_rows = caption[0]
    c_pre = jnp.dot(caption_rows, c_one, preferred_element_type=jnp.float32) + own_slice(
        parts[C_BIAS_ONE], part, width_local
    )
    c_hidden = gelu_tanh(c_pre).astype(jnp.bfloat16)
    c_part = lax.dot_general(c_hidden, c_two, CONTRACT_LAST, preferred_element_type=jnp.float32)
    t_sum, c_sum = (
        lax.psum(t_part.astype(jnp.bfloat16), MP).astype(jnp.float32),
        lax.psum(c_part.astype(jnp.bfloat16), MP).astype(jnp.float32),
    )
    t_emb = t_sum + parts[T_BIAS_TWO]
    context = (c_sum + parts[C_BIAS_TWO]).astype(jnp.bfloat16)
    t_emb_local = own_slice(t_emb, part, width_local)
    silu_local = jax.nn.silu(t_emb_local).astype(jnp.bfloat16)
    t_mod_vec = (
        lax.psum(jnp.dot(t_mod, silu_local, preferred_element_type=jnp.float32), MP)
        + parts[T_BIAS_MOD]
    )
    token_ids = part * rows + jnp.arange(rows, dtype=jnp.int32)
    frame_slot = token_ids // PM
    patch_slot = token_ids % PM
    area = height * width_grid
    shifted = patch_slot - (PM - area)
    valid = (frame_slot >= FR - frames) & (patch_slot >= PM - area)
    setup = {
        AT_ATTN: attn_all.reshape(3, D, heads, 4, HD),
        AT_FFN: ffn_all,
        AT_PARTS: parts,
        AT_PART: part,
        AT_CONTEXT: context,
        AT_KEEP: {
            AT_SPACE: (jnp.arange(PM, dtype=jnp.int32) >= PM - area).reshape(1, 1, 1, PM),
            AT_TIME: (jnp.arange(FR, dtype=jnp.int32) >= FR - frames).reshape(1, 1, 1, FR),
            AT_CROSS: (jnp.arange(CAP, dtype=jnp.int32) < cap_len).reshape(1, 1, CAP),
        },
    }
    noisy = jnp.sqrt(alpha_bar) * latents[0] + jnp.sqrt(1.0 - alpha_bar) * noise[0]
    noisy_low = noisy.astype(jnp.bfloat16)
    position = jnp.concatenate(
        [
            waves((shifted // width_grid).astype(jnp.float32), D // 2),
            waves((shifted % width_grid).astype(jnp.float32), D // 2),
        ],
        -1,
    )
    x = jnp.dot(
        noisy_low, parts[PATCH_W].astype(jnp.bfloat16), preferred_element_type=jnp.float32
    )
    x = x + parts[PATCH_B] + position
    tables = parts[TABLES] + t_mod_vec.reshape(1, 6, D)
    x, saved_space = block_forward(x, AT_SPACE, tables[0], setup)
    x = x + waves((frame_slot - (FR - frames)).astype(jnp.float32), D)
    x, saved_time = block_forward(x, AT_TIME, tables[1], setup)
    final_mods = parts[FINAL_TABLE] + t_emb
    final_source = modulate(x, final_mods[0], final_mods[1]).astype(jnp.bfloat16)
    final_low = parts[FINAL_W].astype(jnp.bfloat16)
    output = (
        lax.dot_general(final_source, final_low, CONTRACT_LAST, preferred_element_type=jnp.float32)
        + parts[FINAL_B]
    )
    frozen = output[:, :CIN]

    def shard_loss(values):
        losses = token_losses(
            values, frozen, latents[0], noise[0], (noisy, alpha_bar, alpha_prev, beta_now)
        )
        return jnp.sum(jnp.where(valid, losses, 0.0))

    loss_part, loss_pull = jax.vjp(shard_loss, output)
    loss_total = lax.psum(loss_part, (DP, MP))
    d_output = loss_pull(1.0 / count)[0].astype(jnp.bfloat16)
    d_final_w = lax.dot_general(
        d_output, final_source, CONTRACT_ROWS, preferred_element_type=jnp.float32
    )
    d_final_b = jnp.sum(d_output.astype(jnp.float32), 0)
    d_final_source = jnp.dot(d_output, final_low, preferred_element_type=jnp.float32)
    unused, final_pull = jax.vjp(modulate, x, final_mods[0], final_mods[1])
    grad_x, d_final_shift, d_final_scale = final_pull(d_final_source)
    grad_x, time_grads, unused = block_backward(grad_x, AT_TIME, tables[1], saved_time, setup)
    grad_x, space_grads, cross_grads = block_backward(
        grad_x, AT_SPACE, tables[0], saved_space, setup
    )
    d_patch = grad_x.astype(jnp.bfloat16)
    d_patch_b = jnp.sum(d_patch.astype(jnp.float32), 0)
    d_patch_w = lax.dot_general(
        noisy_low, d_patch, CONTRACT_ROWS, preferred_element_type=jnp.float32
    )
    d_mod_part = space_grads[4].reshape(-1) + time_grads[4].reshape(-1)
    d_temb_part = d_final_shift + d_final_scale
    d_mod_vec, d_temb_sum, d_context = (
        lax.psum(d_mod_part.astype(jnp.bfloat16), MP).astype(jnp.float32),
        lax.psum(d_temb_part.astype(jnp.bfloat16), MP).astype(jnp.float32),
        lax.psum(cross_grads[2].astype(jnp.bfloat16), MP).astype(jnp.float32),
    )
    d_t_mod = jnp.outer(d_mod_vec, silu_local.astype(jnp.float32))
    d_silu_local = jnp.dot(d_mod_vec, t_mod, preferred_element_type=jnp.float32)
    unused, silu_pull = jax.vjp(jax.nn.silu, t_emb_local)
    d_temb_local = silu_pull(d_silu_local)[0]
    d_temb = d_temb_sum + lax.all_gather(d_temb_local, MP, axis=0, tiled=True)
    d_t_two = jnp.outer(d_temb, t_hidden.astype(jnp.float32))
    d_t_hidden = jnp.dot(d_temb, t_two, preferred_element_type=jnp.float32)
    unused, pre_pull = jax.vjp(jax.nn.silu, t_pre)
    d_t_pre = pre_pull(d_t_hidden)[0]
    d_t_one = jnp.outer(freq.astype(jnp.float32), d_t_pre)
    d_context = d_context.astype(jnp.bfloat16)
    d_c_bias_two = jnp.sum(d_context.astype(jnp.float32), 0) * (part == 0).astype(jnp.float32)
    d_c_two = lax.dot_general(
        d_context, c_hidden, CONTRACT_ROWS, preferred_element_type=jnp.float32
    )
    d_c_hidden = jnp.dot(d_context, c_two, preferred_element_type=jnp.float32)
    unused, cap_pull = jax.vjp(gelu_tanh, c_pre)
    d_c_pre = cap_pull(d_c_hidden)[0].astype(jnp.bfloat16)
    d_c_one = lax.dot_general(
        caption_rows, d_c_pre, CONTRACT_ROWS, preferred_element_type=jnp.float32
    )
    d_c_bias_one = jnp.sum(d_c_pre.astype(jnp.float32), 0)
    d_attn = jnp.stack([space_grads[0], time_grads[0], cross_grads[0]]).reshape(
        3, D, heads * 4 * HD
    )
    d_ffn = jnp.stack([space_grads[2], time_grads[2]])
    d_embed = jnp.concatenate([d_t_one, d_c_one, d_t_two, d_c_two, d_t_mod], 0)
    vector_grads = {
        PATCH_W: d_patch_w,
        PATCH_B: d_patch_b,
        FINAL_W: d_final_w,
        FINAL_B: d_final_b,
        T_BIAS_ONE: placed(d_t_pre, part, D),
        T_BIAS_TWO: d_temb_part + placed(d_temb_local, part, D),
        T_BIAS_MOD: d_mod_part,
        C_BIAS_ONE: placed(d_c_bias_one, part, D),
        C_BIAS_TWO: d_c_bias_two,
        ATTN_BIAS: jnp.stack([space_grads[1], time_grads[1], cross_grads[1]]),
        FFN_BIAS_ONE: jnp.stack([space_grads[3][0], time_grads[3][0]]),
        FFN_BIAS_TWO: jnp.stack([space_grads[3][1], time_grads[3][1]]),
        TABLES: jnp.stack([space_grads[4], time_grads[4]]),
        FINAL_TABLE: jnp.stack([d_final_shift, d_final_scale]),
    }
    vector_grad = jnp.concatenate(
        [vector_grads[label].reshape(-1) for label, extent in vector_parts()]
    )
    g_attn, g_ffn, g_embed = (
        lax.psum_scatter(d_attn.astype(jnp.bfloat16), DP, scatter_dimension=1, tiled=True).astype(
            jnp.float32
        ),
        lax.psum_scatter(d_ffn.astype(jnp.bfloat16), DP, scatter_dimension=2, tiled=True).astype(
            jnp.float32
        ),
        lax.psum_scatter(
            d_embed.astype(jnp.bfloat16), DP, scatter_dimension=0, tiled=True
        ).astype(jnp.float32),
    )
    g_vector = lax.psum(vector_grad, (DP, MP))
    matrix_squares = jnp.sum(g_attn * g_attn) + jnp.sum(g_ffn * g_ffn) + jnp.sum(g_embed * g_embed)
    squares = lax.psum(matrix_squares, (DP, MP)) + jnp.sum(g_vector * g_vector)
    grad_norm = jnp.sqrt(squares)
    factor = CLIP_NORM / (grad_norm + 1e-06)
    new_attn = adam_update(
        attn_mats, attn_first, attn_second, attn_ema, g_attn * factor, LEARN_RATE
    )
    new_ffn = adam_update(ffn_mats, ffn_first, ffn_second, ffn_ema, g_ffn * factor, LEARN_RATE)
    new_embed = adam_update(
        embed_mats, embed_first, embed_second, embed_ema, g_embed * factor, LEARN_RATE
    )
    new_vector = adam_update(
        vectors, vector_first, vector_second, vector_ema, g_vector * factor, VECTOR_RATE
    )
    return (
        loss_total,
        count,
        grad_norm,
        new_attn[0],
        new_ffn[0],
        new_embed[0],
        new_vector[0],
        new_attn[1],
        new_ffn[1],
        new_embed[1],
        new_vector[1],
        new_attn[2],
        new_ffn[2],
        new_embed[2],
        new_vector[2],
        new_attn[3],
        new_ffn[3],
        new_embed[3],
        new_vector[3],
    )


SPAN = 4 * HD
EMB_ALL = TFREQ + TXT + 8 * D
EMB_LOCAL = EMB_ALL // 8
MESH = pl.DeviceIdType.MESH
BLOCK = 144
BIG = 58 * 2**20
PIECES = {1: 2, 2: 2}


class Chips:
    def __init__(self):
        dp = lax.axis_index(DP)
        mp = lax.axis_index(MP)
        self.z, self.x = dp // 2, dp % 2
        self.y, self.c = mp // 2, mp % 2

    def z_at(self, j):
        z = self.z
        return (z, z + 1 - 2 * (z % 2), z + 2 - 4 * (z // 2), 3 - z)[j]

    def dp_at(self, jz, jx):
        return self.z_at(jz) * 2 + (1 - self.x if jx else self.x)

    def mp_at(self, jy, jc):
        return (1 - self.y if jy else self.y) * 2 + (1 - self.c if jc else self.c)

    def peer_x(self):
        return {DP: self.dp_at(0, 1)}

    def peer_y(self):
        return {MP: self.mp_at(1, 0)}

    def peer_core(self):
        return {MP: self.mp_at(0, 1)}

    def peer_z(self, j):
        return {DP: self.dp_at(j, 0)}

    def greet(self):
        barrier = pltpu.get_barrier_semaphore()
        peers = [self.peer_x(), self.peer_y(), self.peer_core()]
        peers += [self.peer_z(j) for j in (1, 2, 3)]
        for peer in peers:
            pl.semaphore_signal(barrier, inc=1, device_id=peer, device_id_type=MESH)
        pl.semaphore_wait(barrier, len(peers))


class Work:
    def __init__(self, chips, send, recv):
        self.chips, self.send, self.recv = chips, send, recv
        self.started = []

    def start(self, src, dst, slot, peer):
        def copy():
            return pltpu.make_async_remote_copy(
                src_ref=src(),
                dst_ref=dst(),
                send_sem=self.send.at[slot],
                recv_sem=self.recv.at[slot],
                device_id=peer(),
                device_id_type=MESH,
            )

        copy().start()
        self.started.append(copy)

    def arrived(self, dst, slot):
        pltpu.make_async_remote_copy(
            src_ref=dst,
            dst_ref=dst,
            send_sem=self.send.at[slot],
            recv_sem=self.recv.at[slot],
            device_id=self.chips.peer_core(),
            device_id_type=MESH,
        ).wait_recv()

    def finish(self):
        for copy in self.started:
            copy().wait_send()


class Gather(Work):
    def __init__(self, chips, shard, full, row, size, send, recv, local):
        super().__init__(chips, send, recv)
        self.source, self.full, self.local = shard, full, local
        self.rows = pl.ds(row, size)

    def shard(self):
        return self.source.at[:, self.rows]

    def block(self, jy, jz, jx, jc=0):
        chips = self.chips
        return self.full.at[:, chips.mp_at(jy, jc), chips.dp_at(jz, jx), self.rows]

    def arrive(self, jy, jz, jx, jc=0):
        self.arrived(self.block(jy, jz, jx, jc), jc * 16 + jy * 8 + jz * 2 + jx)

    def pass_on(self, place, slot, peer):
        self.start(lambda: self.block(*place), lambda: self.block(*place), slot, peer)

    def core(self, jy, jz, jx):
        self.pass_on((jy, jz, jx), 16 + jy * 8 + jz * 2 + jx, self.chips.peer_core)

    def own(self):
        return pltpu.make_async_copy(self.shard(), self.block(0, 0, 0), self.local)

    def begin(self):
        chips = self.chips
        shard, block = self.shard, (lambda: self.block(0, 0, 0))
        self.start(shard, block, 1, chips.peer_x)
        self.start(shard, block, 8, chips.peer_y)
        for j in (1, 2, 3):
            self.start(shard, block, 2 * j, functools.partial(chips.peer_z, j))
        self.start(shard, block, 16, chips.peer_core)
        self.own().start()

    def second(self, jz):
        self.arrive(0, jz, 0)
        self.pass_on((0, jz, 0), jz * 2 + 1, self.chips.peer_x)
        self.pass_on((0, jz, 0), jz * 2 + 8, self.chips.peer_y)
        self.core(0, jz, 0)

    def third(self, jz):
        place = (0, jz, 1) if jz < 2 else (1, jz, 0)
        self.arrive(*place)
        self.pass_on(place, 9 + jz * 2, self.chips.peer_y if jz < 2 else self.chips.peer_x)
        self.core(*place)

    def fourth(self, jz):
        place = (1, jz, 0) if jz < 2 else (0, jz, 1)
        self.arrive(*place)
        self.core(*place)

    def fifth(self, jz):
        self.arrive(1, jz, 1)
        self.core(1, jz, 1)

    def last(self):
        self.own().wait()
        for jy in range(2):
            for jz in range(4):
                for jx in range(2):
                    self.arrive(jy, jz, jx, 1)

    def steps(self):
        order = (0, 2, 1, 3)
        parts = [[self.begin]]
        parts.append([functools.partial(self.second, j) for j in (1, 2, 3)])
        parts.append([functools.partial(self.third, j) for j in order])
        parts.append([functools.partial(self.fourth, j) for j in order])
        parts.append([functools.partial(self.fifth, j) for j in order])
        parts.append([self.last])
        return parts


GATHER_SEMS = [
    pltpu.SemaphoreType.DMA((32,)),
    pltpu.SemaphoreType.DMA((32,)),
    pltpu.SemaphoreType.DMA,
]


class Ticks:
    def __init__(self, steps, spots):
        self.step = pl.program_id(0)
        total = 4 * spots
        self.table = [[] for unused in range(total)]
        count = len(steps)
        for i, step in enumerate(steps):
            at = 0 if i == 0 else total - 1 if i == count - 1 else 1 + (i - 1) * (total - 2) // (count - 2)
            self.table[at].append(step)
        self.spots = spots

    def __call__(self, spot):
        for turn in range(4):
            todo = self.table[turn * self.spots + spot]
            if todo:

                @pl.when(self.step == turn)
                def run(todo=todo):
                    for step in todo:
                        step()


def no_ticks(spot):
    return None


def woven(plans):
    order = [step for plan in plans for step in plan[0]]
    plans = [plan[1:] for plan in plans]
    deep = max(len(plan) for plan in plans)
    for turn in range(len(plans) + deep - 1):
        for i, plan in enumerate(plans):
            if 0 <= turn - i < len(plan):
                order += plan[turn - i]
    return order


ROWS = {1: [144], 2: [80, 64], 3: [48, 48, 48]}
GATHER_PIECES = {1: 3, 2: 3}


def gather_steps(chips, shard, full, sems):
    pieces = len(sems) // 3
    sizes = ROWS[pieces]
    works = [
        Gather(chips, shard, full, sum(sizes[:i]), sizes[i], *sems[3 * i : 3 * i + 3])
        for i in range(pieces)
    ]

    def finish():
        for work in works:
            work.finish()

    return woven([work.steps() for work in works]) + [finish]


def entered(chips, steps, begins, spots):
    def enter():
        chips.greet()
        for begin in steps[:begins]:
            begin()

    return Ticks([enter] + steps[begins:], spots)


def gather_ticks(refs, spots, unused):
    chips = Chips()
    return entered(chips, gather_steps(chips, refs[0], refs[1], refs[2:]), len(refs) // 3, spots)


def gather_kernel(shard, full, *sems):
    chips = Chips()
    chips.greet()
    for step in gather_steps(chips, shard, full, sems):
        step()


def gather_all(shard, ident):
    return pl.pallas_call(
        gather_kernel,
        out_shape=jax.ShapeDtypeStruct((shard.shape[0], 4, 8) + shard.shape[1:], shard.dtype),
        in_specs=[pl.BlockSpec(memory_space=pl.ANY)],
        out_specs=pl.BlockSpec(memory_space=pl.ANY),
        scratch_shapes=GATHER_SEMS * GATHER_PIECES[shard.shape[0]],
        compiler_params=pltpu.CompilerParams(collective_id=ident, has_side_effects=True),
    )(shard)


def sorted_columns(value):
    return jnp.concatenate(
        [value[:, (h * 4 + k) * HD : (h * 4 + k + 1) * HD] for k in range(4) for h in range(4)], 1
    )


def unsorted_columns(value):
    return jnp.concatenate(
        [value[:, (k * 4 + h) * HD : (k * 4 + h + 1) * HD] for h in range(4) for k in range(4)], 1
    )


def sort_kernel(mats, out):
    out[0] = sorted_columns(mats[0]).astype(jnp.bfloat16)


def sort_panels(mats):
    spec = pl.BlockSpec((1,) + mats.shape[1:], lambda i: (i, 0, 0))
    return pl.pallas_call(
        sort_kernel,
        grid=(3,),
        in_specs=[spec],
        out_specs=spec,
        out_shape=jax.ShapeDtypeStruct(mats.shape, jnp.bfloat16),
    )(mats)


class Scatter(Work):
    def __init__(self, chips, full, total, m, row, near, far, own, send, recv, load):
        super().__init__(chips, send, recv)
        self.sorted = full.shape[0] == 1
        self.full, self.total = full, total
        self.m, self.row, self.size = m, row, near.shape[1]
        self.near, self.far, self.own, self.load = near, far, own, load
        diagonal = [(1, jz, 1) for jz in (0, 2, 1, 3)]
        straight = [(1, jz, 0) if jz < 2 else (0, jz, 1) for jz in (0, 2, 1, 3)]
        bent = [(0, jz, 1) if jz < 2 else (1, jz, 0) for jz in (0, 2, 1, 3)]
        column = [(0, jz, 0) for jz in (2, 3, 1, 0)]
        self.order = diagonal + straight + bent + column
        self.turns = {jy * 8 + jz * 2 + jx: i for i, (jy, jz, jx) in enumerate(self.order)}

    def block(self, jy, jz, jx, jc):
        chips = self.chips
        return self.full.at[
            self.m, chips.mp_at(jy, jc), chips.dp_at(jz, jx), pl.ds(self.row, self.size)
        ]

    def fetch(self, turn):
        buffer = turn % self.own.shape[0]
        return pltpu.make_async_copy(
            self.block(*self.order[turn], 0), self.own.at[buffer], self.load.at[buffer]
        )

    def begin(self):
        for place in self.order:
            slot = place[0] * 8 + place[1] * 2 + place[2]
            self.start(
                functools.partial(self.block, *place, 1),
                functools.partial(lambda at: self.near.at[at], slot),
                slot,
                self.chips.peer_core,
            )
        for turn in range(self.own.shape[0]):
            self.fetch(turn).start()

    def add(self, slot, others):
        turn, near, own = self.turns[slot], self.near, self.own
        buffer = turn % own.shape[0]
        self.fetch(turn).wait()
        self.arrived(near.at[slot], slot)

        def rows(i, carry):
            at = pl.ds(pl.multiple_of(i * 16, 16), 16)
            value = near[slot, at].astype(jnp.float32) + own[buffer, at].astype(jnp.float32)
            for index in others:
                value += self.far[index, at].astype(jnp.float32)
            near[slot, at] = value.astype(jnp.bfloat16)
            return carry

        lax.fori_loop(0, self.size // 16, rows, 0)
        if turn + own.shape[0] < 16:
            self.fetch(turn + own.shape[0]).start()

    def move(self, slot, index, where, peer):
        self.start(lambda: self.near.at[slot], lambda: self.far.at[index], where, peer)

    def along_x(self, slot, jz):
        self.move(slot, 4 + jz, 20 + jz, self.chips.peer_x)

    def along_y(self, slot, jz):
        self.move(slot, 8 + jz, 24 + jz, self.chips.peer_y)

    def diagonal(self, jz):
        slot = 9 + jz * 2
        self.add(slot, [])
        self.move(slot, jz, 16 + jz, self.chips.peer_y if jz < 2 else self.chips.peer_x)

    def straight(self, jz):
        slot = jz * 2 + (8 if jz < 2 else 1)
        self.add(slot, [])
        (self.along_y if jz < 2 else self.along_x)(slot, jz)

    def bent(self, jz):
        slot = jz * 2 + (1 if jz < 2 else 8)
        self.arrived(self.far.at[jz], 16 + jz)
        self.add(slot, [jz])
        (self.along_x if jz < 2 else self.along_y)(slot, jz)

    def column(self, jz):
        self.arrived(self.far.at[4 + jz], 20 + jz)
        self.arrived(self.far.at[8 + jz], 24 + jz)
        if jz:
            self.add(jz * 2, [4 + jz, 8 + jz])
            self.move(jz * 2, 11 + jz, 27 + jz, functools.partial(self.chips.peer_z, jz))

    def last(self):
        turn, near, own, far = 15, self.near, self.own, self.far
        buffer = turn % own.shape[0]
        self.fetch(turn).wait()
        self.arrived(near.at[0], 0)
        for jz in (2, 3, 1):
            self.arrived(far.at[11 + jz], 27 + jz)

        def rows(i, carry):
            at = pl.ds(pl.multiple_of(i * 16, 16), 16)
            value = near[0, at].astype(jnp.float32) + own[buffer, at].astype(jnp.float32)
            for index in (4, 8, 12, 13, 14):
                value += far[index, at].astype(jnp.float32)
            if self.sorted:
                value = unsorted_columns(value)
            self.total[self.m, pl.ds(pl.multiple_of(self.row + i * 16, 16), 16)] = value
            return carry

        lax.fori_loop(0, self.size // 16, rows, 0)

    def steps(self):
        order = (0, 2, 1, 3)
        parts = [[self.begin]]
        parts.append([functools.partial(self.diagonal, j) for j in order])
        parts[-1] += [functools.partial(self.straight, j) for j in order]
        parts.append([functools.partial(self.bent, j) for j in order])
        parts.append([functools.partial(self.column, j) for j in (2, 3, 1, 0)])
        parts.append([self.last])
        return parts


def chunks_of(k, pieces):
    sizes = ROWS[pieces]
    return [(m, sum(sizes[:i]), sizes[i]) for m in range(k) for i in range(pieces)]


def scatter_scratch(chunks):
    out = []
    for unused, unused_row, size in chunks:
        out += [
            pltpu.VMEM((16, size, 1152), jnp.bfloat16),
            pltpu.VMEM((15, size, 1152), jnp.bfloat16),
            pltpu.VMEM((4, size, 1152), jnp.bfloat16),
            pltpu.SemaphoreType.DMA((31,)),
            pltpu.SemaphoreType.DMA((31,)),
            pltpu.SemaphoreType.DMA((4,)),
        ]
    return out


def scatter_steps(chips, full, total, scratch, chunks):
    works = [
        Scatter(chips, full, total, m, row, *scratch[6 * i : 6 * i + 6])
        for i, (m, row, unused) in enumerate(chunks)
    ]

    def finish():
        for work in works:
            work.finish()

    return woven([work.steps() for work in works]) + [finish]


def scatter_ticks(refs, spots, chunks):
    chips = Chips()
    return entered(chips, scatter_steps(chips, refs[0], refs[1], refs[2:], chunks), len(chunks), spots)


def scatter_kernel(chunks, full, total, *scratch):
    chips = Chips()
    chips.greet()
    for step in scatter_steps(chips, full, total, scratch, chunks):
        step()


def scatter_one(full, ident, pieces=PIECES):
    k = full.shape[0]
    chunks = chunks_of(k, pieces[k])
    return pl.pallas_call(
        functools.partial(scatter_kernel, chunks),
        out_shape=jax.ShapeDtypeStruct((k,) + full.shape[3:], jnp.float32),
        in_specs=[pl.BlockSpec(memory_space=pl.ANY)],
        out_specs=pl.BlockSpec(memory_space=pltpu.VMEM),
        scratch_shapes=scatter_scratch(chunks),
        compiler_params=pltpu.CompilerParams(
            collective_id=ident, has_side_effects=True, vmem_limit_bytes=BIG
        ),
    )(full)


def normal_parts(x):
    centered = x - jnp.mean(x, -1, keepdims=True)
    inverse = lax.rsqrt(jnp.mean(centered * centered, -1, keepdims=True) + EPS_NORM)
    return centered * inverse, inverse


def normal_back(x, scale_vec, grad):
    normed, inverse = normal_parts(x)
    inner = grad * (1.0 + scale_vec)
    d_x = inverse * (
        inner
        - jnp.mean(inner, -1, keepdims=True)
        - normed * jnp.mean(inner * normed, -1, keepdims=True)
    )
    return d_x, jnp.sum(grad, 0, keepdims=True), jnp.sum(grad * normed, 0, keepdims=True)


def mxu(left, right, dims=(((1,), (0,)), ((), ()))):
    return lax.dot_general(left, right, dims, preferred_element_type=jnp.float32)


def padded_heads(pieces, before, after):
    rows = pieces[0].shape[0]
    parts = list(pieces)
    if before:
        parts.insert(0, jnp.zeros((rows, before), pieces[0].dtype))
    if after:
        parts.append(jnp.zeros((rows, after), pieces[0].dtype))
    return jnp.concatenate(parts, 1)


def head_forward(query, key_rows, value_rows, bias):
    scores = mxu(key_rows, query, CONTRACT_LAST) * HD ** (-0.5) + bias
    expd = jnp.exp(scores - jnp.max(scores, 0, keepdims=True))
    probs = (expd / jnp.sum(expd, 0, keepdims=True)).astype(jnp.bfloat16)
    return mxu(probs, value_rows, CONTRACT_ROWS)


def head_backward(query, key_rows, value_rows, bias, d_mixed):
    scores = mxu(key_rows, query, CONTRACT_LAST) * HD ** (-0.5) + bias
    expd = jnp.exp(scores - jnp.max(scores, 0, keepdims=True))
    probs = expd / jnp.sum(expd, 0, keepdims=True)
    d_value = mxu(probs.astype(jnp.bfloat16), d_mixed)
    d_probs = mxu(value_rows, d_mixed, CONTRACT_LAST)
    offset = jnp.sum(d_probs * probs, 0, keepdims=True)
    d_scores = (probs * (d_probs - offset) * HD ** (-0.5)).astype(jnp.bfloat16)
    d_query = mxu(d_scores, key_rows, CONTRACT_ROWS)
    d_key = mxu(d_scores, query)
    return d_query, d_key, d_value


def self_forward_kernel(tiles, tick, x, mods, bias, panel, mask, out, branch, source, proj, mixed, total):
    step = pl.program_id(0)
    rows = PM // tiles
    tick(0)

    @pl.when(step == 0)
    def first():
        normed, unused = normal_parts(x[...])
        source[...] = (normed * (1.0 + mods[1:2]) + mods[0:1]).astype(jnp.bfloat16)
        total[...] = jnp.zeros_like(total)

    values = mxu(source[...], panel[0, :, :896]) + bias[0]
    values = values.astype(jnp.bfloat16)
    proj[0] = values
    heads = []
    for h in range(4):
        tops = []
        for t in range(tiles):
            part = values[t * rows : (t + 1) * rows]
            at = h * HD
            tops.append(
                head_forward(
                    part[:, at : at + HD],
                    part[:, SPAN + at : SPAN + at + HD],
                    part[:, 2 * SPAN + at : 2 * SPAN + at + HD],
                    mask[...],
                )
            )
        heads.append(jnp.concatenate(tops, 0) if tiles > 1 else tops[0])
        tick(h + 1)
    packed = padded_heads(heads, 96, 0).astype(jnp.bfloat16)
    mixed[0] = packed
    total[...] += mxu(packed, panel[0, :, 768:], CONTRACT_LAST)

    @pl.when(step == 3)
    def last():
        value = total[...] + mods[6:7]
        branch[...] = value
        out[...] = x[...] + mods[2:3] * value

    tick(5)


def whole(shape):
    return pl.BlockSpec(shape, lambda i: (0,) * len(shape), pipeline_mode=pl.Buffered(1))


def slab(shape):
    return pl.BlockSpec((1,) + shape, lambda i: (i,) + (0,) * len(shape))


def grid_params(ident=None):
    if ident is None:
        return pltpu.CompilerParams(vmem_limit_bytes=BIG)
    return pltpu.CompilerParams(vmem_limit_bytes=BIG, collective_id=ident, has_side_effects=True)


def beside(kernel, ticks, spots, inputs, outputs, scratch, chunks):
    def run(*refs):
        ins, given = refs[:inputs], refs[inputs]
        outs, made = refs[inputs + 1 : inputs + 1 + outputs], refs[inputs + 1 + outputs]
        rest = refs[inputs + outputs + 2 :]
        kernel(ticks((given, made) + rest[scratch:], spots, chunks), *ins, *outs, *rest[:scratch])

    return run


def call_with(kernel, spots, operands, in_specs, out_specs, out_shape, scratch, given, ident):
    if given is None:
        return pl.pallas_call(
            functools.partial(kernel, no_ticks),
            grid=(4,),
            in_specs=in_specs,
            out_specs=out_specs,
            out_shape=out_shape,
            scratch_shapes=scratch,
            compiler_params=grid_params(),
        )(*operands)
    remote = pl.BlockSpec(memory_space=pl.ANY)
    k = given.shape[0]
    if given.ndim == 3:
        ticks, chunks, extra = gather_ticks, None, GATHER_SEMS * GATHER_PIECES[k]
        made = jax.ShapeDtypeStruct((k, 4, 8) + given.shape[1:], given.dtype)
        made_spec = remote
    else:
        ticks, chunks = scatter_ticks, chunks_of(k, PIECES[k])
        extra = scatter_scratch(chunks)
        made = jax.ShapeDtypeStruct((k,) + given.shape[3:], jnp.float32)
        made_spec = whole(made.shape)
    return pl.pallas_call(
        beside(kernel, ticks, spots, len(in_specs), len(out_specs), len(scratch), chunks),
        grid=(4,),
        in_specs=in_specs + [remote],
        out_specs=out_specs + [made_spec],
        out_shape=out_shape + [made],
        scratch_shapes=scratch + extra,
        compiler_params=grid_params(ident),
    )(*operands, given)


def self_forward(x, mods, bias, panels, mask, tiles, given=None, ident=None):
    f32, bf16 = jnp.float32, jnp.bfloat16
    rows = PM // tiles
    return call_with(
        functools.partial(self_forward_kernel, tiles),
        6,
        (x, mods, bias, panels, mask),
        [whole((PM, D)), whole((8, D)), slab((1, 896)), slab((D, D)), whole((rows, rows))],
        [whole((PM, D)), whole((PM, D)), whole((PM, D)), slab((PM, 896)), slab((PM, 384))],
        [
            jax.ShapeDtypeStruct((PM, D), f32),
            jax.ShapeDtypeStruct((PM, D), f32),
            jax.ShapeDtypeStruct((PM, D), bf16),
            jax.ShapeDtypeStruct((4, PM, 896), bf16),
            jax.ShapeDtypeStruct((4, PM, 384), bf16),
        ],
        [pltpu.VMEM((PM, D), f32)],
        given,
        ident,
    )


def self_backward_kernel(
    tiles, tick, x, grad, mods, branch, source, proj, mixed, panel, mask, out, sums, d_bias, d_panel, d_branch, total, pieces, held
):
    step = pl.program_id(0)
    rows = PM // tiles
    tick(0)

    @pl.when(step == 0)
    def first():
        value = grad[...]
        low = (mods[2:3] * value).astype(jnp.bfloat16)
        d_branch[...] = low
        sums[2:3] = jnp.sum(value * branch[...], 0, keepdims=True)
        sums[3:4] = jnp.sum(low.astype(jnp.float32), 0, keepdims=True)
        total[...] = jnp.zeros_like(total)

    low = d_branch[...]
    d_mixed = mxu(low, panel[0, :, 768:]).astype(jnp.bfloat16)
    held[...] = d_mixed
    pieces[:, 3 * SPAN :] = jnp.zeros((PM, 32), jnp.bfloat16)
    for h in range(4):
        at = h * HD
        for t in range(tiles):
            here = slice(t * rows, (t + 1) * rows)
            part = proj[0, here]
            three = head_backward(
                part[:, at : at + HD],
                part[:, SPAN + at : SPAN + at + HD],
                part[:, 2 * SPAN + at : 2 * SPAN + at + HD],
                mask[...],
                held[here, 96 + at : 96 + at + HD],
            )
            for index in range(3):
                base = index * SPAN + at
                pieces[here, base : base + HD] = three[index].astype(jnp.bfloat16)
        tick(h + 1)
    low = d_branch[...]
    d_proj = pieces[...]
    d_bias[0] = jnp.sum(d_proj.astype(jnp.float32), 0, keepdims=True)
    columns = lax.broadcasted_iota(jnp.int32, (1, 896), 1)
    kept = jnp.where(columns < 3 * SPAN, panel[0, :, :896], jnp.zeros((), jnp.bfloat16))
    total[...] += mxu(d_proj, kept, CONTRACT_LAST)
    src = source[...]
    d_panel[0, :, :768] = mxu(src, d_proj[:, :768], CONTRACT_ROWS).astype(jnp.bfloat16)
    tick(5)
    packed = mixed[0]
    d_panel[0, :, 768:896] = (
        mxu(src, d_proj[:, 768:], CONTRACT_ROWS) + mxu(low, packed[:, :128], CONTRACT_ROWS)
    ).astype(jnp.bfloat16)
    d_panel[0, :, 896:] = mxu(low, packed[:, 128:], CONTRACT_ROWS).astype(jnp.bfloat16)

    @pl.when(step == 3)
    def last():
        d_x, d_shift, d_scale = normal_back(x[...], mods[1:2], total[...])
        sums[0:1] = d_shift
        sums[1:2] = d_scale
        out[...] = grad[...] + d_x

    tick(6)


def self_backward(x, grad, mods, branch, source, proj, mixed, panels, mask, tiles, given=None, ident=None):
    f32, bf16 = jnp.float32, jnp.bfloat16
    rows = PM // tiles
    return call_with(
        functools.partial(self_backward_kernel, tiles),
        7,
        (x, grad, mods, branch, source, proj, mixed, panels, mask),
        [
            whole((PM, D)),
            whole((PM, D)),
            whole((8, D)),
            whole((PM, D)),
            whole((PM, D)),
            slab((PM, 896)),
            slab((PM, 384)),
            slab((D, D)),
            whole((rows, rows)),
        ],
        [whole((PM, D)), whole((8, D)), slab((1, 896)), slab((D, D))],
        [
            jax.ShapeDtypeStruct((PM, D), f32),
            jax.ShapeDtypeStruct((8, D), f32),
            jax.ShapeDtypeStruct((4, 1, 896), f32),
            jax.ShapeDtypeStruct((4, D, D), bf16),
        ],
        [
            pltpu.VMEM((PM, D), bf16),
            pltpu.VMEM((PM, D), f32),
            pltpu.VMEM((PM, 896), bf16),
            pltpu.VMEM((PM, 384), bf16),
        ],
        given,
        ident,
    )


def cross_forward_kernel(tick, x, mods, bias, context, panel, mask, out, proj, pair, mixed, total):
    step = pl.program_id(0)
    tick(0)

    @pl.when(step == 0)
    def first():
        total[...] = jnp.zeros_like(total)

    query = (mxu(x[...].astype(jnp.bfloat16), panel[0, :, :384]) + bias[0, :, :384]).astype(jnp.bfloat16)
    both = (mxu(context[...], panel[0, :, 256:896]) + bias[0, :, 256:896]).astype(jnp.bfloat16)
    proj[0] = query
    pair[0] = both
    heads = []
    for h in range(4):
        at = h * HD
        heads.append(
            head_forward(
                query[:, at : at + HD],
                both[:, 32 + at : 32 + at + HD],
                both[:, 32 + SPAN + at : 32 + SPAN + at + HD],
                mask[...],
            )
        )
        tick(h + 1)
    packed = padded_heads(heads, 96, 0).astype(jnp.bfloat16)
    mixed[0] = packed
    total[...] += mxu(packed, panel[0, :, 768:], CONTRACT_LAST)

    @pl.when(step == 3)
    def last():
        out[...] = x[...] + total[...] + mods[6:7]

    tick(5)


def cross_forward(x, mods, bias, context, panels, mask, given=None, ident=None):
    f32, bf16 = jnp.float32, jnp.bfloat16
    return call_with(
        cross_forward_kernel,
        6,
        (x, mods, bias, context, panels, mask),
        [
            whole((PM, D)),
            whole((8, D)),
            slab((1, 896)),
            whole((128, D)),
            slab((D, D)),
            whole((128, 1)),
        ],
        [whole((PM, D)), slab((PM, 384)), slab((128, 640)), slab((PM, 384))],
        [
            jax.ShapeDtypeStruct((PM, D), f32),
            jax.ShapeDtypeStruct((4, PM, 384), bf16),
            jax.ShapeDtypeStruct((4, 128, 640), bf16),
            jax.ShapeDtypeStruct((4, PM, 384), bf16),
        ],
        [pltpu.VMEM((PM, D), f32)],
        given,
        ident,
    )


def cross_backward_kernel(
    tick, x, grad, context, proj, pair, mixed, panel, mask, out, d_context, sums, d_bias, d_panel, total, ask, keys, held
):
    step = pl.program_id(0)
    tick(0)

    @pl.when(step == 0)
    def first():
        low = grad[...].astype(jnp.bfloat16)
        sums[0:1] = jnp.sum(low.astype(jnp.float32), 0, keepdims=True)
        total[...] = jnp.zeros_like(total)
        d_context[...] = jnp.zeros_like(d_context)

    low = grad[...].astype(jnp.bfloat16)
    d_mixed = mxu(low, panel[0, :, 768:]).astype(jnp.bfloat16)
    held[...] = d_mixed
    ask[:, SPAN:] = jnp.zeros((PM, 96), jnp.bfloat16)
    keys[...] = jnp.zeros_like(keys)
    for h in range(4):
        at = h * HD
        query, both = proj[0], pair[0]
        three = head_backward(
            query[:, at : at + HD],
            both[:, 32 + at : 32 + at + HD],
            both[:, 32 + SPAN + at : 32 + SPAN + at + HD],
            mask[...],
            held[:, 96 + at : 96 + at + HD],
        )
        ask[:, at : at + HD] = three[0].astype(jnp.bfloat16)
        keys[:, 32 + at : 32 + at + HD] = three[1].astype(jnp.bfloat16)
        keys[:, 32 + SPAN + at : 32 + SPAN + at + HD] = three[2].astype(jnp.bfloat16)
        tick(h + 1)
    d_ask, d_both = ask[...], keys[...]
    low = grad[...].astype(jnp.bfloat16)
    sum_both = jnp.sum(d_both.astype(jnp.float32), 0, keepdims=True)
    d_bias[0, :, :384] = jnp.sum(d_ask.astype(jnp.float32), 0, keepdims=True)
    d_bias[0, :, 384:] = sum_both
    total[...] += mxu(d_ask, panel[0, :, :384], CONTRACT_LAST)
    d_context[...] += mxu(d_both, panel[0, :, 256:896], CONTRACT_LAST)
    src, ctx, packed = x[...].astype(jnp.bfloat16), context[...], mixed[0]
    d_panel[0, :, :256] = mxu(src, d_ask[:, :256], CONTRACT_ROWS).astype(jnp.bfloat16)
    d_panel[0, :, 256:384] = (
        mxu(src, d_ask[:, 256:], CONTRACT_ROWS) + mxu(ctx, d_both[:, :128], CONTRACT_ROWS)
    ).astype(jnp.bfloat16)
    tick(5)
    d_panel[0, :, 384:768] = mxu(ctx, d_both[:, 128:512], CONTRACT_ROWS).astype(jnp.bfloat16)
    d_panel[0, :, 768:896] = (
        mxu(ctx, d_both[:, 512:], CONTRACT_ROWS) + mxu(low, packed[:, :128], CONTRACT_ROWS)
    ).astype(jnp.bfloat16)
    d_panel[0, :, 896:] = mxu(low, packed[:, 128:], CONTRACT_ROWS).astype(jnp.bfloat16)

    @pl.when(step == 3)
    def last():
        out[...] = grad[...] + total[...]

    tick(6)


def cross_backward(x, grad, context, proj, pair, mixed, panels, mask, given=None, ident=None):
    f32, bf16 = jnp.float32, jnp.bfloat16
    return call_with(
        cross_backward_kernel,
        7,
        (x, grad, context, proj, pair, mixed, panels, mask),
        [
            whole((PM, D)),
            whole((PM, D)),
            whole((128, D)),
            slab((PM, 384)),
            slab((128, 640)),
            slab((PM, 384)),
            slab((D, D)),
            whole((128, 1)),
        ],
        [whole((PM, D)), whole((128, D)), whole((8, D)), slab((1, 1024)), slab((D, D))],
        [
            jax.ShapeDtypeStruct((PM, D), f32),
            jax.ShapeDtypeStruct((128, D), f32),
            jax.ShapeDtypeStruct((8, D), f32),
            jax.ShapeDtypeStruct((4, 1, 1024), f32),
            jax.ShapeDtypeStruct((4, D, D), bf16),
        ],
        [
            pltpu.VMEM((PM, D), f32),
            pltpu.VMEM((PM, 384), bf16),
            pltpu.VMEM((128, 640), bf16),
            pltpu.VMEM((PM, 384), bf16),
        ],
        given,
        ident,
    )


GELU_A = math.sqrt(2.0 / math.pi)
GELU_B = 0.044715


def ffn_forward_kernel(tick, x, mods, bias, w_in, w_out, out, branch, source, pre, total):
    step = pl.program_id(0)
    tick(0)

    @pl.when(step == 0)
    def first():
        normed, unused = normal_parts(x[...])
        source[...] = (normed * (1.0 + mods[4:5]) + mods[3:4]).astype(jnp.bfloat16)
        total[...] = jnp.zeros_like(total)

    value = mxu(source[...], w_in[0, 0]) + bias[0]
    pre[0] = value
    tick(1)
    hidden = 0.5 * value * (1.0 + jnp.tanh(GELU_A * (value + GELU_B * value * value * value)))
    tick(2)
    total[...] += mxu(hidden.astype(jnp.bfloat16), w_out[0, 0], CONTRACT_LAST)

    @pl.when(step == 3)
    def last():
        result = total[...] + mods[6:7]
        branch[...] = result
        out[...] = x[...] + mods[5:6] * result

    tick(3)


def half(index):
    return pl.BlockSpec((1, 1, D, D), lambda i: (index, i, 0, 0))


def ffn_forward_chip(x, mods, bias, panels, given=None, ident=None):
    f32, bf16 = jnp.float32, jnp.bfloat16
    return call_with(
        ffn_forward_kernel,
        4,
        (x, mods, bias, panels, panels),
        [whole((PM, D)), whole((8, D)), slab((1, D)), half(0), half(1)],
        [whole((PM, D)), whole((PM, D)), whole((PM, D)), slab((PM, D))],
        [
            jax.ShapeDtypeStruct((PM, D), f32),
            jax.ShapeDtypeStruct((PM, D), f32),
            jax.ShapeDtypeStruct((PM, D), bf16),
            jax.ShapeDtypeStruct((4, PM, D), f32),
        ],
        [pltpu.VMEM((PM, D), f32)],
        given,
        ident,
    )


def ffn_backward_kernel(
    tick, x, grad, mods, branch, source, pre, w_in, w_out, out, sums, d_bias, d_panel, d_branch, total
):
    step = pl.program_id(0)
    tick(0)

    @pl.when(step == 0)
    def first():
        value = grad[...]
        low = (mods[5:6] * value).astype(jnp.bfloat16)
        d_branch[...] = low
        sums[2:3] = jnp.sum(value * branch[...], 0, keepdims=True)
        sums[3:4] = jnp.sum(low.astype(jnp.float32), 0, keepdims=True)
        total[...] = jnp.zeros_like(total)

    low = d_branch[...]
    value = pre[0]
    square = value * value
    bent = jnp.tanh(GELU_A * (value + GELU_B * value * square))
    slope = 0.5 * (1.0 + bent) + 0.5 * value * (1.0 - bent * bent) * GELU_A * (
        1.0 + 3.0 * GELU_B * square
    )
    hidden = (0.5 * value * (1.0 + bent)).astype(jnp.bfloat16)
    d_pre = (mxu(low, w_out[0, 0]) * slope).astype(jnp.bfloat16)
    tick(1)
    d_bias[0] = jnp.sum(d_pre.astype(jnp.float32), 0, keepdims=True)
    total[...] += mxu(d_pre, w_in[0, 0], CONTRACT_LAST)
    tick(2)
    d_panel[0, 0] = mxu(source[...], d_pre, CONTRACT_ROWS).astype(jnp.bfloat16)
    tick(3)
    d_panel[1, 0] = mxu(low, hidden, CONTRACT_ROWS).astype(jnp.bfloat16)

    @pl.when(step == 3)
    def last():
        d_x, d_shift, d_scale = normal_back(x[...], mods[4:5], total[...])
        sums[0:1] = d_shift
        sums[1:2] = d_scale
        out[...] = grad[...] + d_x

    tick(4)


def ffn_backward_chip(x, grad, mods, branch, source, pre, panels, given=None, ident=None):
    f32, bf16 = jnp.float32, jnp.bfloat16
    return call_with(
        ffn_backward_kernel,
        5,
        (x, grad, mods, branch, source, pre, panels, panels),
        [
            whole((PM, D)),
            whole((PM, D)),
            whole((8, D)),
            whole((PM, D)),
            whole((PM, D)),
            slab((PM, D)),
            half(0),
            half(1),
        ],
        [
            whole((PM, D)),
            whole((8, D)),
            slab((1, D)),
            pl.BlockSpec(
                (2, 1, D, D),
                lambda i: (0, i, 0, 0),
                pipeline_mode=pl.Buffered(2 if given is None else 1),
            ),
        ],
        [
            jax.ShapeDtypeStruct((PM, D), f32),
            jax.ShapeDtypeStruct((8, D), f32),
            jax.ShapeDtypeStruct((4, 1, D), f32),
            jax.ShapeDtypeStruct((2, 4, D, D), bf16),
        ],
        [pltpu.VMEM((PM, D), bf16), pltpu.VMEM((PM, D), f32)],
        given,
        ident,
    )


CLIPS, PARTS = 8, 4
HOLDERS = -(-(TFREQ + TXT) // EMB_LOCAL)


def all_peers(names):
    peers = []
    for name, size in ((DP, CLIPS), (MP, PARTS)):
        if name in names:
            me = lax.axis_index(name)
            peers += [{name: (me + o) % size} for o in range(1, size)]
    return peers


def greet_all(peers):
    barrier = pltpu.get_barrier_semaphore()
    for peer in peers:
        pl.semaphore_signal(barrier, inc=1, device_id=peer, device_id_type=MESH)
    pl.semaphore_wait(barrier, len(peers))


def trade(name, size, source, target, landing, send, recv, first=0):
    me = lax.axis_index(name)

    def copy(o, src, dst):
        return pltpu.make_async_remote_copy(
            src_ref=src,
            dst_ref=dst,
            send_sem=send.at[first + o],
            recv_sem=recv.at[first + o],
            device_id={name: (me + o) % size},
            device_id_type=MESH,
        )

    out = [copy(o, source((me + o) % size), target()) for o in range(1, size)]
    for one in out:
        one.start()
    for o in range(1, size):
        land = landing((me + size - o) % size)
        copy(o, land, land).wait_recv()
    for one in out:
        one.wait_send()


def exchange_call(kernel, ident, out_shape, scratch, operand, anywhere=False):
    spec = pl.BlockSpec(memory_space=pl.ANY if anywhere else pltpu.VMEM)
    return pl.pallas_call(
        kernel,
        out_shape=out_shape,
        in_specs=[spec],
        out_specs=spec,
        scratch_shapes=scratch + [pltpu.SemaphoreType.DMA((18,)), pltpu.SemaphoreType.DMA((18,))],
        compiler_params=pltpu.CompilerParams(
            collective_id=ident, has_side_effects=True, vmem_limit_bytes=BIG
        ),
    )(operand)


def share_kernel(name, size, x, out, send, recv):
    me = lax.axis_index(name)
    greet_all(all_peers((name,)))
    out[me] = x[...]
    trade(name, size, lambda to: x, lambda: out.at[me], lambda at: out.at[at], send, recv)


def share(x, name, ident):
    size = CLIPS if name == DP else PARTS
    shape = jax.ShapeDtypeStruct((size,) + x.shape, x.dtype)
    return exchange_call(functools.partial(share_kernel, name, size), ident, shape, [], x)


def gathered_sum(refs, count):
    value = refs[0]
    for i in range(1, count):
        value = value + refs[i]
    return value


def part_sum_kernel(x, out, near, one, send, recv):
    part, clip = lax.axis_index(MP), lax.axis_index(DP)
    greet_all(all_peers((DP, MP)))
    near[part] = x[...]
    trade(MP, PARTS, lambda to: x, lambda: near.at[part], lambda at: near.at[at], send, recv, 8)
    one[...] = gathered_sum(near, PARTS)
    out[clip] = one[...]
    trade(DP, CLIPS, lambda to: one, lambda: out.at[clip], lambda at: out.at[at], send, recv)


def part_sum(x, ident):
    scratch = [pltpu.VMEM((PARTS,) + x.shape, x.dtype), pltpu.VMEM(x.shape, x.dtype)]
    shape = jax.ShapeDtypeStruct((CLIPS,) + x.shape, x.dtype)
    return exchange_call(part_sum_kernel, ident, shape, scratch, x)


def whole_sum_kernel(rows, count, *refs):
    pieces, out = refs[:count], refs[count]
    x, far, near, one, two, send, recv = refs[count + 1 :]
    part, clip = lax.axis_index(MP), lax.axis_index(DP)
    greet_all(all_peers((DP, MP)))
    at = 0
    for piece in pieces:
        x[at : at + piece.shape[0]] = piece[...]
        at += piece.shape[0]
    x[at:] = jnp.zeros((x.shape[0] - at, x.shape[1]), x.dtype)

    def own(to):
        return x.at[pl.ds(pl.multiple_of(to * rows, rows), rows)]

    far[clip] = own(clip)[...]
    trade(DP, CLIPS, own, lambda: far.at[clip], lambda at: far.at[at], send, recv)
    one[...] = gathered_sum(far, CLIPS)
    near[part] = one[...]
    trade(MP, PARTS, lambda to: one, lambda: near.at[part], lambda at: near.at[at], send, recv, 7)
    two[...] = gathered_sum(near, PARTS)
    out[clip] = two[...]
    trade(DP, CLIPS, lambda to: two, lambda: out.at[clip], lambda at: out.at[at], send, recv, 10)


def whole_sum(pieces, ident):
    width = pieces[0].shape[1]
    total = -(-sum(piece.shape[0] for piece in pieces) // 128) * 128
    rows, f32 = total // CLIPS, jnp.float32
    vmem = pl.BlockSpec(memory_space=pltpu.VMEM)
    return pl.pallas_call(
        functools.partial(whole_sum_kernel, rows, len(pieces)),
        out_shape=jax.ShapeDtypeStruct((CLIPS, rows, width), f32),
        in_specs=[vmem] * len(pieces),
        out_specs=vmem,
        scratch_shapes=[
            pltpu.VMEM((total, width), f32),
            pltpu.VMEM((CLIPS, rows, width), f32),
            pltpu.VMEM((PARTS, rows, width), f32),
            pltpu.VMEM((rows, width), f32),
            pltpu.VMEM((rows, width), f32),
            pltpu.SemaphoreType.DMA((18,)),
            pltpu.SemaphoreType.DMA((18,)),
        ],
        compiler_params=pltpu.CompilerParams(
            collective_id=ident, has_side_effects=True, vmem_limit_bytes=BIG
        ),
    )(*pieces).reshape(total, width)


def deal_kernel(x, out, send, recv):
    clip = lax.axis_index(DP)
    greet_all(all_peers((DP,)))

    def copies(source):
        return [
            pltpu.make_async_remote_copy(
                src_ref=x.at[(clip + o) % CLIPS],
                dst_ref=out.at[source],
                send_sem=send.at[o],
                recv_sem=recv.at[source],
                device_id={DP: (clip + o) % CLIPS},
                device_id_type=MESH,
            )
            for o in range(1, CLIPS)
        ]

    for source in range(HOLDERS):

        @pl.when(clip == source)
        def give(source=source):
            out[source] = x[source]
            for copy in copies(source):
                copy.start()

    for source in range(HOLDERS):

        @pl.when(clip != source)
        def take(source=source):
            land = out.at[source]
            pltpu.make_async_remote_copy(
                src_ref=land,
                dst_ref=land,
                send_sem=send.at[1],
                recv_sem=recv.at[source],
                device_id={DP: (clip + 1) % CLIPS},
                device_id_type=MESH,
            ).wait_recv()

        @pl.when(clip == source)
        def sent(source=source):
            for copy in copies(source):
                copy.wait_send()


def deal(x, ident):
    shape = jax.ShapeDtypeStruct((HOLDERS,) + x.shape[1:], x.dtype)
    return exchange_call(deal_kernel, ident, shape, [], x)


def silu(value):
    return value * jax.nn.sigmoid(value)


def start_kernel(
    shard, freq, table, bias_one, bias_two, full, t_pre, t_emb, mods, *scratch
):
    part, clip = lax.axis_index(MP), lax.axis_index(DP)
    far_one, near_two, far_two, near_three = scratch[:4]
    one, two, three, send, recv = scratch[4:9]
    sems = scratch[9:]
    chips = Chips()
    greet_all(all_peers((DP, MP)))
    one[...] = mxu(freq[...], table[...])
    far_one[clip] = one[...]
    trade(DP, CLIPS, lambda to: one, lambda: far_one.at[clip], lambda at: far_one.at[at], send, recv)
    pre = gathered_sum(far_one, CLIPS) + bias_one[...]
    t_pre[...] = pre
    near_two[part] = mxu(silu(pre).astype(jnp.bfloat16), table[...], CONTRACT_LAST)
    mine = near_two.at[part]
    trade(MP, PARTS, lambda to: mine, lambda: mine, lambda at: near_two.at[at], send, recv, 7)
    two[...] = gathered_sum(near_two, PARTS)
    lead = TFREQ + TXT
    holder, row = lead // EMB_LOCAL, lead % EMB_LOCAL
    give(two, far_two, (holder, holder + 1), send, recv, 11)
    steps = gather_steps(chips, shard, full, sems)
    for step in steps[: len(sems) // 3]:
        step()
    emb = [far_two[0][:, row:], far_two[1][:, : D + row - EMB_LOCAL]]
    emb = jnp.concatenate(emb, 1) + bias_two[...]
    t_emb[...] = emb
    local = emb[:, :SPAN]
    for i in range(1, PARTS):
        local = jnp.where(part == i, emb[:, i * SPAN : (i + 1) * SPAN], local)
    near_three[part] = mxu(silu(local).astype(jnp.bfloat16), table[...], CONTRACT_LAST)
    last = near_three.at[part]
    trade(MP, PARTS, lambda to: last, lambda: last, lambda at: near_three.at[at], send, recv, 21)
    product = gathered_sum(near_three, PARTS)
    for i in range(CLIPS):
        three[i] = product[i : i + 1]
    mods[clip] = three[clip]
    trade(DP, CLIPS, lambda to: three.at[to], lambda: mods.at[clip], lambda at: mods.at[at], send, recv, 24)
    for step in steps[len(sems) // 3 :]:
        step()


def give(x, out, sources, send, recv, first):
    clip = lax.axis_index(DP)

    def copies(i):
        return [
            pltpu.make_async_remote_copy(
                src_ref=x,
                dst_ref=out.at[i],
                send_sem=send.at[first + o],
                recv_sem=recv.at[first + i],
                device_id={DP: (clip + o) % CLIPS},
                device_id_type=MESH,
            )
            for o in range(1, CLIPS)
        ]

    for i, source in enumerate(sources):

        @pl.when(clip == source)
        def begin(i=i):
            out[i] = x[...]
            for copy in copies(i):
                copy.start()

    for i, source in enumerate(sources):

        @pl.when(clip != source)
        def take(i=i):
            copies(i)[0].wait_recv()

        @pl.when(clip == source)
        def sent(i=i):
            for copy in copies(i):
                copy.wait_send()


def start(shard, freq, table, bias_one, bias_two, ident):
    f32 = jnp.float32
    wide = (CLIPS, EMB_LOCAL)
    vmem, remote = pl.BlockSpec(memory_space=pltpu.VMEM), pl.BlockSpec(memory_space=pl.ANY)
    return pl.pallas_call(
        start_kernel,
        out_shape=[
            jax.ShapeDtypeStruct((shard.shape[0], 4, 8) + shard.shape[1:], shard.dtype),
            jax.ShapeDtypeStruct((CLIPS, SPAN), f32),
            jax.ShapeDtypeStruct((CLIPS, D), f32),
            jax.ShapeDtypeStruct((CLIPS, 1, EMB_LOCAL), f32),
        ],
        in_specs=[remote, vmem, vmem, vmem, vmem],
        out_specs=[remote, vmem, vmem, vmem],
        scratch_shapes=[
            pltpu.VMEM((CLIPS, CLIPS, SPAN), f32),
            pltpu.VMEM((PARTS,) + wide, f32),
            pltpu.VMEM((2,) + wide, f32),
            pltpu.VMEM((PARTS,) + wide, f32),
            pltpu.VMEM((CLIPS, SPAN), f32),
            pltpu.VMEM(wide, f32),
            pltpu.VMEM((CLIPS, 1, EMB_LOCAL), f32),
            pltpu.SemaphoreType.DMA((32,)),
            pltpu.SemaphoreType.DMA((32,)),
        ]
        + GATHER_SEMS * GATHER_PIECES[shard.shape[0]],
        compiler_params=pltpu.CompilerParams(
            collective_id=ident, has_side_effects=True, vmem_limit_bytes=BIG
        ),
    )(shard, freq, table, bias_one, bias_two)


def to_time_kernel(x, out, local, send, recv):
    part = lax.axis_index(MP)
    greet_all(all_peers((MP,)))
    own = pltpu.make_async_copy(x.at[part], out.at[:, part], local)
    own.start()
    trade(MP, PARTS, lambda to: x.at[to], lambda: out.at[:, part], lambda at: out.at[:, at], send, recv)
    own.wait()


def to_space_kernel(x, out, local, send, recv):
    part = lax.axis_index(MP)
    greet_all(all_peers((MP,)))
    own = pltpu.make_async_copy(x.at[:, part], out.at[part], local)
    own.start()
    trade(MP, PARTS, lambda to: x.at[:, to], lambda: out.at[part], lambda at: out.at[at], send, recv)
    own.wait()


def to_time(x, ident):
    shape = jax.ShapeDtypeStruct((2, FR, PM // 8, D), x.dtype)
    operand = x.reshape(FR, 2, PM // 8, D)
    return exchange_call(
        to_time_kernel, ident, shape, [pltpu.SemaphoreType.DMA], operand, True
    ).reshape(PM, D)


def to_space(x, ident):
    shape = jax.ShapeDtypeStruct((FR, 2, PM // 8, D), x.dtype)
    operand = x.reshape(2, FR, PM // 8, D)
    return exchange_call(
        to_space_kernel, ident, shape, [pltpu.SemaphoreType.DMA], operand, True
    ).reshape(PM, D)


def modulate_back(x, shift_vec, scale_vec, grad):
    unused, pull = jax.vjp(modulate, x, shift_vec, scale_vec)
    return pull(grad)


def padded_rows(value):
    return jnp.pad(value, ((0, 128 - value.shape[0]), (0, 0)))


def local_rows(full, group):
    return lax.dynamic_slice_in_dim(full, group * EMB_LOCAL, EMB_LOCAL, 1)


def per_device_chips(
    latents,
    noise,
    caption,
    caption_lens,
    timesteps,
    grid_hw,
    frame_counts,
    attn_mats,
    ffn_mats,
    embed_mats,
    vectors,
    attn_first,
    ffn_first,
    embed_first,
    vector_first,
    attn_second,
    ffn_second,
    embed_second,
    vector_second,
    attn_ema,
    ffn_ema,
    embed_ema,
    vector_ema,
):
    group = lax.axis_index(DP)
    part = lax.axis_index(MP)
    clips = timesteps.shape[0]
    parts = unpack(vectors)
    bf16 = jnp.bfloat16
    f32 = jnp.float32

    attn_low = sort_panels(attn_mats)
    ffn_low = ffn_mats.astype(bf16)

    def panels(full):
        full = full.reshape(full.shape[:2] + (D, D))
        return full if full.shape[0] > 1 else full[0]


    pick = jnp.arange(clips, dtype=jnp.int32) == group

    def select(values):
        return jnp.sum(jnp.where(pick, values, 0))

    tstep = select(timesteps)
    cap_len = select(caption_lens)
    height = select(grid_hw[:, 0])
    width_grid = select(grid_hw[:, 1])
    frames = select(frame_counts)
    count = jnp.sum(frame_counts * grid_hw[:, 0] * grid_hw[:, 1]).astype(f32)
    betas, cumul = roster()
    step_ids = jnp.arange(1000, dtype=jnp.int32)
    alpha_bar = jnp.sum(jnp.where(step_ids == tstep, cumul, 0.0))
    alpha_prev = jnp.sum(jnp.where(step_ids == tstep - 1, cumul, 0.0))
    beta_now = jnp.sum(jnp.where(step_ids == tstep, betas, 0.0))

    embed_low = embed_mats.astype(bf16)
    width_local = embed_low.shape[1]
    captions = lax.all_gather(caption[0], DP, axis=0, tiled=True)
    lead = TFREQ + TXT
    cap_rows = local_rows(jnp.pad(captions, ((0, 0), (TFREQ, EMB_ALL - lead))), group)
    freq = waves(timesteps.astype(f32), TFREQ).astype(bf16)
    freq_rows = local_rows(jnp.pad(freq, ((0, 0), (0, EMB_ALL - TFREQ))), group)

    full, t_pre, t_emb_all, mod_rows = start(
        attn_low[0:1],
        freq_rows,
        embed_low,
        own_slice(parts[T_BIAS_ONE], part, width_local)[None],
        parts[T_BIAS_TWO][None],
        0,
    )
    w_space = panels(full)
    t_hidden = jax.nn.silu(t_pre).astype(bf16)
    t_emb_local = lax.dynamic_slice_in_dim(t_emb_all, part * width_local, width_local, 1)
    silu_local = jax.nn.silu(t_emb_local).astype(bf16)
    mod_sum = mod_rows.reshape(EMB_ALL)
    t_mod_vec = mod_sum[lead + 2 * D :] + parts[T_BIAS_MOD]
    t_emb = jnp.sum(jnp.where(pick[:, None], t_emb_all, 0.0), 0)

    def over_clips(value):
        return jnp.sum(share(value, DP, 2), 0)

    c_two_row = lead + D - group * EMB_LOCAL
    c_row_ids = c_two_row + jnp.arange(D, dtype=jnp.int32)
    c_held = (c_two_row >= 0) & (c_two_row + D <= EMB_LOCAL)
    c_two = lax.dynamic_slice_in_dim(embed_low, jnp.clip(c_two_row, 0, EMB_LOCAL - D), D, 0)
    c_two = lax.psum(jnp.where(c_held, c_two, jnp.zeros_like(c_two)), DP)
    c_product = jnp.dot(cap_rows, embed_low, preferred_element_type=f32)
    c_product = jnp.pad(c_product.astype(bf16).reshape(clips, CAP, width_local), ((0, 0), (0, 8), (0, 0)))
    c_pre = jnp.sum(deal(c_product, 3).astype(f32), 0)[:CAP]
    c_pre = c_pre + own_slice(parts[C_BIAS_ONE], part, width_local)
    c_hidden = gelu_tanh(c_pre).astype(bf16)
    c_part = lax.dot_general(c_hidden, c_two, CONTRACT_LAST, preferred_element_type=f32)

    def over_parts(value):
        return jnp.sum(share(padded_rows(value.astype(bf16)), MP, 4).astype(f32), 0)

    context = padded_rows((over_parts(c_part)[:CAP] + parts[C_BIAS_TWO]).astype(bf16))

    area = height * width_grid
    patch_ids = jnp.arange(PM, dtype=jnp.int32)
    shifted = patch_ids - (PM - area)
    noisy = jnp.sqrt(alpha_bar) * latents[0] + jnp.sqrt(1.0 - alpha_bar) * noise[0]
    noisy_low = noisy.astype(bf16)
    position = jnp.concatenate(
        [
            waves((shifted // width_grid).astype(f32), D // 2),
            waves((shifted % width_grid).astype(f32), D // 2),
        ],
        -1,
    )
    x = jnp.dot(noisy_low, parts[PATCH_W].astype(bf16), preferred_element_type=f32)
    x = x + parts[PATCH_B] + position
    tables = parts[TABLES] + t_mod_vec.reshape(1, 6, D)
    mods0, mods1 = tables[0], tables[1]
    mask_space = jnp.where(patch_ids >= PM - area, 0.0, NEG_LARGE)[:, None]
    mask_space = jnp.broadcast_to(mask_space, (PM, PM))
    mask_cross = jnp.where(jnp.arange(128, dtype=jnp.int32) < cap_len, 0.0, NEG_LARGE)[:, None]
    half_ids = jnp.arange(PM // 2, dtype=jnp.int32)
    frame_ids, place_ids = half_ids // (PM // 8), half_ids % (PM // 8)
    mask_time = jnp.where(
        (place_ids[:, None] == place_ids[None]) & (frame_ids[:, None] >= FR - frames), 0.0, NEG_LARGE
    )
    biases = parts[ATTN_BIAS]

    def side(values):
        blank = jnp.zeros((4, SPAN), f32)
        rows = [values[0].reshape(4, SPAN), blank, values[1].reshape(4, SPAN), blank[:, :32]]
        return jnp.concatenate(rows, 1)[:, None]

    def vectors_of(mods, out_bias):
        return jnp.concatenate([mods, out_bias[None], jnp.zeros((1, D), f32)])

    x0 = x
    m_space, m_ffn0 = vectors_of(mods0, biases[0, 2]), vectors_of(mods0, parts[FFN_BIAS_TWO][0])
    x1, branch0, source0, proj0, mixed0, full = self_forward(
        x0, m_space, side(biases[0]), w_space, mask_space, 1, attn_low[2:3], 5
    )
    w_cross = panels(full)
    m_cross = vectors_of(mods0, biases[2, 2])
    x2, cross_q, cross_kv, mixed1, full = cross_forward(
        x1, m_cross, side(biases[2]), context, w_cross, mask_cross, ffn_low[0], 6
    )
    w_ffn0 = panels(full)
    bias_ffn = parts[FFN_BIAS_ONE].reshape(2, 4, 1, D)
    x3, branch2, source2, pre2, full = ffn_forward_chip(
        x2, m_ffn0, bias_ffn[0], w_ffn0, attn_low[1:2], 7
    )
    w_time = panels(full)
    x3 = x3 + waves((part - (FR - frames)).astype(f32)[None], D)

    share_rows = PM // FR
    pixels = jnp.concatenate([latents[0], noise[0]], 1).reshape(FR, share_rows, -1)
    pixels = lax.all_to_all(pixels, MP, 0, 0, tiled=True).reshape(FR, 2, PM // 8, -1)
    pixels = pixels.swapaxes(0, 1).reshape(PM, -1)
    latent_time, noise_time = pixels[:, :CIN], pixels[:, CIN:]
    x4 = to_time(x3, 8)
    m_time, m_ffn1 = vectors_of(mods1, biases[1, 2]), vectors_of(mods1, parts[FFN_BIAS_TWO][1])
    x5, branch4, source4, proj4, mixed4, full = self_forward(
        x4, m_time, side(biases[1]), w_time, mask_time, 2, ffn_low[1], 9
    )
    w_ffn1 = panels(full)
    x6, branch5, source5, pre5 = ffn_forward_chip(x5, m_ffn1, bias_ffn[1], w_ffn1)

    final_mods = parts[FINAL_TABLE] + t_emb
    final_source = modulate(x6, final_mods[0], final_mods[1]).astype(bf16)
    final_low = parts[FINAL_W].astype(bf16)
    output = (
        lax.dot_general(final_source, final_low, CONTRACT_LAST, preferred_element_type=f32)
        + parts[FINAL_B]
    )
    frozen = output[:, :CIN]
    noisy_time = jnp.sqrt(alpha_bar) * latent_time + jnp.sqrt(1.0 - alpha_bar) * noise_time
    row_ids = jnp.arange(PM, dtype=jnp.int32)
    row_frames = (row_ids % (PM // 2)) // (PM // 8)
    row_patches = part * share_rows + (row_ids // (PM // 2)) * (PM // 8) + row_ids % (PM // 8)
    valid = (row_frames >= FR - frames) & (row_patches >= PM - area)

    def shard_loss(values):
        losses = token_losses(
            values, frozen, latent_time, noise_time, (noisy_time, alpha_bar, alpha_prev, beta_now)
        )
        return jnp.sum(jnp.where(valid, losses, 0.0))

    loss_part, loss_pull = jax.vjp(shard_loss, output)
    d_output = loss_pull(1.0 / count)[0].astype(bf16)
    d_final_w = lax.dot_general(d_output, final_source, CONTRACT_ROWS, preferred_element_type=f32)
    d_final_b = jnp.sum(d_output.astype(f32), 0)
    d_final_source = jnp.dot(d_output, final_low, preferred_element_type=f32)
    grad_x, d_final_shift, d_final_scale = modulate_back(
        x6, final_mods[0], final_mods[1], d_final_source
    )

    def blocks(grads):
        return grads.reshape((-1, 4, 8, BLOCK, D))

    grad_x, sums5, bias5, d_ffn1 = ffn_backward_chip(
        x5, grad_x, m_ffn1, branch5, source5, pre5, w_ffn1
    )
    grad_x, sums4, bias4, d_time, g_ffn1 = self_backward(
        x4, grad_x, m_time, branch4, source4, proj4, mixed4, w_time, mask_time, 2, blocks(d_ffn1), 10
    )
    d_mods1 = jnp.concatenate([sums4[:3], sums5[:3]])
    grad_x = to_space(grad_x, 12)

    grad_x, sums2, bias2, d_ffn0, g_time = ffn_backward_chip(
        x2, grad_x, m_ffn0, branch2, source2, pre2, w_ffn0, blocks(d_time), 11
    )
    grad_x, d_context, sums1, bias1, d_cross, g_ffn0 = cross_backward(
        x1, grad_x, context, cross_q, cross_kv, mixed1, w_cross, mask_cross, blocks(d_ffn0), 16
    )

    first_part = (part == 0).astype(f32)
    d_context = over_parts(d_context)[:CAP].astype(bf16)
    d_c_bias_two = jnp.sum(d_context.astype(f32), 0) * first_part
    d_c_hidden = jnp.dot(d_context, c_two, preferred_element_type=f32)
    unused, cap_pull = jax.vjp(gelu_tanh, c_pre)
    d_c_pre = cap_pull(d_c_hidden)[0].astype(bf16)
    d_c_bias_one = jnp.sum(d_c_pre.astype(f32), 0)
    caption_all = lax.all_gather(
        jnp.concatenate([d_context, c_hidden, d_c_pre], 1), DP, axis=0, tiled=True
    )
    d_context_all = caption_all[:, :D]
    c_hidden_all = caption_all[:, D : D + width_local]
    d_c_pre_all = caption_all[:, D + width_local :]
    d_c_one = lax.dot_general(cap_rows, d_c_pre_all, CONTRACT_ROWS, preferred_element_type=f32)
    context_rows = local_rows(
        jnp.pad(d_context_all, ((0, 0), (lead + D, EMB_ALL - lead - 2 * D))), group
    )
    d_c_two = lax.dot_general(context_rows, c_hidden_all, CONTRACT_ROWS, preferred_element_type=f32)

    grad_x, sums0, bias0, d_space, g_cross = self_backward(
        x0, grad_x, m_space, branch0, source0, proj0, mixed0, w_space, mask_space, 1, blocks(d_cross), 17
    )
    g_space = scatter_one(blocks(d_space), 18)
    d_mods0 = jnp.concatenate([sums0[:3], sums2[:3]])

    def side_sums(values, at_query, at_value, out_bias):
        rows = [values[:, 0, at : at + SPAN].reshape(-1) for at in (at_query, at_value)]
        return jnp.stack(rows + [out_bias])

    d_patch = grad_x.astype(bf16)
    d_patch_b = jnp.sum(d_patch.astype(f32), 0)
    d_patch_w = lax.dot_general(noisy_low, d_patch, CONTRACT_ROWS, preferred_element_type=f32)

    d_mod_part = (d_mods0 + d_mods1).reshape(-1)
    d_temb_part = d_final_shift + d_final_scale
    d_mod_all = part_sum(jnp.concatenate([d_mod_part, d_temb_part]).reshape(8, 7 * D // 8), 13)
    d_mod_all = d_mod_all.reshape(clips, 7 * D)
    d_temb_sum = d_mod_all[:, 6 * D :]
    d_mod_low = d_mod_all[:, : 6 * D].astype(bf16)
    d_mod_rows = local_rows(jnp.pad(d_mod_low, ((0, 0), (lead + 2 * D, 0))), group)
    d_silu = over_clips(jnp.dot(d_mod_rows, embed_low, preferred_element_type=f32))
    unused, silu_pull = jax.vjp(jax.nn.silu, t_emb_local)
    d_temb_local = silu_pull(d_silu)[0]
    d_temb = share(d_temb_local, MP, 14).swapaxes(0, 1).reshape(clips, D) + d_temb_sum
    d_temb_rows = local_rows(jnp.pad(d_temb, ((0, 0), (lead, EMB_ALL - lead - D))), group)
    d_t_hidden = over_clips(
        jnp.dot(d_temb_rows, embed_low.astype(f32), precision=lax.Precision.HIGHEST)
    )
    unused, pre_pull = jax.vjp(jax.nn.silu, t_pre)
    d_t_pre = pre_pull(d_t_hidden)[0]

    def outer(left, right):
        return lax.dot_general(
            left.astype(f32), right.astype(f32), CONTRACT_ROWS, precision=lax.Precision.HIGHEST
        )

    g_embed = (
        lax.dot_general(d_mod_rows, silu_local, CONTRACT_ROWS, preferred_element_type=f32)
        + outer(jnp.concatenate([d_temb_rows, freq_rows.astype(f32)]), jnp.concatenate([t_hidden.astype(f32), d_t_pre]))
        + d_c_one
        + d_c_two
    )

    here = pick.astype(f32)[:, None]

    def place_row(local):
        return placed(jnp.sum(local * here, 0), part, D)[None]

    vector_rows = [
            d_patch_w,
            d_patch_b[None],
            d_final_w,
            place_row(d_t_pre),
            d_temb_part[None] + place_row(d_temb_local),
            d_mods0 + d_mods1,
            placed(d_c_bias_one, part, D)[None],
            d_c_bias_two[None],
            side_sums(bias0, 0, 2 * SPAN, sums0[3]),
            side_sums(bias4, 0, 2 * SPAN, sums4[3]),
            side_sums(bias1, 0, 416 + SPAN, sums1[0]),
            bias2[:, 0],
            bias5[:, 0],
            sums2[3:4],
            sums5[3:4],
            d_mods0,
            d_mods1,
            d_final_shift[None],
            d_final_scale[None],
    ]
    g_attn = jnp.stack([g_space[0], g_time[0], g_cross[0]])
    g_ffn = jnp.stack([g_ffn0, g_ffn1])
    matrix_squares = jnp.sum(g_attn * g_attn) + jnp.sum(g_ffn * g_ffn) + jnp.sum(g_embed * g_embed)
    count_rows = sum(rows.shape[0] for rows in vector_rows)
    tail = jnp.concatenate([d_final_b, matrix_squares[None], loss_part[None], jnp.zeros((D - COUT - 2,), f32)])
    totals = whole_sum(vector_rows + [tail[None]], 15)
    tail = totals[count_rows]
    cut = CIN + 1 + COUT
    g_vector = jnp.concatenate(
        [totals[:cut].reshape(-1), tail[:COUT], totals[cut:count_rows].reshape(-1)]
    )
    loss_total = tail[COUT + 1]
    squares = tail[COUT] + jnp.sum(g_vector * g_vector)
    grad_norm = jnp.sqrt(squares)
    factor = CLIP_NORM / (grad_norm + 1e-06)
    new_attn = adam_update(
        attn_mats, attn_first, attn_second, attn_ema, g_attn * factor, LEARN_RATE
    )
    new_ffn = adam_update(ffn_mats, ffn_first, ffn_second, ffn_ema, g_ffn * factor, LEARN_RATE)
    new_embed = adam_update(
        embed_mats, embed_first, embed_second, embed_ema, g_embed * factor, LEARN_RATE
    )
    new_vector = adam_update(
        vectors, vector_first, vector_second, vector_ema, g_vector * factor, VECTOR_RATE
    )
    return (loss_total, count, grad_norm) + tuple(
        group_new[kind]
        for kind in range(4)
        for group_new in (new_attn, new_ffn, new_embed, new_vector)
    )


def solution(mesh):
    fits = dict(mesh.shape) == {DP: CLIPS, MP: FR}
    program = per_device_chips if fits else per_device
    return jax.shard_map(
        program,
        mesh=mesh,
        in_specs=(
            P(DP, MP, None),
            P(DP, MP, None),
            P(DP, None, None),
            P(),
            P(),
            P(),
            P(),
            P(None, DP, MP),
            P(None, None, DP, MP),
            P(DP, MP),
            P(),
            P(None, DP, MP),
            P(None, None, DP, MP),
            P(DP, MP),
            P(),
            P(None, DP, MP),
            P(None, None, DP, MP),
            P(DP, MP),
            P(),
            P(None, DP, MP),
            P(None, None, DP, MP),
            P(DP, MP),
            P(),
        ),
        out_specs=(
            P(),
            P(),
            P(),
            P(None, DP, MP),
            P(None, None, DP, MP),
            P(DP, MP),
            P(),
            P(None, DP, MP),
            P(None, None, DP, MP),
            P(DP, MP),
            P(),
            P(None, DP, MP),
            P(None, None, DP, MP),
            P(DP, MP),
            P(),
            P(None, DP, MP),
            P(None, None, DP, MP),
            P(DP, MP),
            P(),
        ),
        check_vma=False,
    )
```
